32 devices in a mesh: stream: 2 (over x), dp: 8 (over z, y), mp: 2 (over core).
Axes of the slice: x: 2, y: 2, z: 4, core: 2. Of those that a mesh axis runs over, the one named last changes fastest.
Arguments:
- inputs: bfloat16 [2, 8, 512, 768], P('stream', 'dp'), may hold values from -6 to 6
- w_query: bfloat16 [2, 2, 768, 768], P('stream', None, None, 'mp'), may hold values from -0.21875 to 0.21875
- w_key: bfloat16 [2, 2, 768, 768], P('stream', None, None, 'mp'), may hold values from -0.21875 to 0.21875
- w_value: bfloat16 [2, 2, 768, 768], P('stream', None, None, 'mp'), may hold values from -0.21875 to 0.21875
- w_out: bfloat16 [2, 2, 768, 768], P('stream', None, 'mp'), may hold values from -2.5 to 2.5
- w_up: bfloat16 [2, 2, 768, 3072], P('stream', None, None, 'mp'), may hold values from -0.21875 to 0.21875
- w_down: bfloat16 [2, 2, 3072, 768], P('stream', None, 'mp'), may hold values from -0.109375 to 0.109375
- norm_gain: float32 [2, 2, 2, 768], P('stream'), may hold values from 0.5 to 1.5
- norm_shift: float32 [2, 2, 2, 768], P('stream'), may hold values from -1.2 to 1.2
- box_table: float32 [2, 2, 12, 64], P('stream', None, 'mp'), may hold values from -4 to 4
- boxes: int32 [2, 2, 8, 512], P('stream', None, 'dp'), may hold values from 0 to 32
- pages: int32 [2, 8, 512], P(None, 'dp'), may hold values from 0 to 3, as said below
- cotangent: bfloat16 [2, 8, 512, 768], P('stream', 'dp'), may hold values from -6 to 6
Outputs:
- output: bfloat16 [2, 8, 512, 768], P('stream', 'dp')
- grad_inputs: float32 [2, 8, 512, 768], P('stream', 'dp')
- grad_query: float32 [2, 2, 768, 768], P('stream', None, 'dp', 'mp')
- grad_key: float32 [2, 2, 768, 768], P('stream', None, 'dp', 'mp')
- grad_value: float32 [2, 2, 768, 768], P('stream', None, 'dp', 'mp')
- grad_out: float32 [2, 2, 768, 768], P('stream', None, 'mp', 'dp')
- grad_up: float32 [2, 2, 768, 3072], P('stream', None, 'dp', 'mp')
- grad_down: float32 [2, 2, 3072, 768], P('stream', None, 'mp', 'dp')
- grad_gain: float32 [2, 2, 2, 768], P('stream', None, None, 'dp')
- grad_shift: float32 [2, 2, 2, 768], P('stream', None, None, 'dp')
- grad_table: float32 [2, 2, 12, 64], P('stream', None, 'mp', 'dp')
The draws below stay inside these ranges and needn't reach their ends.
Inputs may be any that keep to these rules, and one draw needn't show every extreme that they name: `pages`: along each row of each stream the page number never falls, and every page number from 0 to 3 occurs in that row of both streams.
All inputs are finite; a program needn't handle non-finite values.
Results may differ from the reference program's by a relative error of at most 0.038.
Values may be sent and summed in bfloat16 or wider, within the bound.
No kernel may reach another device: no remote copies, remote signals or barrier semaphores. Data moves between devices by JAX's collectives and lax.ppermute only.
A program may use at most 320 MiB of HBM per device.

```python
import jax
import jax.numpy as jnp
from jax import lax

D = 768
HEADS = 12
HEAD_DIM = 64
FF = 3072
SEQ = 512
PAGES = 4
NB = 32
ROWS = 8
N_MP = 2


def draw_pages(key, part):
    key = jax.random.fold_in(key, 7)
    keys = jax.random.split(key, 2 * ROWS)

    def one_row(row_key):
        order = jax.random.permutation(row_key, SEQ - 1).astype(jnp.int32)
        cuts = jnp.sort(order[:PAGES - 1]) + 1
        spots = jnp.arange(SEQ, dtype=jnp.int32)
        return jnp.sum((spots[:, None] >= cuts[None, :]).astype(jnp.int32), axis=1)
    return jax.vmap(one_row)(keys).reshape(2, ROWS, SEQ).astype(jnp.int32)


def touch_ends(entries, rng, low, largest):
    spot = [jax.random.randint(jax.random.fold_in(rng, axis), (), 0, length) for axis, length in enumerate(entries.shape)]
    widest = entries.shape.index(max(entries.shape))
    beside = spot[:widest] + [(spot[widest] + 1) % entries.shape[widest]] + spot[widest + 1:]
    return entries.at[tuple(spot)].set(low).at[tuple(beside)].set(largest)


def strengthened(array, own_key, source, target, parts, factor):
    def block_of(axis_at):
        return (jnp.arange(array.shape[axis_at]) // (array.shape[axis_at] // parts)).reshape((-1,) + (1,) * (array.ndim - 1 - axis_at))

    first = jax.random.permutation(own_key, parts)[block_of(target)]
    far = (block_of(target) + parts // 2) % parts
    return jnp.where((block_of(source) == first) | (block_of(source) == far), factor * array, array)


def block_scale(stream_key, extent, pieces, least, top_value):
    loudness, own = 1.0, jax.random.fold_in(stream_key, 6)
    for position, parts in pieces:
        heights = jnp.exp(jax.random.uniform(jax.random.fold_in(own, position), (parts,), jnp.float32, least / len(pieces), top_value / len(pieces)))
        loudness = loudness * jnp.repeat(heights, extent[position] // parts).reshape([-1 if axis == position else 1 for axis in range(len(extent))])
    return loudness


def noise(key, shape, scale, bound, shards=(), held_as=jnp.bfloat16):
    factor_of = block_scale(key, shape, shards, -0.22, 0.18) if shards else 1.0
    entries = jax.random.normal(key, shape, jnp.float32) * scale * factor_of
    return jnp.minimum(jnp.maximum(entries, -bound), bound).astype(held_as)


def gaussian_with(stream_key, extent, width, most, shards, heavy, held_as=jnp.bfloat16):
    values = width * jax.random.normal(stream_key, extent, jnp.float32)
    if shards:
        values = values * block_scale(stream_key, extent, shards, -0.22, 0.18)
    return jnp.clip(strengthened(values, jax.random.fold_in(stream_key, 3), *heavy), -most, most).astype(held_as)


def setup_inputs(seed: int = 0) -> dict:
    seeds = jax.random.split(jax.random.key(seed), 14)
    return {
        "inputs": gaussian_with(seeds[0], (2, ROWS, SEQ, D), 1.0, 6.0, ((0, 2), (1, 8)), (1, 3, 8, 2.0)),
        "w_query": noise(seeds[1], (2, 2, D, D), D ** -0.5, 0.21875, ((0, 2), (3, 2))),
        "w_key": noise(seeds[2], (2, 2, D, D), D ** -0.5, 0.21875, ((0, 2), (3, 2))),
        "w_value": noise(seeds[3], (2, 2, D, D), D ** -0.5, 0.21875, ((0, 2), (3, 2))),
        "w_out": noise(seeds[4], (2, 2, D, D), (D * PAGES // SEQ) ** -0.5, 2.5, ((0, 2), (2, 2))),
        "w_up": noise(seeds[5], (2, 2, D, FF), D ** -0.5, 0.21875, ((0, 2), (3, 2))),
        "w_down": noise(seeds[6], (2, 2, FF, D), FF ** -0.5, 0.109375, ((0, 2), (2, 2))),
        "norm_gain": jnp.clip(1.0 + 0.1 * jax.random.normal(seeds[7], (2, 2, 2, D), jnp.float32), 0.5, 1.5),
        "norm_shift": noise(seeds[8], (2, 2, 2, D), 0.2, 1.2, ((0, 2),), jnp.float32),
        "box_table": noise(seeds[9], (2, 2, HEADS, 2 * NB), 1.0, 4.0, ((0, 2), (2, 2)), jnp.float32),
        "boxes": touch_ends(jax.random.randint(seeds[10], (2, 2, ROWS, SEQ), 0, NB + 1), jax.random.fold_in(seeds[10], 1), 0, NB).astype(jnp.int32),
        "pages": draw_pages(jax.random.fold_in(seeds[13], 71), 0),
        "cotangent": noise(seeds[12], (2, ROWS, SEQ, D), 1.0, 6.0, ((0, 2), (1, 8))),
    }


EPSILON = 1e-05
MASKED = -1e+30
HIGHEST = lax.Precision.HIGHEST

@jax.custom_vjp
def low(v):
    return lax.optimization_barrier(v.astype(jnp.bfloat16)).astype(jnp.float32)

@jax.custom_vjp
def low_back(v):
    return v

def low_keep(v):
    return (low(v), None)

def low_pass(kept, grad):
    return (grad,)

def back_keep(v):
    return (v, None)

def back_low(kept, grad):
    return (low(grad),)
low.defvjp(low_keep, low_pass)
low_back.defvjp(back_keep, back_low)

def layer_norm(values, gain, shift):
    center = values - lax.optimization_barrier(jnp.mean(values, -1, keepdims=True))
    spread = lax.optimization_barrier(jnp.mean(center * center, -1, keepdims=True))
    return center * lax.rsqrt(spread + EPSILON) * gain + shift

def product(left, right):
    return jnp.matmul(left, right, precision=HIGHEST)

def relative_bias(box_row, table):

    def along(coords, column):
        index = (jnp.clip(coords[:, None] - coords[None, :], -NB, NB - 1) + NB).astype(jnp.int32)
        return column[:, index]
    return along(box_row[0], table[0]) + along(box_row[1], table[1])

def attend_rows(queries, keys, values, allowed, box_rows, table, with_bias):
    heads = queries.shape[-1] // HEAD_DIM
    scale = HEAD_DIM ** (-0.5)

    def one_row(items):
        query_row, key_row, value_row, allowed_row, box_row = items
        query_heads = query_row.reshape(SEQ, heads, HEAD_DIM)
        key_heads = key_row.reshape(SEQ, heads, HEAD_DIM)
        value_heads = value_row.reshape(SEQ, heads, HEAD_DIM)
        raw = low_back(jnp.einsum('qhd,khd->hqk', query_heads, key_heads, precision=HIGHEST) * scale)
        if with_bias:
            raw = raw + relative_bias(box_row, table)
        scores = jnp.where(allowed_row[None], raw, MASKED)
        top = lax.optimization_barrier(jnp.max(scores, -1, keepdims=True))
        weights = jnp.exp(scores - top)
        probs = weights / lax.optimization_barrier(jnp.sum(weights, -1, keepdims=True))
        context = jnp.einsum('hqk,khd->qhd', low(probs), value_heads, precision=HIGHEST)
        return context.reshape(SEQ, heads * HEAD_DIM)
    return lax.map(jax.checkpoint(one_row), (queries, keys, values, allowed, box_rows))

def forward(inputs, w_query, w_key, w_value, w_out, w_up, w_down, norm_gain, norm_shift, box_table, boxes, pages):
    half_width = D // N_MP
    half_hidden = FF // N_MP
    half_heads = HEADS // N_MP
    hidden = [inputs[0], inputs[1]]
    for layer in range(2):
        projected = []
        for side in range(2):
            rounded = low(hidden[side])
            groups = []
            for group in range(N_MP):
                start = group * half_width
                copy = low_back(rounded)
                queries = low_back(low(product(copy, w_query[side, layer][:, start:start + half_width])))
                keys = low_back(low(product(copy, w_key[side, layer][:, start:start + half_width])))
                values = low_back(low(product(copy, w_value[side, layer][:, start:start + half_width])))
                groups.append((queries, keys, values))
            projected.append(groups)
        fresh = []
        for side in range(2):
            source = side if layer == 0 else 1 - side
            allowed = pages[side][:, :, None] == pages[source][:, None, :]
            box_rows = jnp.transpose(boxes[side], (1, 0, 2))
            attention = jnp.zeros_like(hidden[side])
            for group in range(N_MP):
                start = group * half_width
                table = box_table[side][:, group * half_heads:(group + 1) * half_heads]
                context = attend_rows(projected[side][group][0], projected[source][group][1], projected[source][group][2], allowed, box_rows, table, layer == 0)
                context = low_back(low(context))
                attention = attention + low(low_back(product(context, w_out[side, layer][start:start + half_width, :])))
            middle = layer_norm(hidden[side] + attention, norm_gain[side, layer, 0], norm_shift[side, layer, 0])
            middle_low = low(middle)
            feed = jnp.zeros_like(middle)
            for group in range(N_MP):
                start = group * half_hidden
                copy = low_back(middle_low)
                upward = low_back(product(copy, w_up[side, layer][:, start:start + half_hidden]))
                active = low(jax.nn.gelu(upward, approximate=False))
                feed = feed + low(low_back(product(active, w_down[side, layer][start:start + half_hidden, :])))
            fresh.append(layer_norm(middle + feed, norm_gain[side, layer, 1], norm_shift[side, layer, 1]))
        hidden = fresh
    return jnp.stack(hidden)

def reference(inputs, w_query, w_key, w_value, w_out, w_up, w_down, norm_gain, norm_shift, box_table, boxes, pages, cotangent):
    floats = (inputs.astype(jnp.float32), w_query.astype(jnp.float32), w_key.astype(jnp.float32), w_value.astype(jnp.float32), w_out.astype(jnp.float32), w_up.astype(jnp.float32), w_down.astype(jnp.float32), norm_gain.astype(jnp.float32), norm_shift.astype(jnp.float32), box_table.astype(jnp.float32))

    def run(*params):
        return forward(*params, boxes, pages)
    result, pullback = jax.vjp(run, *floats)
    grads = pullback(cotangent.astype(jnp.float32))
    return (result.astype(jnp.bfloat16), grads[0], grads[1], grads[2], grads[3], grads[4], grads[5], grads[6], grads[7], grads[8], grads[9])
```

```python
import functools

import jax
import jax.numpy as jnp
from jax import lax
from jax.experimental import pallas as pl
from jax.experimental.pallas import tpu as pltpu
from jax.sharding import PartitionSpec as P

HEAD_DIM = 64
EPSILON = 1e-05
MASKED = -1e30
LOW = jnp.bfloat16
F32 = jnp.float32
LANES = 128
HIGHEST = lax.Precision.HIGHEST
SCALE = HEAD_DIM ** (-0.5)


def dot(left, right):
    return lax.dot_general(left, right, (((1,), (0,)), ((), ())), preferred_element_type=F32)


def dot_nt(left, right):
    return lax.dot_general(left, right, (((1,), (1,)), ((), ())), preferred_element_type=F32)


def iota(shape, dim):
    return lax.broadcasted_iota(jnp.int32, shape, dim)


def normalized(values):
    center = values - jnp.mean(values, -1, keepdims=True)
    rstd = lax.rsqrt(jnp.mean(center * center, -1, keepdims=True) + EPSILON)
    return center * rstd, rstd


def norm_back(grad, xhat, rstd, gain):
    scaled = grad * gain
    grad_in = rstd * (
        scaled
        - jnp.mean(scaled, -1, keepdims=True)
        - xhat * jnp.mean(scaled * xhat, -1, keepdims=True)
    )
    return grad_in, jnp.sum(grad * xhat, 0, keepdims=True), jnp.sum(grad, 0, keepdims=True)


def call(kernel, outs, *args, smem=(), scratch=(), cost=None):
    in_specs = [
        pl.BlockSpec(memory_space=pltpu.SMEM if i in smem else pltpu.VMEM)
        for i in range(len(args))
    ]
    return pl.pallas_call(
        kernel,
        out_shape=[jax.ShapeDtypeStruct(s, d) for s, d in outs],
        in_specs=in_specs,
        out_specs=[pl.BlockSpec(memory_space=pltpu.VMEM)] * len(outs),
        scratch_shapes=list(scratch),
        compiler_params=pltpu.CompilerParams(vmem_limit_bytes=48 * 1024 * 1024),
        cost_estimate=cost,
    )(*args)


def cost_of(flops, nbytes):
    return pl.CostEstimate(flops=int(flops), bytes_accessed=int(nbytes), transcendentals=0)


def page_mask(cols, rows):
    return jnp.where(cols == rows, 0.0, MASKED).astype(F32)


def key_marks(cols, levels):
    lane = iota((cols.shape[0], LANES), 1)
    want = levels - lane % levels
    picked = jnp.where((lane // levels) % 2 == 0, cols[:, 0:1], cols[:, 1:2])
    return (picked == want).astype(F32).astype(LOW)


def query_marks(cols, levels):
    lane = iota((cols.shape[0], LANES), 1)
    hit = (lane == levels - cols[:, 0:1]) | (lane == levels + 40 - cols[:, 1:2])
    return hit.astype(F32).astype(LOW)


def bias_rows(table, head, levels):
    lane = iota((40, LANES), 1)
    blocks = []
    for dim in range(2):
        line = table[dim][head : head + 1, :]
        line = jnp.concatenate(
            [line, jnp.broadcast_to(line[:, -1:], (1, LANES - line.shape[1]))], axis=1
        )
        base = jnp.broadcast_to(pltpu.roll(line, LANES - levels, 1), (40, LANES))
        spread = pltpu.roll(base, 0, 1, stride=1, stride_axis=0)
        spread = jnp.where(lane < levels, spread - spread[:, levels : levels + 1], 0.0)
        upper = spread.astype(LOW).astype(F32)
        lower = spread - upper
        blocks.append(
            pltpu.roll(upper, dim * levels, 1) + pltpu.roll(lower, (2 + dim) * levels, 1)
            if dim
            else upper + pltpu.roll(lower, 2 * levels, 1)
        )
    blocks.append(jnp.zeros((LANES - 80, LANES), F32))
    return jnp.concatenate(blocks, axis=0).astype(LOW)


def half_masks():
    lane = iota((1, LANES), 1)
    first = (lane < HEAD_DIM).astype(F32).astype(LOW)
    return first, (1 - first.astype(F32)).astype(LOW)


def attend(q_ref, k_ref, v_ref, ext_ref, key_ext, mask, lse_ref, ctx_ref):
    seq, width = q_ref.shape
    halves = half_masks()
    lane = iota((seq, LANES), 1)
    ones = jnp.ones((seq, LANES), LOW)
    lse = jnp.zeros((seq, LANES), F32)
    for pair in range(width // LANES):
        at = slice(pair * LANES, (pair + 1) * LANES)
        queries, keys = q_ref[:, at], k_ref[:, at]
        if key_ext is not None:
            keys = jnp.concatenate([keys, key_ext], axis=1)
        values = jnp.concatenate([v_ref[:, at], ones], axis=1)
        parts = []
        for half in range(2):
            head = 2 * pair + half
            left = queries * halves[half]
            if key_ext is not None:
                left = jnp.concatenate([left, ext_ref[:, head * LANES : (head + 1) * LANES]], axis=1)
            scores = dot_nt(left, keys) + mask
            top = jnp.max(scores, -1, keepdims=True)
            weights = jnp.exp(scores - top).astype(LOW)
            out = dot(weights, values)
            total = out[:, LANES:]
            parts.append(out[:, :LANES] / total)
            lse = jnp.where(lane == head, top + jnp.log(total), lse)
        ctx_ref[:, at] = jnp.where(lane < HEAD_DIM, parts[0], parts[1]).astype(LOW)
    lse_ref[...] = lse


def first_attention(levels, x, wq, wk, wv, wo, cols, rows, table, part, q, k, v, lse, ctx, ext):
    states = x[...]
    q[...] = (dot(states, wq[...]).astype(LOW).astype(F32) * SCALE).astype(LOW)
    k[...] = dot(states, wk[...]).astype(LOW)
    v[...] = dot(states, wv[...]).astype(LOW)
    marks = query_marks(cols[...], levels)
    tables = [table[0], table[1]]
    for head in range(q.shape[1] // HEAD_DIM):
        ext[:, head * LANES : (head + 1) * LANES] = dot(
            marks, bias_rows(tables, head, levels)
        ).astype(LOW)
    mask = page_mask(cols[:, 2:3], rows[2:3, :])
    attend(q, k, v, ext, key_marks(cols[...], levels), mask, lse, ctx)
    part[...] = dot(ctx[...], wo[...]).astype(LOW)


def next_project(mixed, gain1, shift1, own, far, gain2, shift2, wq, wk, wv, combined, hidden, rounded, q, k, v):
    xhat, _ = normalized(mixed[...])
    total = xhat * gain1[...] + shift1[...] + (own[...].astype(F32) + far[...].astype(F32))
    combined[...] = total
    xhat, _ = normalized(total)
    state = xhat * gain2[...] + shift2[...]
    hidden[...] = state
    low = state.astype(LOW)
    rounded[...] = low
    k[...] = dot(low, wk[...]).astype(LOW)
    v[...] = dot(low, wv[...]).astype(LOW)
    q[...] = (dot(low, wq[...]).astype(LOW).astype(F32) * SCALE).astype(LOW)


def next_attention(q, k, v, wo, cols, rows, part, lse, ctx):
    mask = page_mask(cols[:, 2:3], rows[3:4, :])
    attend(q, k, v, None, None, mask, lse, ctx)
    part[...] = dot(ctx[...], wo[...]).astype(LOW)


def normal_cdf(values):
    return 0.5 * (1.0 + lax.erf(values * (0.5**0.5)))


def feed_forward(hidden, own, far, gain, shift, w_up, w_down, mixed, middle, upward, active, part):
    total = hidden[...].astype(F32) + (own[...].astype(F32) + far[...].astype(F32))
    mixed[...] = total
    xhat, _ = normalized(total)
    low = (xhat * gain[...] + shift[...]).astype(LOW)
    middle[...] = low
    step = 512
    acc = None
    for start in range(0, w_up.shape[1], step):
        at = slice(start, start + step)
        up = dot(low, w_up[:, at])
        upward[:, at] = up.astype(LOW)
        act = (up * normal_cdf(up)).astype(LOW)
        active[:, at] = act
        piece = dot(act, w_down[at, :])
        acc = piece if acc is None else acc + piece
    part[...] = acc.astype(LOW)


def feed_back_body(grad, combined, gain, w_up, w_down, upward, grad_comb, down_cot, grad_up, part, dgain, dshift):
    xhat, rstd = normalized(combined)
    grad_in, dgain[...], dshift[...] = norm_back(grad, xhat, rstd, gain)
    grad_comb[...] = grad_in
    low = grad_in.astype(LOW)
    down_cot[...] = low
    step = 512
    acc = None
    for start in range(0, w_up.shape[1], step):
        at = slice(start, start + step)
        back = dot_nt(low, w_down[at, :])
        up = upward[:, at].astype(F32)
        slope = normal_cdf(up) + up * (jnp.exp(-0.5 * up * up) * 0.3989422804014327)
        gup = (back * slope).astype(LOW)
        grad_up[:, at] = gup
        piece = dot_nt(gup, w_up[:, at])
        acc = piece if acc is None else acc + piece
    part[...] = acc.astype(LOW)


def last_feed_back(cot, mixed, gain1, shift1, own, far, gain, shift, w_up, w_down, upward, output, grad_comb, down_cot, grad_up, part, dgain, dshift):
    xhat, _ = normalized(mixed[...])
    combined = xhat * gain1[...] + shift1[...] + (own[...].astype(F32) + far[...].astype(F32))
    xhat, _ = normalized(combined)
    output[...] = (xhat * gain[...] + shift[...]).astype(LOW)
    feed_back_body(cot[...].astype(F32), combined, gain[...], w_up, w_down, upward, grad_comb, down_cot, grad_up, part, dgain, dshift)


def first_feed_back(grad_mixed, own, far, combined, gain, w_up, w_down, upward, grad_comb, down_cot, grad_up, part, dgain, dshift):
    grad = grad_mixed[...] + (own[...].astype(F32) + far[...].astype(F32))
    feed_back_body(grad, combined[...], gain[...], w_up, w_down, upward, grad_comb, down_cot, grad_up, part, dgain, dshift)


def attention_back_body(levels, page_row, grad_comb, own, far, mixed, gain, wo, q, k, v, lse, ctx, ext, cols, rows, grad_mixed, out_cot, gq, gkt, gvt, dgain, dshift, dtable):
    seq, width = q.shape
    grad = grad_comb[...] + (own[...].astype(F32) + far[...].astype(F32))
    xhat, rstd = normalized(mixed[...])
    grad_in, dgain[...], dshift[...] = norm_back(grad, xhat, rstd, gain[...])
    grad_mixed[...] = grad_in
    low = grad_in.astype(LOW)
    out_cot[...] = low
    gctx = dot_nt(low, wo[...]).astype(LOW)
    mask = page_mask(cols[:, 2:3], rows[page_row : page_row + 1, :])
    halves = half_masks()
    lane = iota((seq, LANES), 1)
    if ext is not None:
        key_ext = key_marks(cols[...], levels)
        back_ext = (
            (lane == levels - cols[:, 0:1]) | (lane == levels + HEAD_DIM - cols[:, 1:2])
        ).astype(F32).astype(LOW)
        line = iota((LANES, seq), 0)
        marks_t = ((line == rows[0:1, :]) | (line == rows[1:2, :] + HEAD_DIM)).astype(F32).astype(LOW)
        dtable[...] = jnp.zeros(dtable.shape, F32)
    for pair in range(width // LANES):
        at = slice(pair * LANES, (pair + 1) * LANES)
        queries, keys, values = q[:, at], k[:, at], v[:, at]
        gc = gctx[:, at]
        product = gc.astype(F32) * ctx[:, at].astype(F32)
        gc_t = jnp.transpose(gc)
        q_t = jnp.transpose(queries)
        keys_left = keys if ext is None else jnp.concatenate([keys, key_ext], axis=1)
        keys_right = keys if ext is None else jnp.concatenate([keys, back_ext], axis=1)
        parts = []
        for half in range(2):
            head = 2 * pair + half
            rows_at = slice(half * HEAD_DIM, (half + 1) * HEAD_DIM)
            out_at = slice(head * HEAD_DIM, (head + 1) * HEAD_DIM)
            left = queries * halves[half]
            if ext is not None:
                left = jnp.concatenate([left, ext[:, head * LANES : (head + 1) * LANES]], axis=1)
            scores = dot_nt(left, keys_left) + mask
            probs = jnp.exp(scores - lse[:, head : head + 1])
            delta = jnp.sum(
                jnp.where((lane < HEAD_DIM) == (half == 0), product, 0.0), -1, keepdims=True
            )
            grad_scores = probs * (dot_nt(gc * halves[half], values) - delta)
            score_cot = grad_scores.astype(LOW)
            gvt[out_at, :] = dot(gc_t[rows_at, :], probs.astype(LOW)).astype(LOW)
            gkt[out_at, :] = dot(q_t[rows_at, :], score_cot).astype(LOW)
            out = dot(score_cot, keys_right)
            parts.append(out[:, :LANES])
            if ext is not None:
                spread = out[:, LANES:]
                upper = spread.astype(LOW)
                lower = (spread - upper.astype(F32)).astype(LOW)
                block = dot(marks_t, upper) + dot(marks_t, lower)
                small = iota((40, LANES), 1)
                for dim in range(2):
                    piece = block[dim * HEAD_DIM : dim * HEAD_DIM + 40, :]
                    if dim:
                        piece = pltpu.roll(piece, HEAD_DIM, 1)
                    piece = jnp.where(small <= levels, piece, 0.0)
                    piece = pltpu.roll(piece, 0, 1, stride=1, stride_axis=0)
                    line = jnp.sum(piece, 0, keepdims=True)
                    over = pltpu.roll(line, LANES - 1, 1)
                    place = iota((1, LANES), 1)
                    line = jnp.where(place == 2 * levels - 1, line + over, line)
                    dtable[dim, head : head + 1, :] = line
        gq[:, at] = (jnp.where(lane < HEAD_DIM, parts[0], parts[1]) * SCALE).astype(LOW)


def next_attention_back(grad_comb, own, far, mixed, gain, wo, q, k, v, lse, ctx, cols, rows, grad_mixed, out_cot, gq, gkt, gvt, dgain, dshift):
    attention_back_body(0, 3, grad_comb, own, far, mixed, gain, wo, q, k, v, lse, ctx, None, cols, rows, grad_mixed, out_cot, gq, gkt, gvt, dgain, dshift, None)


def first_attention_back(levels, grad_comb, own, far, mixed, gain, wo, q, k, v, lse, ctx, ext, cols, rows, wq, wk, wv, grad_mixed, out_cot, gq, gkt, gvt, dgain, dshift, dtable, part):
    attention_back_body(levels, 2, grad_comb, own, far, mixed, gain, wo, q, k, v, lse, ctx, ext, cols, rows, grad_mixed, out_cot, gq, gkt, gvt, dgain, dshift, dtable)
    input_back(gq, gkt, gvt, wq, wk, wv, part)


def input_back(gq, gkt, gvt, wq, wk, wv, part):
    part[...] = (
        dot_nt(gq[...], wq[...])
        + dot_nt(jnp.transpose(gkt[...]), wk[...])
        + dot_nt(jnp.transpose(gvt[...]), wv[...])
    ).astype(LOW)


def feed_weights(down_cot, active, middle, grad_up, out):
    width = active.shape[1]
    step = 512
    left = jnp.transpose(down_cot[...])
    for start in range(0, width, step):
        out[:, start : start + step] = dot(left, active[:, start : start + step]).astype(LOW)
    left = jnp.transpose(middle[...])
    for start in range(0, width, step):
        out[:, width + start : width + start + step] = dot(
            left, grad_up[:, start : start + step]
        ).astype(LOW)


def attention_weights(rounded, gq, gkt, gvt, out_cot, ctx, out):
    width = gq.shape[1]
    left = jnp.transpose(rounded[...])
    out[:, :width] = dot(left, gq[...]).astype(LOW)
    out[:, width : 2 * width] = dot_nt(left, gkt[...]).astype(LOW)
    out[:, 2 * width : 3 * width] = dot_nt(left, gvt[...]).astype(LOW)
    left = jnp.transpose(out_cot[...])
    out[:, 3 * width :] = dot(left, ctx[...]).astype(LOW)


def other(block, axis):
    return lax.ppermute(block, axis, [(0, 1), (1, 0)])


def body(inputs, w_query, w_key, w_value, w_out, w_up, w_down, norm_gain, norm_shift, box_table, boxes, pages, cotangent):
    side = lax.axis_index("stream")
    _, rows_here, seq, d_model = inputs.shape
    assert rows_here == 1
    width = w_query.shape[3]
    hidden_width = w_up.shape[3]
    heads = width // HEAD_DIM
    levels = box_table.shape[3] // 2
    own_pages = lax.dynamic_index_in_dim(pages[:, 0], side, 0, keepdims=True)
    far_pages = lax.dynamic_index_in_dim(pages[:, 0], 1 - side, 0, keepdims=True)
    rows = jnp.concatenate([boxes[0, :, 0], own_pages, far_pages], axis=0)
    cols = jnp.transpose(rows)
    x = inputs[0, 0]
    gain = lambda layer, which: norm_gain[0, layer, which][None]
    shift = lambda layer, which: norm_shift[0, layer, which][None]
    wide = ((seq, d_model), F32)
    thin = ((seq, d_model), LOW)
    proj = ((seq, width), LOW)
    proj_t = ((width, seq), LOW)
    ff = ((seq, hidden_width), LOW)
    stats = ((seq, LANES), F32)
    vec = ((1, d_model), F32)

    part, q0, k0, v0, lse0, ctx0, ext0 = call(
        functools.partial(first_attention, levels),
        [thin, proj, proj, proj, stats, proj, ((seq, heads * LANES), LOW)],
        x, w_query[0, 0], w_key[0, 0], w_value[0, 0], w_out[0, 0], cols, rows, box_table[0],
    )
    mixed0, middle0, upward0, active0, feed = call(
        feed_forward, [wide, thin, ff, ff, thin],
        x, part, other(part, "mp"), gain(0, 0), shift(0, 0), w_up[0, 0], w_down[0, 0],
    )
    combined0, hidden1, rounded1, q1, k1, v1 = call(
        next_project, [wide, wide, thin, proj, proj, proj],
        mixed0, gain(0, 0), shift(0, 0), feed, other(feed, "mp"), gain(0, 1), shift(0, 1),
        w_query[0, 1], w_key[0, 1], w_value[0, 1],
    )
    k1, v1 = other(k1, "stream"), other(v1, "stream")
    part, lse1, ctx1 = call(next_attention, [thin, stats, proj], q1, k1, v1, w_out[0, 1], cols, rows)
    mixed1, middle1, upward1, active1, feed = call(
        feed_forward, [wide, thin, ff, ff, thin],
        hidden1, part, other(part, "mp"), gain(1, 0), shift(1, 0), w_up[0, 1], w_down[0, 1],
    )
    output, grad_comb, down_cot, grad_up, part, dgain11, dshift11 = call(
        last_feed_back, [thin, wide, thin, ff, thin, vec, vec],
        cotangent[0, 0], mixed1, gain(1, 0), shift(1, 0), feed, other(feed, "mp"), gain(1, 1), shift(1, 1),
        w_up[0, 1], w_down[0, 1], upward1,
    )
    (grads_ff1,) = call(
        feed_weights, [((d_model, 2 * hidden_width), LOW)], down_cot, active1, middle1, grad_up
    )
    grad_mixed, out_cot, gq, gkt, gvt, dgain10, dshift10 = call(
        next_attention_back, [wide, thin, proj, proj_t, proj_t, vec, vec],
        grad_comb, part, other(part, "mp"), mixed1, gain(1, 0), w_out[0, 1], q1, k1, v1, lse1, ctx1, cols, rows,
    )
    gkt, gvt = other(gkt, "stream"), other(gvt, "stream")
    (part,) = call(input_back, [thin], gq, gkt, gvt, w_query[0, 1], w_key[0, 1], w_value[0, 1])
    (grads_at1,) = call(
        attention_weights, [((d_model, 4 * width), LOW)], rounded1, gq, gkt, gvt, out_cot, ctx1
    )
    grad_comb, down_cot, grad_up, part, dgain01, dshift01 = call(
        first_feed_back, [wide, thin, ff, thin, vec, vec],
        grad_mixed, part, other(part, "mp"), combined0, gain(0, 1), w_up[0, 0], w_down[0, 0], upward0,
    )
    (grads_ff0,) = call(
        feed_weights, [((d_model, 2 * hidden_width), LOW)], down_cot, active0, middle0, grad_up
    )
    grad_mixed, out_cot, gq, gkt, gvt, dgain00, dshift00, dtable, part = call(
        functools.partial(first_attention_back, levels),
        [wide, thin, proj, proj_t, proj_t, vec, vec, ((2, 8, LANES), F32), thin],
        grad_comb, part, other(part, "mp"), mixed0, gain(0, 0), w_out[0, 0], q0, k0, v0, lse0, ctx0, ext0, cols, rows,
        w_query[0, 0], w_key[0, 0], w_value[0, 0],
    )
    (grads_at0,) = call(
        attention_weights, [((d_model, 4 * width), LOW)], x, gq, gkt, gvt, out_cot, ctx0
    )
    grad_inputs = grad_mixed + (part.astype(F32) + other(part, "mp").astype(F32))

    scatter = lambda block: lax.psum_scatter(block, "dp", scatter_dimension=0, tiled=True)
    ff1, at1, ff0, at0 = (scatter(g).astype(F32) for g in (grads_ff1, grads_at1, grads_ff0, grads_at0))
    n_dp = lax.axis_size("dp")
    vectors = jnp.concatenate(
        [dgain00, dgain01, dgain10, dgain11, dshift00, dshift01, dshift10, dshift11], axis=0
    )
    vectors = jnp.transpose(vectors.reshape(8, n_dp, d_model // n_dp), (1, 0, 2)).reshape(n_dp, -1)
    tables = dtable[:, :heads, : 2 * levels].reshape(2 * heads, n_dp, -1)
    tables = jnp.transpose(tables, (1, 0, 2)).reshape(n_dp, -1)
    small = scatter(jnp.concatenate([vectors, tables], axis=1).reshape(-1))
    cut = 8 * d_model // n_dp
    vectors = small[:cut].reshape(2, 2, 2, d_model // n_dp)
    grad_table = small[cut:].reshape(1, 2, heads, 2 * levels // n_dp)

    def columns(start, stop, a, b, flip=False):
        pair = (a[:, start:stop], b[:, start:stop])
        return jnp.stack([jnp.transpose(p) for p in pair] if flip else list(pair))[None]

    return (
        output[None, None],
        grad_inputs[None, None],
        columns(0, width, at0, at1),
        columns(width, 2 * width, at0, at1),
        columns(2 * width, 3 * width, at0, at1),
        columns(3 * width, 4 * width, at0, at1, True),
        columns(hidden_width, 2 * hidden_width, ff0, ff1),
        columns(0, hidden_width, ff0, ff1, True),
        vectors[:1],
        vectors[1:],
        grad_table,
    )


def solution(mesh):
    in_specs = (
        P("stream", "dp", None, None),
        P("stream", None, None, "mp"),
        P("stream", None, None, "mp"),
        P("stream", None, None, "mp"),
        P("stream", None, "mp", None),
        P("stream", None, None, "mp"),
        P("stream", None, "mp", None),
        P("stream", None, None, None),
        P("stream", None, None, None),
        P("stream", None, "mp", None),
        P("stream", None, "dp", None),
        P(None, "dp", None),
        P("stream", "dp", None, None),
    )
    out_specs = (
        P("stream", "dp", None, None),
        P("stream", "dp", None, None),
        P("stream", None, "dp", "mp"),
        P("stream", None, "dp", "mp"),
        P("stream", None, "dp", "mp"),
        P("stream", None, "mp", "dp"),
        P("stream", None, "dp", "mp"),
        P("stream", None, "mp", "dp"),
        P("stream", None, None, "dp"),
        P("stream", None, None, "dp"),
        P("stream", None, "mp", "dp"),
    )
    return jax.shard_map(body, mesh=mesh, in_specs=in_specs, out_specs=out_specs, check_vma=False)
```

```python
import functools

import jax
import jax.numpy as jnp
from jax import lax
from jax.experimental import pallas as pl
from jax.experimental.pallas import tpu as pltpu
from jax.sharding import PartitionSpec as P

HEAD_DIM = 64
EPSILON = 1e-05
MASKED = -1e30
LOW = jnp.bfloat16
F32 = jnp.float32
LANES = 128
SCALE = HEAD_DIM ** (-0.5)


def dot(left, right):
    return lax.dot_general(left, right, (((1,), (0,)), ((), ())), preferred_element_type=F32)


def dot_nt(left, right):
    return lax.dot_general(left, right, (((1,), (1,)), ((), ())), preferred_element_type=F32)


def iota(shape, dim):
    return lax.broadcasted_iota(jnp.int32, shape, dim)


def normalized(values):
    center = values - jnp.mean(values, -1, keepdims=True)
    rstd = lax.rsqrt(jnp.mean(center * center, -1, keepdims=True) + EPSILON)
    return center * rstd, rstd


def norm_back(grad, xhat, rstd, gain):
    scaled = grad * gain
    grad_in = rstd * (
        scaled
        - jnp.mean(scaled, -1, keepdims=True)
        - xhat * jnp.mean(scaled * xhat, -1, keepdims=True)
    )
    return grad_in, jnp.sum(grad * xhat, 0, keepdims=True), jnp.sum(grad, 0, keepdims=True)


class Held:
    def __init__(self, array, *index):
        self.array, self.dtype = array, array.dtype
        self.index = tuple(slice(None) if i is None else i for i in index)
        plain = tuple(0 if callable(i) else i for i in self.index)
        self.shape = jax.eval_shape(lambda: jnp.zeros(array.shape, jnp.int8)[plain]).shape

    def part(self, ref):
        return ref.at[tuple(i() if callable(i) else i for i in self.index)] if self.index else ref


class Arriving:
    def __init__(self, source, target, semaphore):
        self.copy = pltpu.make_async_copy(source, target, semaphore)
        self.copy.start()
        self.target, self.waited = target, False
        self.shape, self.dtype = target.shape, target.dtype

    def arrive(self):
        if not self.waited:
            self.copy.wait()
        self.waited = True

    def __getitem__(self, at):
        self.arrive()
        return self.target[at]


class Leaving:
    def __init__(self, source, target, semaphore):
        self.copy = pltpu.make_async_copy(source, target, semaphore)
        self.source, self.left = source, False
        self.shape, self.dtype = source.shape, source.dtype

    def leave(self):
        if not self.left:
            self.copy.start()
        self.left = True

    def __getitem__(self, at):
        return self.source[at]

    def __setitem__(self, at, value):
        self.source[at] = value


def leave(*refs):
    for ref in refs:
        if isinstance(ref, Leaving):
            ref.leave()


SAVE = "save"
FREE = "free"


def call(kernel, outs, *args, after=(), scratch=(), vmem=24, time=0.0):
    arrays, specs, held = [], [], []
    for place, arg in enumerate(args):
        if isinstance(arg, Held):
            specs.append(pl.BlockSpec(memory_space=pltpu.HBM))
            arrays.append(pltpu.with_memory_space_constraint(arg.array, pltpu.HBM))
            held.append((place, arg))
        else:
            specs.append(pl.BlockSpec(memory_space=pltpu.VMEM))
            arrays.append(pltpu.with_memory_space_constraint(arg, pltpu.VMEM))
    saved = [place for place, out in enumerate(outs) if out[2:] == (SAVE,)]
    out_shape, out_specs = [], []
    for out in outs:
        kind = out[2] if len(out) > 2 else None
        make = {None: pltpu.VMEM, SAVE: pltpu.HBM, FREE: jax.ShapeDtypeStruct}[kind]
        out_shape.append(make(out[0], out[1]))
        out_specs.append(pl.BlockSpec(memory_space=pltpu.HBM if kind == SAVE else pltpu.VMEM))
    count, waits, n_outs, n_own = len(args), len(after), len(outs), len(scratch)
    buffers = [pltpu.VMEM(arg.shape, arg.dtype) for _, arg in held]
    buffers += [pltpu.VMEM(*outs[place][:2]) for place in saved]
    moves = len(buffers)

    def run(*refs):
        ins = list(refs[:count])
        results = list(refs[count + waits : count + waits + n_outs])
        rest = refs[count + waits + n_outs :]
        own, targets = rest[:n_own], rest[n_own : n_own + moves]
        semaphores = rest[-1] if moves else None
        for order, (place, arg) in enumerate(held):
            ins[place] = Arriving(arg.part(ins[place]), targets[order], semaphores.at[order])
        for order, place in enumerate(saved, len(held)):
            results[place] = Leaving(targets[order], results[place], semaphores.at[order])
        kernel(*ins, *results, *own)
        for place, _ in held:
            ins[place].arrive()
        for place in saved:
            results[place].leave()
        for place in saved:
            results[place].copy.wait()

    results = pl.pallas_call(
        run,
        out_shape=out_shape,
        in_specs=specs + [pl.BlockSpec(memory_space=pl.ANY)] * waits,
        out_specs=out_specs,
        scratch_shapes=list(scratch) + buffers + ([pltpu.SemaphoreType.DMA((moves,))] if moves else []),
        compiler_params=pltpu.CompilerParams(vmem_limit_bytes=vmem * 1024 * 1024),
        cost_estimate=pl.CostEstimate(flops=int(1e5 + time * 1e9), bytes_accessed=1, transcendentals=0),
    )(*arrays, *after)
    return [Held(r) if place in saved else r for place, r in enumerate(results)]


def token_marks(boxes, pages):
    first = lax.axis_index("stream") == 0
    own = jnp.where(first, pages[0:1, :], pages[1:2, :])
    far = jnp.where(first, pages[1:2, :], pages[0:1, :])
    rows = jnp.concatenate([boxes[...], own, far, boxes[...], own, far], axis=0).astype(F32)
    return rows, jnp.transpose(rows)


def page_mask(cols, rows):
    return jnp.where(cols == rows, 0.0, MASKED).astype(F32)


def key_marks(cols, levels):
    lane = iota((cols.shape[0], LANES), 1)
    want = (levels - lane % levels).astype(F32)
    picked = jnp.where((lane // levels) % 2 == 0, cols[:, 0:1], cols[:, 1:2])
    return (picked == want).astype(F32).astype(LOW)


def query_marks(cols, levels):
    lane = iota((cols.shape[0], LANES), 1).astype(F32)
    hit = (lane == levels - cols[:, 0:1]) | (lane == levels + 40 - cols[:, 1:2])
    return hit.astype(F32).astype(LOW)


def bias_rows(table, head, levels):
    lane = iota((40, LANES), 1)
    blocks = []
    for dim in range(2):
        line = table[head][dim : dim + 1, :]
        line = jnp.concatenate(
            [line, jnp.broadcast_to(line[:, -1:], (1, LANES - line.shape[1]))], axis=1
        )
        base = jnp.broadcast_to(pltpu.roll(line, LANES - levels, 1), (40, LANES))
        spread = pltpu.roll(base, 0, 1, stride=1, stride_axis=0)
        spread = jnp.where(lane < levels, spread - spread[:, levels : levels + 1], 0.0)
        upper = spread.astype(LOW).astype(F32)
        lower = spread - upper
        blocks.append(
            pltpu.roll(upper, dim * levels, 1) + pltpu.roll(lower, (2 + dim) * levels, 1)
            if dim
            else upper + pltpu.roll(lower, 2 * levels, 1)
        )
    blocks.append(jnp.zeros((LANES - 80, LANES), F32))
    return jnp.concatenate(blocks, axis=0).astype(LOW)


def half_masks():
    lane = iota((1, LANES), 1)
    first = (lane < HEAD_DIM).astype(F32).astype(LOW)
    return first, (1 - first.astype(F32)).astype(LOW)


def attend(q_ref, k_ref, v_ref, ext_ref, key_ext, mask, lse_ref, ctx_ref):
    seq, width = q_ref.shape
    halves = half_masks()
    lane = iota((seq, LANES), 1)
    ones = jnp.ones((seq, LANES), LOW)
    lse = jnp.zeros((seq, LANES), F32)
    for pair in range(width // LANES):
        at = slice(pair * LANES, (pair + 1) * LANES)
        queries, keys = q_ref[:, at], k_ref[:, at]
        if key_ext is not None:
            keys = jnp.concatenate([keys, key_ext], axis=1)
        values = jnp.concatenate([v_ref[:, at], ones], axis=1)
        parts = []
        for half in range(2):
            head = 2 * pair + half
            left = queries * halves[half]
            if key_ext is not None:
                left = jnp.concatenate([left, ext_ref[:, head * LANES : (head + 1) * LANES]], axis=1)
            scores = dot_nt(left, keys) + mask
            top = jnp.max(scores, -1, keepdims=True)
            weights = jnp.exp(scores - top).astype(LOW)
            out = dot(weights, values)
            total = out[:, LANES:]
            parts.append(out[:, :LANES] / total)
            lse = jnp.where(lane == head, top + jnp.log(total), lse)
        ctx_ref[:, at] = jnp.where(lane < HEAD_DIM, parts[0], parts[1]).astype(LOW)
    lse_ref[...] = lse
    leave(lse_ref, ctx_ref)


def put_halves(value, first, second):
    half = first.shape[0]
    first[...] = value[:half].astype(LOW)
    second[...] = value[half:].astype(LOW)


def summed(parts):
    first, second, far_first, far_second = (ref[...].astype(F32) for ref in parts)
    return jnp.concatenate([first + far_first, second + far_second], axis=0)


def first_attention(levels, x, wq, wk, wv, boxes, pages, table, wo, part, part2, q, k, v, lse, ctx, ext):
    states = x[...]
    q[...] = (dot(states, wq[...]).astype(LOW).astype(F32) * SCALE).astype(LOW)
    k[...] = dot(states, wk[...]).astype(LOW)
    v[...] = dot(states, wv[...]).astype(LOW)
    leave(q, k, v)
    rows, cols = token_marks(boxes, pages)
    marks = query_marks(cols, levels)
    tables = [table[head] for head in range(table.shape[0])]
    for head in range(q.shape[1] // HEAD_DIM):
        ext[:, head * LANES : (head + 1) * LANES] = dot(
            marks, bias_rows(tables, head, levels)
        ).astype(LOW)
    leave(ext)
    mask = page_mask(cols[:, 2:3], rows[2:3, :])
    attend(q, k, v, ext, key_marks(cols, levels), mask, lse, ctx)
    put_halves(dot(ctx[...], wo[...]), part, part2)


def next_states(own, own2, far, far2, mixed, gain, shift, combined, hidden, rounded, share):
    xhat, _ = normalized(mixed[...])
    total = xhat * gain[0:1, :] + shift[0:1, :] + summed((own, own2, far, far2))
    combined[...] = total
    leave(combined)
    xhat, _ = normalized(total)
    state = xhat * gain[1:2, :] + shift[1:2, :]
    hidden[...] = state
    rounded[...] = state.astype(LOW)
    leave(hidden, rounded)
    half = share.shape[0]
    share[...] = rounded[pl.ds(pl.multiple_of(lax.axis_index("mp") * half, half), half), :]


def next_queries(rounded, wq, q):
    q[...] = (dot(rounded[...], wq[...]).astype(LOW).astype(F32) * SCALE).astype(LOW)


def next_attention(near_half, far_half, weights, q, boxes, pages, wo, part, part2, k, v, lse, ctx):
    half, width = near_half.shape[0], q.shape[1]
    far_weights = weights[...]
    here = lax.axis_index("mp")
    for index, states in ((here, near_half), (1 - here, far_half)):
        both = dot(states[...], far_weights).astype(LOW)
        at = pl.ds(pl.multiple_of(index * half, half), half)
        k[at, :] = both[:, :width]
        v[at, :] = both[:, width:]
    leave(k, v)
    rows, cols = token_marks(boxes, pages)
    mask = page_mask(cols[:, 2:3], rows[3:4, :])
    attend(q, k, v, None, None, mask, lse, ctx)
    put_halves(dot(ctx[...], wo[...]), part, part2)


def normal_cdf(values):
    return 0.5 * (1.0 + lax.erf(values * (0.5**0.5)))


def feed_forward(own, own2, far, far2, hidden, gain, shift, *refs):
    weights, (mixed, middle, upward, active, part, part2) = refs[:-6], refs[-6:]
    total = hidden[...].astype(F32) + summed((own, own2, far, far2))
    mixed[...] = total
    xhat, _ = normalized(total)
    low = (xhat * gain[0:1, :] + shift[0:1, :]).astype(LOW)
    middle[...] = low
    leave(mixed, middle)
    step = weights[0].shape[1]
    acc = None
    for index in range(len(weights) // 2):
        at = slice(index * step, (index + 1) * step)
        up = dot(low, weights[2 * index][...])
        upward[:, at] = up.astype(LOW)
        act = (up * normal_cdf(up)).astype(LOW)
        active[:, at] = act
        piece = dot(act, weights[2 * index + 1][...])
        acc = piece if acc is None else acc + piece
    leave(upward, active)
    put_halves(acc, part, part2)


def feed_back_body(grad, combined, gain, weights, upward, grad_comb, down_cot, grad_up, part, part2, dgain, dshift):
    xhat, rstd = normalized(combined)
    grad_in, dgain[...], dshift[...] = norm_back(grad, xhat, rstd, gain)
    grad_comb[...] = grad_in
    low = grad_in.astype(LOW)
    down_cot[...] = low
    step = weights[0].shape[1]
    acc = None
    for index in range(len(weights) // 2):
        at = slice(index * step, (index + 1) * step)
        back = dot_nt(low, weights[2 * index + 1][...])
        up = upward[:, at].astype(F32)
        slope = normal_cdf(up) + up * (jnp.exp(-0.5 * up * up) * 0.3989422804014327)
        gup = (back * slope).astype(LOW)
        grad_up[:, at] = gup
        piece = dot_nt(gup, weights[2 * index][...])
        acc = piece if acc is None else acc + piece
    put_halves(acc, part, part2)


def last_feed_back(own, own2, far, far2, mixed, gain, shift, cot, upward, *refs):
    weights, (output, *outs) = refs[:-8], refs[-8:]
    xhat, _ = normalized(mixed[...])
    combined = xhat * gain[0:1, :] + shift[0:1, :] + summed((own, own2, far, far2))
    xhat, _ = normalized(combined)
    output[...] = (xhat * gain[1:2, :] + shift[1:2, :]).astype(LOW)
    feed_back_body(cot[...].astype(F32), combined, gain[1:2, :], weights, upward, *outs)


def first_feed_back(own, own2, far, far2, grad_mixed, combined, gain, upward, *refs):
    weights, outs = refs[:-7], refs[-7:]
    grad = grad_mixed[...] + summed((own, own2, far, far2))
    feed_back_body(grad, combined[...], gain[1:2, :], weights, upward, *outs)


def attention_back_body(levels, page_row, own, own2, far, far2, grad_comb, mixed, gain, wo, q, k, v, lse, ctx, ext, boxes, pages, grad_mixed, out_cot, gq, gkt, gvt, dgain, dshift, dtable):
    seq, width = q.shape
    grad = grad_comb[...] + summed((own, own2, far, far2))
    xhat, rstd = normalized(mixed[...])
    grad_in, dgain[...], dshift[...] = norm_back(grad, xhat, rstd, gain[0:1, :])
    grad_mixed[...] = grad_in
    low = grad_in.astype(LOW)
    out_cot[...] = low
    gctx = dot_nt(low, wo[...]).astype(LOW)
    rows, cols = token_marks(boxes, pages)
    mask = page_mask(cols[:, 2:3], rows[page_row : page_row + 1, :])
    halves = half_masks()
    lane = iota((seq, LANES), 1)
    if ext is not None:
        key_ext = key_marks(cols, levels)
        place = lane.astype(F32)
        back_ext = (
            (place == levels - cols[:, 0:1]) | (place == levels + HEAD_DIM - cols[:, 1:2])
        ).astype(F32).astype(LOW)
        line = iota((LANES, seq), 0).astype(F32)
        marks_t = ((line == rows[0:1, :]) | (line == rows[1:2, :] + HEAD_DIM)).astype(F32).astype(LOW)
        dtable[...] = jnp.zeros(dtable.shape, F32)
    for pair in range(width // LANES):
        at = slice(pair * LANES, (pair + 1) * LANES)
        queries, keys, values = q[:, at], k[:, at], v[:, at]
        gc = gctx[:, at]
        product = gc.astype(F32) * ctx[:, at].astype(F32)
        gc_t = jnp.transpose(gc)
        q_t = jnp.transpose(queries)
        keys_left = keys if ext is None else jnp.concatenate([keys, key_ext], axis=1)
        keys_right = keys if ext is None else jnp.concatenate([keys, back_ext], axis=1)
        parts = []
        for half in range(2):
            head = 2 * pair + half
            rows_at = slice(half * HEAD_DIM, (half + 1) * HEAD_DIM)
            out_at = slice(head * HEAD_DIM, (head + 1) * HEAD_DIM)
            left = queries * halves[half]
            if ext is not None:
                left = jnp.concatenate([left, ext[:, head * LANES : (head + 1) * LANES]], axis=1)
            scores = dot_nt(left, keys_left) + mask
            probs = jnp.exp(scores - lse[:, head : head + 1])
            delta = jnp.sum(
                jnp.where((lane < HEAD_DIM) == (half == 0), product, 0.0), -1, keepdims=True
            )
            grad_scores = probs * (dot_nt(gc * halves[half], values) - delta)
            score_cot = grad_scores.astype(LOW)
            gvt[out_at, :] = dot(gc_t[rows_at, :], probs.astype(LOW)).astype(LOW)
            gkt[out_at, :] = dot(q_t[rows_at, :], score_cot).astype(LOW)
            out = dot(score_cot, keys_right)
            parts.append(out[:, :LANES])
            if ext is not None:
                spread = out[:, LANES:]
                upper = spread.astype(LOW)
                lower = (spread - upper.astype(F32)).astype(LOW)
                block = dot(marks_t, upper) + dot(marks_t, lower)
                small = iota((40, LANES), 1)
                for dim in range(2):
                    piece = block[dim * HEAD_DIM : dim * HEAD_DIM + 40, :]
                    if dim:
                        piece = pltpu.roll(piece, HEAD_DIM, 1)
                    piece = jnp.where(small <= levels, piece, 0.0)
                    piece = pltpu.roll(piece, 0, 1, stride=1, stride_axis=0)
                    line = jnp.sum(piece, 0, keepdims=True)
                    over = pltpu.roll(line, LANES - 1, 1)
                    place = iota((1, LANES), 1)
                    line = jnp.where(place == 2 * levels - 1, line + over, line)
                    dtable[dim, head : head + 1, :] = line
        gq[:, at] = (jnp.where(lane < HEAD_DIM, parts[0], parts[1]) * SCALE).astype(LOW)


def next_attention_back(own, own2, far, far2, grad_comb, mixed, gain, wo, q, k, v, lse, ctx, boxes, pages, *outs):
    attention_back_body(0, 3, own, own2, far, far2, grad_comb, mixed, gain, wo, q, k, v, lse, ctx, None, boxes, pages, *outs, None)


def first_attention_back(levels, own, own2, far, far2, grad_comb, mixed, gain, wo, q, k, v, lse, ctx, ext, boxes, pages, wq, wk, wv, *outs):
    outs, parts = outs[:-2], outs[-2:]
    attention_back_body(levels, 2, own, own2, far, far2, grad_comb, mixed, gain, wo, q, k, v, lse, ctx, ext, boxes, pages, *outs)
    input_back(*outs[2:5], wq, wk, wv, *parts)


def input_back(gq, gkt, gvt, wq, wk, wv, part, part2):
    put_halves(
        dot_nt(gq[...], wq[...])
        + dot_nt(jnp.transpose(gkt[...]), wk[...])
        + dot_nt(jnp.transpose(gvt[...]), wv[...]),
        part,
        part2,
    )


def slice_order(bits):
    count = len(bits)
    return [
        sum(bit for place, bit in enumerate(bits) if block >> (count - 1 - place) & 1)
        for block in range(1 << count)
    ]


def arranged(order, source, held, moved):
    held[...] = jnp.transpose(source[...])
    if order is None:
        return held
    size = held.shape[0] // len(order)
    here = lax.axis_index("dp")
    for block, flip in enumerate(order):
        at = pl.multiple_of((here ^ flip) * size, size)
        moved[block * size : (block + 1) * size, :] = held[pl.ds(at, size), :]
    return moved


def weight_products(order, plan, parts, *refs):
    groups, position = [], 0
    for kinds in plan:
        stop = position + 1 + len(kinds)
        groups.append((refs[position], list(zip(refs[position + 1 : stop], kinds))))
        position = stop
    outs, scratch = refs[position : position + parts], refs[position + parts :]
    column = 0
    for place, (source, rights) in enumerate(groups):
        left = arranged(order, source, scratch[2 * place], scratch[2 * place + 1])
        for right, flipped in rights:
            wide = right.shape[0] if flipped else right.shape[1]
            step = 384 if flipped else min(512, wide)
            for start in range(0, wide, step):
                for index in reversed(range(parts)):
                    size = outs[index].shape[0]
                    rows = left[index * size : (index + 1) * size, :]
                    if flipped:
                        block = dot_nt(rows, right[start : start + step, :])
                    else:
                        block = dot(rows, right[:, start : start + step])
                    outs[index][:, column + start : column + start + step] = block.astype(LOW)
            column += wide


def weight_gradients(order, groups, after=()):
    plan, args, columns = [], [], 0
    for left, rights in groups:
        plan.append([flipped for _, flipped in rights])
        args.append(left)
        for right, flipped in rights:
            args.append(right)
            columns += right.shape[0] if flipped else right.shape[1]
    seq, d_model = groups[0][0].shape
    parts = 1 if order is None else 2
    return call(
        functools.partial(weight_products, order, plan, parts),
        [((d_model // parts, columns), LOW)] * parts,
        *args, after=after, scratch=[pltpu.VMEM((d_model, seq), LOW)] * (2 * len(groups)),
    )


def merge_kernel(kept, got, keep, send):
    half = keep.shape[0]
    send[...] = (kept[half:, :].astype(F32) + got[half:, :].astype(F32)).astype(LOW)
    keep[...] = (kept[:half, :].astype(F32) + got[:half, :].astype(F32)).astype(LOW)


def merge(kept, got, after=()):
    half = ((kept.shape[0] // 2, kept.shape[1]), LOW)
    return call(merge_kernel, [half, half], kept, got, after=after)


def finish_kernel(plan, count, *refs):
    outs = refs[-count:]
    for place, targets in enumerate(plan):
        kept, got = refs[2 * place], refs[2 * place + 1]
        wide = kept.shape[1] // len(targets)
        for block, (out, layer) in enumerate(targets):
            at = slice(block * wide, (block + 1) * wide)
            outs[out][layer] = kept[:, at].astype(F32) + got[:, at].astype(F32)


def finish(plan, pairs, count, after=()):
    size, columns = pairs[0][0].shape
    outs = [((2, size, columns // len(plan[0])), F32, FREE)] * count
    return call(functools.partial(finish_kernel, plan, count), outs, *[a for pair in pairs for a in pair], after=after)


def pack_kernel(*refs):
    table, out = refs[-2], refs[-1]
    lines = len(refs) - 2
    for place in range(lines):
        out[place : place + 1, :] = refs[place][...]
    rows = table.shape[1]
    rest = jnp.zeros((rows, out.shape[1] - LANES), F32)
    for dim in range(2):
        at = slice(lines + dim * rows, lines + (dim + 1) * rows)
        out[at, :] = jnp.concatenate([table[dim], rest], axis=1)


def other(block, axis):
    return lax.ppermute(block, axis, [(0, 1), (1, 0)])


def body(inputs, w_query, w_key, w_value, w_out, w_up, w_down, norm_gain, norm_shift, box_table, boxes, pages, cotangent):
    _, rows_here, seq, d_model = inputs.shape
    assert rows_here == 1
    width = w_query.shape[3]
    hidden_width = w_up.shape[3]
    heads = width // HEAD_DIM
    levels = box_table.shape[3] // 2
    n_dp = lax.axis_size("dp")
    me = lax.axis_index("dp")
    bits = [1 << place for place in range(n_dp.bit_length() - 1)]
    near_first = far_first = None
    if n_dp == 1 << len(bits) and len(bits) == 3 and d_model % (16 * n_dp) == 0:
        far_bits = bits[1:] + bits[:1]
        near_first, far_first = slice_order(bits), slice_order(far_bits)

    def ff_weights(layer):
        cuts = [slice(at, at + 512) for at in range(0, hidden_width, 512)]
        return [w for cut in cuts for w in (Held(w_up, 0, layer, None, cut), Held(w_down, 0, layer, cut))]

    def flip(block, bit):
        return lax.ppermute(block, "dp", [(i, i ^ bit) for i in range(n_dp)])

    def exchange(*parts):
        return [*parts, *(other(part, "mp") for part in parts)]

    wide = ((seq, d_model), F32)
    thin = ((seq, d_model), LOW)
    half = ((seq // 2, d_model), LOW)
    proj = ((seq, width), LOW)
    proj_t = ((width, seq), LOW)
    ff = ((seq, hidden_width), LOW)
    stats = ((seq, LANES), F32)
    vec = ((1, d_model), F32)
    keep = lambda spec: (*spec, SAVE)
    x = Held(inputs, 0, 0)
    box = Held(boxes, 0, None, 0)
    page = Held(pages, None, 0)
    table = Held(jnp.transpose(box_table[0], (1, 0, 2)))
    norms = [[Held(array, 0, layer) for array in (norm_gain, norm_shift)] for layer in range(2)]

    mine = jnp.concatenate([w_key[0, 1], w_value[0, 1]], axis=1)
    far_weights = lax.all_gather(mine, "stream", axis=0, tiled=False)
    part, part2, q0, k0, v0, lse0, ctx0, ext0 = call(
        functools.partial(first_attention, levels),
        [half, half, keep(proj), keep(proj), keep(proj), keep(stats), keep(proj), ((seq, heads * LANES), LOW, SAVE)],
        x, Held(w_query, 0, 0), Held(w_key, 0, 0), Held(w_value, 0, 0), box, page, table, Held(w_out, 0, 0),
        after=[mine], time=7,
    )
    mixed0, middle0, upward0, active0, part, part2 = call(
        feed_forward, [keep(wide), keep(thin), keep(ff), keep(ff), half, half],
        *exchange(part, part2), x, *norms[0], *ff_weights(0), time=5,
    )
    combined0, hidden1, rounded1, share = call(
        next_states, [keep(wide), keep(wide), keep(thin), half],
        *exchange(part, part2), mixed0, *norms[0], time=2,
    )
    near_half = other(share, "stream")
    (q1,) = call(next_queries, [keep(proj)], rounded1, Held(w_query, 0, 1), time=1)
    far_half = other(near_half, "mp")
    part, part2, k1, v1, lse1, ctx1 = call(
        next_attention, [half, half, keep(proj), keep(proj), keep(stats), keep(proj)],
        near_half, far_half, Held(far_weights, lambda: 1 - lax.axis_index("stream")), q1, box, page, Held(w_out, 0, 1), time=5,
    )
    mixed1, middle1, upward1, active1, part, part2 = call(
        feed_forward, [keep(wide), keep(thin), keep(ff), keep(ff), half, half],
        *exchange(part, part2), hidden1, *norms[1], *ff_weights(1), time=5,
    )
    output, grad_comb, down_cot, grad_up, part, part2, dgain11, dshift11 = call(
        last_feed_back, [(*thin, FREE), wide, thin, ff, half, half, vec, vec],
        *exchange(part, part2), mixed1, *norms[1], Held(cotangent, 0, 0), upward1, *ff_weights(1),
    )
    ff1 = weight_gradients(near_first, [(down_cot, [(active1, False)]), (middle1, [(grad_up, False)])])
    if near_first:
        got_ff1 = flip(ff1[1], bits[0])
    grad_mixed, out_cot, gq, gkt, gvt, dgain10, dshift10 = call(
        next_attention_back, [wide, thin, proj, proj_t, proj_t, vec, vec],
        *exchange(part, part2), grad_comb, mixed1, norms[1][0], Held(w_out, 0, 1),
        q1, k1, v1, lse1, ctx1, box, page, after=[ff1[-1]],
    )
    gkt, gvt = other(gkt, "stream"), other(gvt, "stream")
    qo1 = weight_gradients(far_first, [(rounded1, [(gq, False)]), (out_cot, [(ctx1, False)])])
    if near_first:
        got_qo1 = flip(qo1[1], far_bits[0])
    part, part2 = call(
        input_back, [half, half], gq, gkt, gvt, Held(w_query, 0, 1), Held(w_key, 0, 1), Held(w_value, 0, 1), after=[qo1[-1]]
    )
    kv1 = weight_gradients(far_first, [(rounded1, [(gkt, True), (gvt, True)])])
    before = [kv1[-1]]
    if near_first:
        got_kv1 = flip(kv1[1], far_bits[0])
        qo1 = merge(qo1[0], got_qo1)
        got_qo1 = flip(qo1[1], far_bits[1])
        before.append(qo1[1])
    grad_comb, down_cot, grad_up, part, part2, dgain01, dshift01 = call(
        first_feed_back, [wide, thin, ff, half, half, vec, vec],
        *exchange(part, part2), grad_mixed, combined0, norms[0][0], upward0, *ff_weights(0), after=before,
    )
    ff0 = weight_gradients(near_first, [(down_cot, [(active0, False)]), (middle0, [(grad_up, False)])])
    before = [ff0[-1]]
    if near_first:
        got_ff0 = flip(ff0[1], bits[0])
        kv1 = merge(kv1[0], got_kv1)
        got_kv1 = flip(kv1[1], far_bits[1])
        ff1 = merge(ff1[0], got_ff1, after=[kv1[1]])
        got_ff1 = flip(ff1[1], bits[1])
        before.append(ff1[1])
    grad_mixed, out_cot, gq, gkt, gvt, dgain00, dshift00, dtable, part, part2 = call(
        functools.partial(first_attention_back, levels),
        [wide, thin, proj, proj_t, proj_t, vec, vec, ((2, 8, LANES), F32), half, half],
        *exchange(part, part2), grad_comb, mixed0, norms[0][0], Held(w_out, 0, 0),
        q0, k0, v0, lse0, ctx0, ext0, box, page, Held(w_query, 0, 0), Held(w_key, 0, 0), Held(w_value, 0, 0), after=before,
    )
    at0 = weight_gradients(
        near_first, [(x, [(gq, False), (gkt, True), (gvt, True)]), (out_cot, [(ctx0, False)])]
    )
    (small,) = call(
        pack_kernel, [((24, d_model), F32)],
        dgain00, dgain01, dgain10, dgain11, dshift00, dshift01, dshift10, dshift11, dtable, after=[at0[-1]],
    )
    far = [other(p, "mp") for p in (part, part2)]
    grad_inputs = grad_mixed + jnp.concatenate(
        [own.astype(F32) + got.astype(F32) for own, got in zip((part, part2), far)], axis=0
    )
    if near_first:
        got_at0 = flip(at0[1], bits[0])
        qo1 = merge(qo1[0], got_qo1, after=[small])
        got_qo1 = flip(qo1[1], far_bits[2])
        kv1 = merge(kv1[0], got_kv1, after=[qo1[1]])
        got_kv1 = flip(kv1[1], far_bits[2])
        small = small + flip(small, bits[1])
        ff1 = merge(ff1[0], got_ff1, after=[kv1[1]])
        got_ff1 = flip(ff1[1], bits[2])
        small = small + flip(small, bits[2])
        ff0 = merge(ff0[0], got_ff0, after=[ff1[1]])
        got_ff0 = flip(ff0[1], bits[1])
        at0 = merge(at0[0], got_at0, after=[ff0[1]])
        got_at0 = flip(at0[1], bits[1])
        small = small + flip(small, bits[0])
        ff0 = merge(ff0[0], got_ff0, after=[at0[1]])
        got_ff0 = flip(ff0[1], bits[2])
        at0 = merge(at0[0], got_at0, after=[ff0[1]])
        got_at0 = flip(at0[1], bits[2])
        ff0, ff1, at0, qo1, kv1 = (
            (ff0[0], got_ff0), (ff1[0], got_ff1), (at0[0], got_at0), (qo1[0], got_qo1), (kv1[0], got_kv1)
        )
    else:
        small = lax.psum(small, "dp")
        ff0, ff1, at0, qo1, kv1 = (
            (lax.psum_scatter(g[0], "dp", scatter_dimension=0, tiled=True), jnp.zeros((d_model // n_dp, g[0].shape[1]), LOW))
            for g in (ff0, ff1, at0, qo1, kv1)
        )
    grad_down, grad_up = finish([[(0, 0), (1, 0)], [(0, 1), (1, 1)]], [ff0, ff1], 2)
    grad_q, grad_k, grad_v, grad_o = finish(
        [[(0, 0), (1, 0), (2, 0), (3, 0)], [(0, 1), (3, 1)], [(1, 1), (2, 1)]], [at0, qo1, kv1], 4
    )
    cut = d_model // n_dp
    vectors = lax.dynamic_slice_in_dim(small[:8], me * cut, cut, 1).reshape(2, 2, 2, cut)
    cut = 2 * levels // n_dp
    grad_table = lax.dynamic_slice_in_dim(small[8:], me * cut, cut, 1).reshape(1, 2, 8, cut)[:, :, :heads]
    flipped = lambda block: jnp.transpose(block, (0, 2, 1))[None]
    return (
        output[None, None],
        grad_inputs[None, None],
        grad_q[None],
        grad_k[None],
        grad_v[None],
        flipped(grad_o),
        grad_up[None],
        flipped(grad_down),
        vectors[:1],
        vectors[1:],
        grad_table,
    )


def solution(mesh):
    in_specs = (
        P("stream", "dp", None, None),
        P("stream", None, None, "mp"),
        P("stream", None, None, "mp"),
        P("stream", None, None, "mp"),
        P("stream", None, "mp", None),
        P("stream", None, None, "mp"),
        P("stream", None, "mp", None),
        P("stream", None, None, None),
        P("stream", None, None, None),
        P("stream", None, "mp", None),
        P("stream", None, "dp", None),
        P(None, "dp", None),
        P("stream", "dp", None, None),
    )
    out_specs = (
        P("stream", "dp", None, None),
        P("stream", "dp", None, None),
        P("stream", None, "dp", "mp"),
        P("stream", None, "dp", "mp"),
        P("stream", None, "dp", "mp"),
        P("stream", None, "mp", "dp"),
        P("stream", None, "dp", "mp"),
        P("stream", None, "mp", "dp"),
        P("stream", None, None, "dp"),
        P("stream", None, None, "dp"),
        P("stream", None, "mp", "dp"),
    )
    return jax.shard_map(body, mesh=mesh, in_specs=in_specs, out_specs=out_specs, check_vma=False)
```

```python
import functools

import jax
import jax.numpy as jnp
from jax import lax
from jax.experimental import pallas as pl
from jax.experimental.pallas import tpu as pltpu
from jax.sharding import PartitionSpec as P

HEAD_DIM = 64
EPSILON = 1e-05
MASKED = -1e30
LOW = jnp.bfloat16
F32 = jnp.float32
LANES = 128
SCALE = HEAD_DIM ** (-0.5)


def dot(left, right):
    return lax.dot_general(left, right, (((1,), (0,)), ((), ())), preferred_element_type=F32)


def dot_nt(left, right):
    return lax.dot_general(left, right, (((1,), (1,)), ((), ())), preferred_element_type=F32)


def iota(shape, dim):
    return lax.broadcasted_iota(jnp.int32, shape, dim)


def normalized(values):
    center = values - jnp.mean(values, -1, keepdims=True)
    rstd = lax.rsqrt(jnp.mean(center * center, -1, keepdims=True) + EPSILON)
    return center * rstd, rstd


def norm_back(grad, xhat, rstd, gain):
    scaled = grad * gain
    grad_in = rstd * (
        scaled
        - jnp.mean(scaled, -1, keepdims=True)
        - xhat * jnp.mean(scaled * xhat, -1, keepdims=True)
    )
    return grad_in, jnp.sum(grad * xhat, 0, keepdims=True), jnp.sum(grad, 0, keepdims=True)


class Held:
    def __init__(self, array, *index):
        self.array, self.dtype = array, array.dtype
        self.index = tuple(slice(None) if i is None else i for i in index)
        plain = tuple(0 if callable(i) else i for i in self.index)
        self.shape = jax.eval_shape(lambda: jnp.zeros(array.shape, jnp.int8)[plain]).shape

    def part(self, ref):
        return ref.at[tuple(i() if callable(i) else i for i in self.index)] if self.index else ref


class Arriving:
    def __init__(self, source, target, semaphore):
        self.copy = pltpu.make_async_copy(source, target, semaphore)
        self.copy.start()
        self.target, self.waited = target, False
        self.shape, self.dtype = target.shape, target.dtype

    def arrive(self):
        if not self.waited:
            self.copy.wait()
        self.waited = True

    def __getitem__(self, at):
        self.arrive()
        return self.target[at]


class Leaving:
    def __init__(self, source, target, semaphore):
        self.copy = pltpu.make_async_copy(source, target, semaphore)
        self.source, self.left = source, False
        self.shape, self.dtype = source.shape, source.dtype

    def leave(self):
        if not self.left:
            self.copy.start()
        self.left = True

    def __getitem__(self, at):
        return self.source[at]

    def __setitem__(self, at, value):
        self.source[at] = value


def leave(*refs):
    for ref in refs:
        if isinstance(ref, Leaving):
            ref.leave()


SAVE = "save"
BOTH = "both"
FREE = "free"
FORE = 4
BACK = 2
TOKEN = ((8, LANES), F32)


def call(kernel, outs, *args, after=(), fetch=(), scratch=(), vmem=24, time=0.0):
    arrays, specs, held = [], [], []
    for place, arg in enumerate(args):
        if isinstance(arg, Held):
            specs.append(pl.BlockSpec(memory_space=pltpu.HBM))
            arrays.append(pltpu.with_memory_space_constraint(arg.array, pltpu.HBM))
            held.append((place, arg))
        else:
            specs.append(pl.BlockSpec(memory_space=pltpu.VMEM))
            arrays.append(pltpu.with_memory_space_constraint(arg, pltpu.VMEM))
    arrays += list(after)
    specs += [pl.BlockSpec(memory_space=pl.ANY)] * len(after)
    for arg in fetch:
        specs.append(pl.BlockSpec(memory_space=pltpu.HBM))
        arrays.append(pltpu.with_memory_space_constraint(arg.array, pltpu.HBM))
    kinds = [out[2] if len(out) > 2 else None for out in outs]
    saved = [place for place, kind in enumerate(kinds) if kind == SAVE]
    both = [place for place, kind in enumerate(kinds) if kind == BOTH]
    out_shape, out_specs = [], []
    for out, kind in zip(outs, kinds):
        make = {None: pltpu.VMEM, BOTH: pltpu.VMEM, SAVE: pltpu.HBM, FREE: jax.ShapeDtypeStruct}[kind]
        out_shape.append(make(out[0], out[1]))
        out_specs.append(pl.BlockSpec(memory_space=pltpu.HBM if kind == SAVE else pltpu.VMEM))
    for place in both:
        out_shape.append(pltpu.HBM(*outs[place][:2]))
        out_specs.append(pl.BlockSpec(memory_space=pltpu.HBM))
    for arg in fetch:
        out_shape.append(pltpu.VMEM(arg.shape, arg.dtype))
        out_specs.append(pl.BlockSpec(memory_space=pltpu.VMEM))
    count, waits, fetched, n_outs, n_own = len(args), len(after), len(fetch), len(outs), len(scratch)
    buffers = [pltpu.VMEM(arg.shape, arg.dtype) for _, arg in held]
    buffers += [pltpu.VMEM(*outs[place][:2]) for place in saved]
    moves = len(buffers) + len(both) + fetched

    def run(*refs):
        refs = list(refs)
        take = lambda size: [refs.pop(0) for _ in range(size)]
        ins, _, sources, results = take(count), take(waits), take(fetched), take(n_outs)
        copies, fetches, own, targets = take(len(both)), take(fetched), take(n_own), take(len(buffers))
        semaphores = [refs[0].at[order] for order in range(moves)] if moves else []
        for place, arg in held:
            ins[place] = Arriving(arg.part(ins[place]), targets.pop(0), semaphores.pop(0))
        for place in saved:
            results[place] = Leaving(targets.pop(0), results[place], semaphores.pop(0))
        for place in both:
            results[place] = Leaving(results[place], copies.pop(0), semaphores.pop(0))
        coming = [Arriving(arg.part(ref), out, semaphores.pop(0)) for arg, ref, out in zip(fetch, sources, fetches)]
        kernel(*ins, *results, *own)
        for place, _ in held:
            ins[place].arrive()
        for ref in coming:
            ref.arrive()
        for place in saved + both:
            results[place].leave()
        for place in saved + both:
            results[place].copy.wait()

    results = pl.pallas_call(
        run,
        out_shape=out_shape,
        in_specs=specs,
        out_specs=out_specs,
        scratch_shapes=list(scratch) + buffers + ([pltpu.SemaphoreType.DMA((moves,))] if moves else []),
        compiler_params=pltpu.CompilerParams(vmem_limit_bytes=vmem * 1024 * 1024),
        cost_estimate=pl.CostEstimate(flops=int(1e5 + time * 1e9), bytes_accessed=1, transcendentals=0),
    )(*arrays)
    wrapped = [Held(r) if place in saved else r for place, r in enumerate(results[:n_outs])]
    wrapped += [Held(r) for r in results[n_outs : n_outs + len(both)]]
    return wrapped + list(results[n_outs + len(both) :])


def token_marks(boxes, pages):
    first = lax.axis_index("stream") == 0
    own = jnp.where(first, pages[0:1, :], pages[1:2, :])
    far = jnp.where(first, pages[1:2, :], pages[0:1, :])
    rows = jnp.concatenate([boxes[...], own, far, boxes[...], own, far], axis=0).astype(F32)
    return rows, jnp.transpose(rows)


def page_mask(cols, rows):
    return jnp.where(cols == rows, 0.0, MASKED).astype(F32)


def key_marks(cols, levels):
    lane = iota((cols.shape[0], LANES), 1)
    want = (levels - lane % levels).astype(F32)
    picked = jnp.where((lane // levels) % 2 == 0, cols[:, 0:1], cols[:, 1:2])
    return (picked == want).astype(F32).astype(LOW)


def query_marks(cols, levels):
    lane = iota((cols.shape[0], LANES), 1).astype(F32)
    hit = (lane == levels - cols[:, 0:1]) | (lane == levels + 40 - cols[:, 1:2])
    return hit.astype(F32).astype(LOW)


def bias_rows(table, head, levels):
    lane = iota((40, LANES), 1)
    blocks = []
    for dim in range(2):
        line = table[head][dim : dim + 1, :]
        line = jnp.concatenate(
            [line, jnp.broadcast_to(line[:, -1:], (1, LANES - line.shape[1]))], axis=1
        )
        base = jnp.broadcast_to(pltpu.roll(line, LANES - levels, 1), (40, LANES))
        spread = pltpu.roll(base, 0, 1, stride=1, stride_axis=0)
        spread = jnp.where(lane < levels, spread - spread[:, levels : levels + 1], 0.0)
        upper = spread.astype(LOW).astype(F32)
        lower = spread - upper
        blocks.append(
            pltpu.roll(upper, dim * levels, 1) + pltpu.roll(lower, (2 + dim) * levels, 1)
            if dim
            else upper + pltpu.roll(lower, 2 * levels, 1)
        )
    blocks.append(jnp.zeros((LANES - 80, LANES), F32))
    return jnp.concatenate(blocks, axis=0).astype(LOW)


def half_masks():
    lane = iota((1, LANES), 1)
    first = (lane < HEAD_DIM).astype(F32).astype(LOW)
    return first, (1 - first.astype(F32)).astype(LOW)


def attend(q_ref, k_ref, v_ref, ext_ref, key_ext, mask, lse_ref, ctx_ref):
    seq, width = q_ref.shape
    halves = half_masks()
    lane = iota((seq, LANES), 1)
    ones = jnp.ones((seq, LANES), LOW)
    lse = jnp.zeros((seq, LANES), F32)
    for pair in range(width // LANES):
        at = slice(pair * LANES, (pair + 1) * LANES)
        queries, keys = q_ref[:, at], k_ref[:, at]
        if key_ext is not None:
            keys = jnp.concatenate([keys, key_ext], axis=1)
        values = jnp.concatenate([v_ref[:, at], ones], axis=1)
        parts = []
        for half in range(2):
            head = 2 * pair + half
            left = queries * halves[half]
            if key_ext is not None:
                left = jnp.concatenate([left, ext_ref[:, head * LANES : (head + 1) * LANES]], axis=1)
            scores = dot_nt(left, keys) + mask
            top = jnp.max(scores, -1, keepdims=True)
            weights = jnp.exp(scores - top).astype(LOW)
            out = dot(weights, values)
            total = out[:, LANES:]
            parts.append(out[:, :LANES] / total)
            lse = jnp.where(lane == head, top + jnp.log(total), lse)
        ctx_ref[:, at] = jnp.where(lane < HEAD_DIM, parts[0], parts[1]).astype(LOW)
    lse_ref[...] = lse
    leave(lse_ref, ctx_ref)


def put_pieces(value, refs):
    size = refs[0].shape[0]
    for place, ref in enumerate(refs):
        ref[...] = value[place * size : (place + 1) * size].astype(LOW)


def summed(parts):
    count = len(parts) // 2
    return jnp.concatenate(
        [own[...].astype(F32) + far[...].astype(F32) for own, far in zip(parts[:count], parts[count:])], axis=0
    )


def first_attention(levels, x, wq, wk, wv, boxes, pages, table, wo, q, k, v, lse, ctx, ext, *parts):
    states = x[...]
    q[...] = (dot(states, wq[...]).astype(LOW).astype(F32) * SCALE).astype(LOW)
    k[...] = dot(states, wk[...]).astype(LOW)
    v[...] = dot(states, wv[...]).astype(LOW)
    leave(q, k, v)
    rows, cols = token_marks(boxes, pages)
    marks = query_marks(cols, levels)
    tables = [table[head] for head in range(table.shape[0])]
    for head in range(q.shape[1] // HEAD_DIM):
        ext[:, head * LANES : (head + 1) * LANES] = dot(
            marks, bias_rows(tables, head, levels)
        ).astype(LOW)
    leave(ext)
    mask = page_mask(cols[:, 2:3], rows[2:3, :])
    attend(q, k, v, ext, key_marks(cols, levels), mask, lse, ctx)
    put_pieces(dot(ctx[...], wo[...]), parts)


def next_states(*refs):
    parts, refs = refs[: 2 * FORE], refs[2 * FORE :]
    mixed, gain, shift, combined, hidden, rounded, *shares = refs
    xhat, _ = normalized(mixed[...])
    total = xhat * gain[0:1, :] + shift[0:1, :] + summed(parts)
    combined[...] = total
    leave(combined)
    xhat, _ = normalized(total)
    state = xhat * gain[1:2, :] + shift[1:2, :]
    hidden[...] = state
    rounded[...] = state.astype(LOW)
    size = shares[0].shape[0]
    first = lax.axis_index("mp") * (size * len(shares))
    for place, share in enumerate(shares):
        share[...] = rounded[pl.ds(pl.multiple_of(first + place * size, size), size), :]


def next_queries(rounded, wq, q):
    q[...] = (dot(rounded[...], wq[...]).astype(LOW).astype(F32) * SCALE).astype(LOW)


def copy_weights(wk, wv, out):
    out[0] = wk[...]
    out[1] = wv[...]


def next_attention(count, *refs):
    near, far, refs = refs[:count], refs[count : 2 * count], refs[2 * count :]
    weights, q, boxes, pages, wo, k, v, lse, ctx, *parts = refs
    size = near[0].shape[0]
    here = lax.axis_index("mp") * (size * count)
    there = size * count - here
    for start, pieces in ((here, near), (there, far)):
        for place, states in enumerate(pieces):
            at = pl.ds(pl.multiple_of(start + place * size, size), size)
            k[at, :] = dot(states[...], weights[0]).astype(LOW)
            v[at, :] = dot(states[...], weights[1]).astype(LOW)
    rows, cols = token_marks(boxes, pages)
    mask = page_mask(cols[:, 2:3], rows[3:4, :])
    attend(q, k, v, None, None, mask, lse, ctx)
    put_pieces(dot(ctx[...], wo[...]), parts)


def normal_cdf(values):
    return 0.5 * (1.0 + lax.erf(values * (0.5**0.5)))


def feed_forward(chunks, *refs):
    parts, refs = refs[: 2 * FORE], refs[2 * FORE :]
    hidden, gain, shift, refs = refs[0], refs[1], refs[2], refs[3:]
    ups, downs, refs = refs[:chunks], refs[chunks : 2 * chunks], refs[2 * chunks :]
    mixed, middle, refs = refs[0], refs[1], refs[2:]
    upward, active, outs = refs[:chunks], refs[chunks : 2 * chunks], refs[2 * chunks :]
    total = hidden[...].astype(F32) + summed(parts)
    mixed[...] = total
    xhat, _ = normalized(total)
    low = (xhat * gain[0:1, :] + shift[0:1, :]).astype(LOW)
    middle[...] = low
    leave(mixed, middle)
    acc = None
    for index in range(chunks):
        up = dot(low, ups[index][...])
        upward[index][...] = up.astype(LOW)
        act = (up * normal_cdf(up)).astype(LOW)
        active[index][...] = act
        leave(upward[index], active[index])
        piece = dot(act, downs[index][...])
        acc = piece if acc is None else acc + piece
    put_pieces(acc, outs)


def down_back(order, chunks, grad, combined, gain, active, refs):
    grad_comb, down_cot, dgain, dshift, *outs, held, moved = refs
    xhat, rstd = normalized(combined)
    grad_in, dgain[...], dshift[...] = norm_back(grad, xhat, rstd, gain)
    grad_comb[...] = grad_in
    down_cot[...] = grad_in.astype(LOW)
    multiply(order, [(down_cot, [(ref, False) for ref in active])], outs, [held, moved])


def last_down_back(order, chunks, *refs):
    parts, refs = refs[: 2 * FORE], refs[2 * FORE :]
    mixed, gain, shift, cot, refs = *refs[:4], refs[4:]
    active, output, refs = refs[:chunks], refs[chunks], refs[chunks + 1 :]
    xhat, _ = normalized(mixed[...])
    combined = xhat * gain[0:1, :] + shift[0:1, :] + summed(parts)
    xhat, _ = normalized(combined)
    output[...] = (xhat * gain[1:2, :] + shift[1:2, :]).astype(LOW)
    leave(output)
    down_back(order, chunks, cot[...].astype(F32), combined, gain[1:2, :], active, refs)


def first_down_back(order, chunks, *refs):
    parts, refs = refs[: 2 * BACK], refs[2 * BACK :]
    grad_mixed, combined, gain, refs = *refs[:3], refs[3:]
    active, refs = refs[:chunks], refs[chunks:]
    grad = grad_mixed[...] + summed(parts)
    down_back(order, chunks, grad, combined[...], gain[1:2, :], active, refs)


def up_back(chunks, down_cot, *refs):
    upward, ups, downs, refs = refs[:chunks], refs[chunks : 2 * chunks], refs[2 * chunks : 3 * chunks], refs[3 * chunks :]
    grad_up, outs = refs[:chunks], refs[chunks:]
    low = down_cot[...]
    acc = None
    for index in range(chunks):
        back = dot_nt(low, downs[index][...])
        up = upward[index][...].astype(F32)
        slope = normal_cdf(up) + up * (jnp.exp(-0.5 * up * up) * 0.3989422804014327)
        gup = (back * slope).astype(LOW)
        grad_up[index][...] = gup
        piece = dot_nt(gup, ups[index][...])
        acc = piece if acc is None else acc + piece
    put_pieces(acc, outs)


def attention_back_body(levels, page_row, parts, grad_comb, mixed, gain, wo, q, k, v, lse, ctx, ext, boxes, pages, grad_mixed, out_cot, gq, gkt, gvt, dgain, dshift, dtable):
    seq, width = q.shape
    grad = grad_comb[...] + summed(parts)
    xhat, rstd = normalized(mixed[...])
    grad_in, dgain[...], dshift[...] = norm_back(grad, xhat, rstd, gain[0:1, :])
    grad_mixed[...] = grad_in
    low = grad_in.astype(LOW)
    out_cot[...] = low
    gctx = dot_nt(low, wo[...]).astype(LOW)
    rows, cols = token_marks(boxes, pages)
    mask = page_mask(cols[:, 2:3], rows[page_row : page_row + 1, :])
    halves = half_masks()
    lane = iota((seq, LANES), 1)
    if ext is not None:
        key_ext = key_marks(cols, levels)
        place = lane.astype(F32)
        back_ext = (
            (place == levels - cols[:, 0:1]) | (place == levels + HEAD_DIM - cols[:, 1:2])
        ).astype(F32).astype(LOW)
        line = iota((LANES, seq), 0).astype(F32)
        marks_t = ((line == rows[0:1, :]) | (line == rows[1:2, :] + HEAD_DIM)).astype(F32).astype(LOW)
        dtable[...] = jnp.zeros(dtable.shape, F32)
    for pair in range(width // LANES):
        at = slice(pair * LANES, (pair + 1) * LANES)
        queries, keys, values = q[:, at], k[:, at], v[:, at]
        gc = gctx[:, at]
        product = gc.astype(F32) * ctx[:, at].astype(F32)
        gc_t = jnp.transpose(gc)
        q_t = jnp.transpose(queries)
        keys_left = keys if ext is None else jnp.concatenate([keys, key_ext], axis=1)
        keys_right = keys if ext is None else jnp.concatenate([keys, back_ext], axis=1)
        parts = []
        for half in range(2):
            head = 2 * pair + half
            rows_at = slice(half * HEAD_DIM, (half + 1) * HEAD_DIM)
            left = queries * halves[half]
            if ext is not None:
                left = jnp.concatenate([left, ext[:, head * LANES : (head + 1) * LANES]], axis=1)
            scores = dot_nt(left, keys_left) + mask
            probs = jnp.exp(scores - lse[:, head : head + 1])
            delta = jnp.sum(
                jnp.where((lane < HEAD_DIM) == (half == 0), product, 0.0), -1, keepdims=True
            )
            grad_scores = probs * (dot_nt(gc * halves[half], values) - delta)
            score_cot = grad_scores.astype(LOW)
            out_at = slice(head * HEAD_DIM, (head + 1) * HEAD_DIM)
            gvt[out_at, :] = dot(gc_t[rows_at, :], probs.astype(LOW)).astype(LOW)
            gkt[out_at, :] = dot(q_t[rows_at, :], score_cot).astype(LOW)
            out = dot(score_cot, keys_right)
            parts.append(out[:, :LANES])
            if ext is not None:
                spread = out[:, LANES:]
                upper = spread.astype(LOW)
                lower = (spread - upper.astype(F32)).astype(LOW)
                block = dot(marks_t, upper) + dot(marks_t, lower)
                small = iota((40, LANES), 1)
                for dim in range(2):
                    piece = block[dim * HEAD_DIM : dim * HEAD_DIM + 40, :]
                    if dim:
                        piece = pltpu.roll(piece, HEAD_DIM, 1)
                    piece = jnp.where(small <= levels, piece, 0.0)
                    piece = pltpu.roll(piece, 0, 1, stride=1, stride_axis=0)
                    line = jnp.sum(piece, 0, keepdims=True)
                    over = pltpu.roll(line, LANES - 1, 1)
                    place = iota((1, LANES), 1)
                    line = jnp.where(place == 2 * levels - 1, line + over, line)
                    dtable[dim, head : head + 1, :] = line
        gq[:, at] = (jnp.where(lane < HEAD_DIM, parts[0], parts[1]) * SCALE).astype(LOW)


def next_attention_back(*refs):
    parts, refs = refs[: 2 * BACK], refs[2 * BACK :]
    grad_comb, mixed, gain, wo, q, k, v, lse, ctx, boxes, pages, *outs = refs
    attention_back_body(0, 3, parts, grad_comb, mixed, gain, wo, q, k, v, lse, ctx, None, boxes, pages, *outs, None)


def first_attention_back(levels, *refs):
    parts, refs = refs[: 2 * BACK], refs[2 * BACK :]
    ins, (wq, wk, wv), outs, pieces = refs[:12], refs[12:15], refs[15:-BACK], refs[-BACK:]
    attention_back_body(levels, 2, parts, *ins, *outs)
    input_back(*outs[2:5], wq, wk, wv, *pieces)


def input_back(gq, gkt, gvt, wq, wk, wv, *parts):
    put_pieces(
        dot_nt(gq[...], wq[...])
        + dot_nt(jnp.transpose(gkt[...]), wk[...])
        + dot_nt(jnp.transpose(gvt[...]), wv[...]),
        parts,
    )


def halving_order(bits):
    count = len(bits)
    flips = [
        sum(bit for place, bit in enumerate(bits) if block >> (count - 1 - place) & 1)
        for block in range(1 << count)
    ]
    return [lambda here, flip=flip: here ^ flip for flip in flips]


def arranged(order, source, held, moved):
    held[...] = jnp.transpose(source[...])
    if order == "plain":
        return held
    size = held.shape[0] // len(order)
    here = lax.axis_index("dp")
    for block, flip in enumerate(order):
        at = pl.multiple_of(flip(here) * size, size)
        moved[block * size : (block + 1) * size, :] = held[pl.ds(at, size), :]
    return moved


def multiply(order, groups, outs, scratch):
    column = 0
    for place, (source, rights) in enumerate(groups):
        left = arranged(order, source, scratch[2 * place], scratch[2 * place + 1])
        for right, flipped in rights:
            wide = right.shape[0] if flipped else right.shape[1]
            step = wide if flipped else min(512, wide)
            for start in range(0, wide, step):
                for index in reversed(range(len(outs))):
                    size = outs[index].shape[0]
                    rows = left[index * size : (index + 1) * size, :]
                    if flipped:
                        block = dot_nt(rows, right[start : start + step, :])
                    else:
                        block = dot(rows, right[:, start : start + step])
                    outs[index][:, column + start : column + start + step] = block.astype(LOW)
            column += wide


def put_vectors(order, lines, table, outs, column, turned, buckets):
    count, rest = len(lines), LANES - len(lines)
    rows = [line[...] for line in lines] + [jnp.zeros((rest, lines[0].shape[1]), F32)]
    turned[...] = jnp.transpose(jnp.concatenate(rows, axis=0))
    rows = [jnp.zeros((count, LANES), F32), table[0], table[1]]
    rows += [jnp.zeros((rest - 2 * table.shape[1], LANES), F32)]
    buckets[...] = jnp.transpose(jnp.concatenate(rows, axis=0))
    here = lax.axis_index("dp")
    size = turned.shape[0] // len(order)
    some = 2 * (LANES // 4) // len(order)
    per_out = len(order) // len(outs)
    for block, flip in enumerate(order):
        index = flip(here)
        part = turned[pl.ds(pl.multiple_of(index * size, size), size), :]
        first = part[:some] + buckets[pl.ds(pl.multiple_of(index * some, some), some), :]
        at = (block % per_out) * size
        outs[block // per_out][at : at + size, column : column + LANES] = jnp.concatenate(
            [first, part[some:]], axis=0
        ).astype(LOW)


def weight_products(order, plan, parts, lines, *refs):
    groups, position = [], 0
    for kinds in plan:
        stop = position + 1 + len(kinds)
        groups.append((refs[position], list(zip(refs[position + 1 : stop], kinds))))
        position = stop
    extras, refs = refs[position : position + lines], refs[position + lines :]
    outs, scratch = refs[:parts], refs[parts:]
    multiply(order, groups, outs, scratch)
    if lines:
        put_vectors(order, extras[:-1], extras[-1], outs, outs[0].shape[1] - LANES, *scratch[-2:])


def weight_gradients(order, groups, after=(), extras=()):
    plan, args, columns = [], [], LANES if extras else 0
    for left, rights in groups:
        plan.append([flipped for _, flipped in rights])
        args.append(left)
        for right, flipped in rights:
            args.append(right)
            columns += right.shape[0] if flipped else right.shape[1]
    seq, d_model = groups[0][0].shape
    parts = 1 if order == "plain" else 2
    scratch = [pltpu.VMEM((d_model, seq), LOW)] * (2 * len(groups))
    if extras:
        scratch += [pltpu.VMEM((d_model, LANES), F32), pltpu.VMEM((LANES, LANES), F32)]
    return call(
        functools.partial(weight_products, order, plan, parts, len(extras)),
        [((d_model // parts, columns), LOW)] * parts,
        *args, *extras, after=after, scratch=scratch,
    )


def merge_kernel(kept, got, keep, send):
    half = keep.shape[0]
    keep[...] = (kept[:half, :].astype(F32) + got[:half, :].astype(F32)).astype(LOW)
    leave(keep)
    send[...] = (kept[half:, :].astype(F32) + got[half:, :].astype(F32)).astype(LOW)


def merge(kept, got, after=(), last=False):
    half = ((kept.shape[0] // 2, kept.shape[1]), LOW)
    return call(merge_kernel, [(*half, SAVE) if last else half, half], kept, got, after=after)


def join_kernel(*refs):
    keep, send = refs[-2:]
    half, column = keep.shape[0], 0
    for kept, got in zip(refs[:-2:2], refs[1:-2:2]):
        at = slice(column, column + kept.shape[1])
        keep[:, at] = (kept[:half, :].astype(F32) + got[:half, :].astype(F32)).astype(LOW)
        send[:, at] = (kept[half:, :].astype(F32) + got[half:, :].astype(F32)).astype(LOW)
        column = at.stop


def join(*pairs, after=()):
    rows, columns = pairs[0][0].shape[0] // 2, sum(pair[0].shape[1] for pair in pairs)
    return call(join_kernel, [((rows, columns), LOW)] * 2, *[a for pair in pairs for a in pair], after=after)


def finish_kernel(plan, count, width, extra, *refs):
    token, ins = refs[-1], []
    token[...] = jnp.zeros(token.shape, F32)
    refs = list(refs)
    for targets, paired in plan:
        ins.append([refs.pop(0) for _ in range(2 if paired else 1)])
    read = lambda group, at: sum(ref[:, at].astype(F32) for ref in group)
    for group, (targets, _) in zip(ins, plan):
        for block, target in enumerate(targets):
            if target is None:
                continue
            out, layer = target
            refs[out][layer] = read(group, slice(block * width, (block + 1) * width))
    if extra is not None:
        size, columns = ins[extra][0].shape
        total = read(ins[extra], slice(columns - LANES, columns))
        total = jnp.concatenate([total, jnp.zeros((LANES - size, LANES), F32)], axis=0)
        refs[count][...] = jnp.transpose(total)


def finish(plan, groups, count, width, extra=None, after=()):
    size = groups[0][0].shape[0]
    outs = [((2, size, width), F32, SAVE)] * count
    if extra is not None:
        outs.append(((LANES, LANES), F32, FREE))
    plan = [(targets, len(group) > 1) for targets, group in zip(plan, groups)]
    results = call(
        functools.partial(finish_kernel, plan, count, width, extra), [*outs, TOKEN],
        *[Held(a) if isinstance(a, jax.Array) else a for group in groups for a in group], after=after,
    )
    return [out.array if isinstance(out, Held) else out for out in results]


def input_sum(*refs):
    *parts, grad, out, token = refs
    out[...] = grad[...] + summed(parts)
    token[...] = jnp.zeros(token.shape, F32)


def pack_kernel(*refs):
    table, out = refs[-2], refs[-1]
    lines = len(refs) - 2
    for place in range(lines):
        out[place : place + 1, :] = refs[place][...]
    rows = table.shape[1]
    rest = jnp.zeros((rows, out.shape[1] - LANES), F32)
    for dim in range(2):
        at = slice(lines + dim * rows, lines + (dim + 1) * rows)
        out[at, :] = jnp.concatenate([table[dim], rest], axis=1)


def other(block, axis):
    return lax.ppermute(block, axis, [(0, 1), (1, 0)])


def body(inputs, w_query, w_key, w_value, w_out, w_up, w_down, norm_gain, norm_shift, box_table, boxes, pages, cotangent):
    _, rows_here, seq, d_model = inputs.shape
    assert rows_here == 1
    width = w_query.shape[3]
    hidden_width = w_up.shape[3]
    heads = width // HEAD_DIM
    levels = box_table.shape[3] // 2
    n_dp = lax.axis_size("dp")
    me = lax.axis_index("dp")
    bits = [1 << place for place in range(n_dp.bit_length() - 1)]
    pairs = n_dp == 8 and d_model % (16 * n_dp) == 0
    far_bits = bits[1:] + bits[:1]
    near_first, far_first = [halving_order(b) if pairs else "plain" for b in (bits, far_bits)]

    cuts = [slice(at, at + 512) for at in range(0, hidden_width, 512)]
    chunks = len(cuts)

    def ff_weights(layer):
        return [Held(w_up, 0, layer, None, cut) for cut in cuts] + [Held(w_down, 0, layer, cut) for cut in cuts]

    def flip(block, bit):
        return lax.ppermute(block, "dp", [(i, i ^ bit) for i in range(n_dp)])

    def exchange(*parts):
        return [*parts, *(other(part, "mp") for part in parts)]

    wide = ((seq, d_model), F32)
    thin = ((seq, d_model), LOW)
    fore = [((seq // FORE, d_model), LOW)] * FORE
    back = [((seq // BACK, d_model), LOW)] * BACK
    proj = ((seq, width), LOW)
    turned = [((width, seq), LOW)] * 2
    ff = [((seq, 512), LOW)] * chunks
    stats = ((seq, LANES), F32)
    vec = ((1, d_model), F32)
    halves = [((d_model // 2, hidden_width), LOW)] * 2 if pairs else [((d_model, hidden_width), LOW)]
    flat = [pltpu.VMEM((d_model, seq), LOW)] * 2
    saved = lambda *shapes: [(*shape, SAVE) for shape in shapes]
    x = Held(inputs, 0, 0)
    box = Held(boxes, 0, None, 0)
    page = Held(pages, None, 0)
    table = Held(jnp.transpose(box_table[0], (1, 0, 2)))
    norms = [[Held(array, 0, layer) for array in (norm_gain, norm_shift)] for layer in range(2)]

    (mine,) = call(
        copy_weights, [((2, d_model, width), LOW)], Held(w_key, 0, 1), Held(w_value, 0, 1)
    )
    far_weights = other(mine, "stream")
    q0, k0, v0, lse0, ctx0, ext0, *rest = call(
        functools.partial(first_attention, levels),
        [*saved(proj, proj, proj, stats, proj, ((seq, heads * LANES), LOW)), *fore],
        x, Held(w_query, 0, 0), Held(w_key, 0, 0), Held(w_value, 0, 0), box, page, table, Held(w_out, 0, 0),
        after=[mine], fetch=[*ff_weights(0), x],
    )
    parts, ff_w, x_here = rest[:FORE], rest[FORE:-1], rest[-1]
    mixed_here, middle0, *rest = call(
        functools.partial(feed_forward, chunks),
        [(*wide, BOTH), *saved(thin, *ff, *ff), *fore],
        *exchange(*parts), x_here, *norms[0], *ff_w, fetch=[Held(w_query, 0, 1)],
    )
    upward0, active0, parts = rest[:chunks], rest[chunks : 2 * chunks], rest[2 * chunks : -2]
    mixed0, wq1 = rest[-2:]
    combined0, hidden1, rounded1, *shares = call(
        next_states, [*saved(wide), wide, thin, *fore[:2]],
        *exchange(*parts), mixed_here, *norms[0],
    )
    near = [other(share, "stream") for share in shares]
    q1, wo1 = call(next_queries, [proj], rounded1, wq1, fetch=[Held(w_out, 0, 1)])
    far = [other(share, "mp") for share in near]
    k1, v1, lse1, ctx1, *rest = call(
        functools.partial(next_attention, len(near)), [proj, proj, stats, proj, *fore],
        *near, *far, far_weights, q1, box, page, wo1, after=[q1], fetch=ff_weights(1),
    )
    parts, ff_w = rest[:FORE], rest[FORE:]
    mixed1, middle1, *rest = call(
        functools.partial(feed_forward, chunks), [wide, thin, *ff, *ff, *fore],
        *exchange(*parts), hidden1, *norms[1], *ff_w, fetch=[Held(cotangent, 0, 0)],
    )
    upward1, active1, parts, cot = rest[:chunks], rest[chunks : 2 * chunks], rest[2 * chunks : -1], rest[-1]

    output, grad_comb, down_cot, dgain11, dshift11, *down1 = call(
        functools.partial(last_down_back, near_first, chunks), [(*thin, SAVE), wide, thin, vec, vec, *halves],
        *exchange(*parts), mixed1, *norms[1], cot, *active1, scratch=flat,
    )
    if pairs:
        got_down1 = flip(down1[1], bits[0])
    rest = call(functools.partial(up_back, chunks), [*ff, *back], down_cot, *upward1, *ff_w, after=down1[-1:])
    grad_up, parts = rest[:chunks], rest[chunks:]
    up1 = weight_gradients(far_first, [(middle1, [(ref, False) for ref in grad_up])])
    if pairs:
        got_up1 = flip(up1[1], far_bits[0])
    grad_mixed, out_cot, gq, *rest = call(
        next_attention_back, [wide, thin, proj, *turned, vec, vec],
        *exchange(*parts), grad_comb, mixed1, norms[1][0], wo1, q1, k1, v1, lse1, ctx1, box, page, after=up1[-1:],
    )
    gkv, (dgain10, dshift10) = [other(ref, "stream") for ref in rest[:2]], rest[2:]
    qo1 = weight_gradients(near_first, [(rounded1, [(gq, False)]), (out_cot, [(ctx1, False)])])
    if pairs:
        got_qo1 = flip(qo1[1], bits[0])
    parts = call(
        input_back, back, gq, *gkv, Held(w_query, 0, 1), Held(w_key, 0, 1), Held(w_value, 0, 1), after=qo1[-1:]
    )
    kv1 = weight_gradients(near_first, [(rounded1, [(ref, True) for ref in gkv])], after=parts[:1])
    before = kv1[-1:]
    if pairs:
        got_kv1 = flip(kv1[1], bits[0])
        down1 = merge(down1[0], got_down1, after=[kv1[1], got_qo1])
        got_down1 = flip(down1[1], bits[1])
        before = [down1[1], got_up1]

    grad_comb, down_cot, dgain01, dshift01, *rest = call(
        functools.partial(first_down_back, near_first, chunks), [wide, thin, vec, vec, *halves],
        *exchange(*parts), grad_mixed, combined0, norms[0][0], *active0, scratch=flat, after=before, fetch=ff_weights(0),
    )
    down0, ff_w = rest[: len(halves)], rest[len(halves) :]
    before = down0[-1:]
    if pairs:
        got_down0 = flip(down0[1], bits[0])
        up1 = merge(up1[0], got_up1, after=[down0[1], got_down1, got_kv1])
        got_up1 = flip(up1[1], far_bits[1])
        at1 = join((qo1[0], got_qo1), (kv1[0], got_kv1), after=up1[1:])
        got_at1 = flip(at1[1], bits[1])
        before = at1[1:]
    rest = call(functools.partial(up_back, chunks), [*ff, *back], down_cot, *upward0, *ff_w, after=before)
    grad_up, parts = rest[:chunks], rest[chunks:]
    grad_mixed, out_cot, gq, *rest = call(
        functools.partial(first_attention_back, levels),
        [wide, thin, proj, *turned, vec, vec, ((2, 8, LANES), F32), *back],
        *exchange(*parts), grad_comb, mixed0, norms[0][0], Held(w_out, 0, 0),
        q0, k0, v0, lse0, ctx0, ext0, box, page, Held(w_query, 0, 0), Held(w_key, 0, 0), Held(w_value, 0, 0),
    )
    gkv, (dgain00, dshift00, dtable), parts = rest[:2], rest[2:5], rest[5:]
    vectors = [dgain00, dgain01, dgain10, dgain11, dshift00, dshift01, dshift10, dshift11]
    before = [dgain00]
    if pairs:
        at1 = merge(at1[0], got_at1, after=[dgain00, got_up1], last=True)
        got_at1 = flip(at1[1], bits[2])
        down1 = merge(down1[0], got_down1, after=at1[1:], last=True)
        got_down1 = flip(down1[1], bits[2])
        before = down1[1:]
    up0 = weight_gradients(near_first, [(middle0, [(ref, False) for ref in grad_up])], after=before)
    before = up0[-1:]
    if pairs:
        got_up0 = flip(up0[1], bits[0])
        down0 = merge(down0[0], got_down0, after=up0[1:])
        got_down0 = flip(down0[1], bits[1])
        before = down0[1:]
    kv0 = weight_gradients(
        near_first, [(x, [(ref, True) for ref in gkv])], after=before, extras=[*vectors, dtable] if pairs else ()
    )
    qo0 = weight_gradients(near_first, [(x, [(gq, False)]), (out_cot, [(ctx0, False)])], after=kv0[-1:])

    before = qo0[-1:]
    if pairs:
        got_kv0, got_qo0 = (flip(part[1], bits[0]) for part in (kv0, qo0))
        up0 = merge(up0[0], got_up0, after=[qo0[1], got_down0, got_at1, got_down1])
        got_up0 = flip(up0[1], bits[1])
        down0 = merge(down0[0], got_down0, after=up0[1:], last=True)
        got_down0 = flip(down0[1], bits[2])

        kv0 = merge(kv0[0], got_kv0, after=[down0[1], got_up0, got_down0])
        got_kv0 = flip(kv0[1], bits[1])
        up0 = merge(up0[0], got_up0, after=kv0[1:], last=True)
        got_up0 = flip(up0[1], bits[2])
        up1 = merge(up1[0], got_up1, after=up0[1:], last=True)
        got_up1 = flip(up1[1], far_bits[2])

        qo0 = merge(qo0[0], got_qo0, after=[up1[1], got_kv0])
        got_qo0 = flip(qo0[1], bits[1])
        kv0 = merge(kv0[0], got_kv0, after=qo0[1:], last=True)
        got_kv0 = flip(kv0[1], bits[2])

        qo0 = merge(qo0[0], got_qo0, after=[kv0[1], got_up0, got_up1], last=True)
        got_qo0 = flip(qo0[1], bits[2])
        before = qo0[1:]
        down0, up0, down1, up1, kv0, qo0, at1 = (
            (down0[0], got_down0), (up0[0], got_up0), (down1[0], got_down1), (up1[0], got_up1),
            (kv0[0], got_kv0), (qo0[0], got_qo0), (at1[0], got_at1),
        )
    grad_inputs, token = call(
        input_sum, [(*wide, SAVE), TOKEN], *exchange(*parts), grad_mixed, after=before,
    )
    if not pairs:
        (small,) = call(pack_kernel, [((24, d_model), F32)], *vectors, dtable)
        small = lax.psum(small, "dp")
        at1 = [jnp.concatenate([qo1[0], kv1[0]], axis=1)]
        down0, up0, down1, up1, kv0, qo0, at1 = (
            (lax.psum_scatter(g[0], "dp", scatter_dimension=0, tiled=True),)
            for g in (down0, up0, down1, up1, kv0, qo0, at1)
        )
    grad_down, grad_up, token = finish(
        [[(0, 0)], [(0, 1)], [(1, 0)], [(1, 1)]], [down0, down1, up0, up1], 2, hidden_width, after=before
    )
    grad_k, grad_v, *rest, token = finish(
        [[(0, 0), (1, 0)], [None, None, (0, 1), (1, 1)]], [kv0, at1], 2, width, 0 if pairs else None, after=[token]
    )
    grad_q, grad_o, _ = finish([[(0, 0), (1, 0)], [(0, 1), (1, 1), None, None]], [qo0, at1], 2, width, after=[token])
    cut = d_model // n_dp
    some = 2 * levels // n_dp
    if pairs:
        vectors, grad_table = rest[0][:8, :cut], rest[0][8:24, :some]
    else:
        vectors = lax.dynamic_slice_in_dim(small[:8], me * cut, cut, 1)
        grad_table = lax.dynamic_slice_in_dim(small[8:], me * some, some, 1)
    vectors = vectors.reshape(2, 2, 2, cut)
    grad_table = grad_table.reshape(1, 2, 8, some)[:, :, :heads]
    flipped = lambda block: jnp.transpose(block, (0, 2, 1))[None]
    return (
        output.array[None, None],
        grad_inputs.array[None, None],
        grad_q[None],
        grad_k[None],
        grad_v[None],
        flipped(grad_o),
        grad_up[None],
        flipped(grad_down),
        vectors[:1],
        vectors[1:],
        grad_table,
    )


def solution(mesh):
    in_specs = (
        P("stream", "dp", None, None),
        P("stream", None, None, "mp"),
        P("stream", None, None, "mp"),
        P("stream", None, None, "mp"),
        P("stream", None, "mp", None),
        P("stream", None, None, "mp"),
        P("stream", None, "mp", None),
        P("stream", None, None, None),
        P("stream", None, None, None),
        P("stream", None, "mp", None),
        P("stream", None, "dp", None),
        P(None, "dp", None),
        P("stream", "dp", None, None),
    )
    out_specs = (
        P("stream", "dp", None, None),
        P("stream", "dp", None, None),
        P("stream", None, "dp", "mp"),
        P("stream", None, "dp", "mp"),
        P("stream", None, "dp", "mp"),
        P("stream", None, "mp", "dp"),
        P("stream", None, "dp", "mp"),
        P("stream", None, "mp", "dp"),
        P("stream", None, None, "dp"),
        P("stream", None, None, "dp"),
        P("stream", None, "mp", "dp"),
    )
    return jax.shard_map(body, mesh=mesh, in_specs=in_specs, out_specs=out_specs, check_vma=False)
```

```python
import functools

import jax
import jax.numpy as jnp
from jax import lax
from jax.experimental import pallas as pl
from jax.experimental.pallas import tpu as pltpu
from jax.sharding import PartitionSpec as P

HEAD_DIM = 64
EPSILON = 1e-05
MASKED = -1e30
LOW = jnp.bfloat16
F32 = jnp.float32
LANES = 128
SCALE = HEAD_DIM ** (-0.5)


def dot(left, right):
    return lax.dot_general(left, right, (((1,), (0,)), ((), ())), preferred_element_type=F32)


def dot_nt(left, right):
    return lax.dot_general(left, right, (((1,), (1,)), ((), ())), preferred_element_type=F32)


def iota(shape, dim):
    return lax.broadcasted_iota(jnp.int32, shape, dim)


def normalized(values):
    center = values - jnp.mean(values, -1, keepdims=True)
    rstd = lax.rsqrt(jnp.mean(center * center, -1, keepdims=True) + EPSILON)
    return center * rstd, rstd


def norm_back(grad, xhat, rstd, gain):
    scaled = grad * gain
    grad_in = rstd * (
        scaled
        - jnp.mean(scaled, -1, keepdims=True)
        - xhat * jnp.mean(scaled * xhat, -1, keepdims=True)
    )
    return grad_in, jnp.sum(grad * xhat, 0, keepdims=True), jnp.sum(grad, 0, keepdims=True)


class Held:
    def __init__(self, array, *index):
        self.array, self.dtype = array, array.dtype
        self.index = tuple(slice(None) if i is None else i for i in index)
        plain = tuple(0 if callable(i) else i for i in self.index)
        self.shape = jax.eval_shape(lambda: jnp.zeros(array.shape, jnp.int8)[plain]).shape

    def part(self, ref):
        return ref.at[tuple(i() if callable(i) else i for i in self.index)] if self.index else ref


class Arriving:
    def __init__(self, source, target, semaphore):
        self.copy = pltpu.make_async_copy(source, target, semaphore)
        self.copy.start()
        self.target, self.waited = target, False
        self.shape, self.dtype = target.shape, target.dtype

    def arrive(self):
        if not self.waited:
            self.copy.wait()
        self.waited = True

    def __getitem__(self, at):
        self.arrive()
        return self.target[at]


class Leaving:
    def __init__(self, source, target, semaphore):
        self.copy = pltpu.make_async_copy(source, target, semaphore)
        self.source, self.left = source, False
        self.shape, self.dtype = source.shape, source.dtype

    def leave(self):
        if not self.left:
            self.copy.start()
        self.left = True

    def __getitem__(self, at):
        return self.source[at]

    def __setitem__(self, at, value):
        self.source[at] = value


def leave(*refs):
    for ref in refs:
        if isinstance(ref, Leaving):
            ref.leave()


SAVE = "save"
BOTH = "both"
FREE = "free"
FORE = 4
BACK = 2
TOKEN = ((8, LANES), F32)


def call(kernel, outs, *args, after=(), fetch=(), scratch=(), vmem=24, time=0.0):
    arrays, specs, held = [], [], []
    for place, arg in enumerate(args):
        if isinstance(arg, Held):
            specs.append(pl.BlockSpec(memory_space=pltpu.HBM))
            arrays.append(pltpu.with_memory_space_constraint(arg.array, pltpu.HBM))
            held.append((place, arg))
        else:
            specs.append(pl.BlockSpec(memory_space=pltpu.VMEM))
            arrays.append(pltpu.with_memory_space_constraint(arg, pltpu.VMEM))
    arrays += list(after)
    specs += [pl.BlockSpec(memory_space=pl.ANY)] * len(after)
    for arg in fetch:
        specs.append(pl.BlockSpec(memory_space=pltpu.HBM))
        arrays.append(pltpu.with_memory_space_constraint(arg.array, pltpu.HBM))
    kinds = [out[2] if len(out) > 2 else None for out in outs]
    saved = [place for place, kind in enumerate(kinds) if kind == SAVE]
    both = [place for place, kind in enumerate(kinds) if kind == BOTH]
    out_shape, out_specs = [], []
    for out, kind in zip(outs, kinds):
        make = {None: pltpu.VMEM, BOTH: pltpu.VMEM, SAVE: pltpu.HBM, FREE: jax.ShapeDtypeStruct}[kind]
        out_shape.append(make(out[0], out[1]))
        out_specs.append(pl.BlockSpec(memory_space=pltpu.HBM if kind == SAVE else pltpu.VMEM))
    for place in both:
        out_shape.append(pltpu.HBM(*outs[place][:2]))
        out_specs.append(pl.BlockSpec(memory_space=pltpu.HBM))
    for arg in fetch:
        out_shape.append(pltpu.VMEM(arg.shape, arg.dtype))
        out_specs.append(pl.BlockSpec(memory_space=pltpu.VMEM))
    count, waits, fetched, n_outs, n_own = len(args), len(after), len(fetch), len(outs), len(scratch)
    buffers = [pltpu.VMEM(arg.shape, arg.dtype) for _, arg in held]
    buffers += [pltpu.VMEM(*outs[place][:2]) for place in saved]
    moves = len(buffers) + len(both) + fetched

    def run(*refs):
        refs = list(refs)
        take = lambda size: [refs.pop(0) for _ in range(size)]
        ins, _, sources, results = take(count), take(waits), take(fetched), take(n_outs)
        copies, fetches, own, targets = take(len(both)), take(fetched), take(n_own), take(len(buffers))
        semaphores = [refs[0].at[order] for order in range(moves)] if moves else []
        for place, arg in held:
            ins[place] = Arriving(arg.part(ins[place]), targets.pop(0), semaphores.pop(0))
        for place in saved:
            results[place] = Leaving(targets.pop(0), results[place], semaphores.pop(0))
        for place in both:
            results[place] = Leaving(results[place], copies.pop(0), semaphores.pop(0))
        coming = [Arriving(arg.part(ref), out, semaphores.pop(0)) for arg, ref, out in zip(fetch, sources, fetches)]
        kernel(*ins, *results, *own)
        for place, _ in held:
            ins[place].arrive()
        for ref in coming:
            ref.arrive()
        for place in saved + both:
            results[place].leave()
        for place in saved + both:
            results[place].copy.wait()

    results = pl.pallas_call(
        run,
        out_shape=out_shape,
        in_specs=specs,
        out_specs=out_specs,
        scratch_shapes=list(scratch) + buffers + ([pltpu.SemaphoreType.DMA((moves,))] if moves else []),
        compiler_params=pltpu.CompilerParams(vmem_limit_bytes=vmem * 1024 * 1024),
        cost_estimate=pl.CostEstimate(flops=int(1e5 + time * 1e9), bytes_accessed=1, transcendentals=0),
    )(*arrays)
    wrapped = [Held(r) if place in saved else r for place, r in enumerate(results[:n_outs])]
    wrapped += [Held(r) for r in results[n_outs : n_outs + len(both)]]
    return wrapped + list(results[n_outs + len(both) :])


def token_marks(boxes, pages):
    first = lax.axis_index("stream") == 0
    own = jnp.where(first, pages[0:1, :], pages[1:2, :])
    far = jnp.where(first, pages[1:2, :], pages[0:1, :])
    rows = jnp.concatenate([boxes[...], own, far, boxes[...], own, far], axis=0).astype(F32)
    return rows, jnp.transpose(rows)


def page_mask(cols, rows):
    return jnp.where(cols == rows, 0.0, MASKED).astype(F32)


def key_marks(cols, levels):
    lane = iota((cols.shape[0], LANES), 1)
    want = (levels - lane % levels).astype(F32)
    picked = jnp.where((lane // levels) % 2 == 0, cols[:, 0:1], cols[:, 1:2])
    return (picked == want).astype(F32).astype(LOW)


def query_marks(cols, levels):
    lane = iota((cols.shape[0], LANES), 1).astype(F32)
    hit = (lane == levels - cols[:, 0:1]) | (lane == levels + 40 - cols[:, 1:2])
    return hit.astype(F32).astype(LOW)


def bias_rows(table, head, levels):
    lane = iota((40, LANES), 1)
    blocks = []
    for dim in range(2):
        line = table[head][dim : dim + 1, :]
        line = jnp.concatenate(
            [line, jnp.broadcast_to(line[:, -1:], (1, LANES - line.shape[1]))], axis=1
        )
        base = jnp.broadcast_to(pltpu.roll(line, LANES - levels, 1), (40, LANES))
        spread = pltpu.roll(base, 0, 1, stride=1, stride_axis=0)
        spread = jnp.where(lane < levels, spread - spread[:, levels : levels + 1], 0.0)
        upper = spread.astype(LOW).astype(F32)
        lower = spread - upper
        blocks.append(
            pltpu.roll(upper, dim * levels, 1) + pltpu.roll(lower, (2 + dim) * levels, 1)
            if dim
            else upper + pltpu.roll(lower, 2 * levels, 1)
        )
    blocks.append(jnp.zeros((LANES - 80, LANES), F32))
    return jnp.concatenate(blocks, axis=0).astype(LOW)


def half_masks():
    lane = iota((1, LANES), 1)
    first = (lane < HEAD_DIM).astype(F32).astype(LOW)
    return first, (1 - first.astype(F32)).astype(LOW)


def attend(q_ref, k_ref, v_ref, ext_ref, key_ext, mask, lse_ref, ctx_ref):
    seq, width = q_ref.shape
    halves = half_masks()
    lane = iota((seq, LANES), 1)
    ones = jnp.ones((seq, LANES), LOW)
    lse = jnp.zeros((seq, LANES), F32)
    for pair in range(width // LANES):
        at = slice(pair * LANES, (pair + 1) * LANES)
        queries, keys = q_ref[:, at], k_ref[:, at]
        if key_ext is not None:
            keys = jnp.concatenate([keys, key_ext], axis=1)
        values = jnp.concatenate([v_ref[:, at], ones], axis=1)
        parts = []
        for half in range(2):
            head = 2 * pair + half
            left = queries * halves[half]
            if key_ext is not None:
                left = jnp.concatenate([left, ext_ref[:, head * LANES : (head + 1) * LANES]], axis=1)
            scores = dot_nt(left, keys) + mask
            top = jnp.max(scores, -1, keepdims=True)
            weights = jnp.exp(scores - top).astype(LOW)
            out = dot(weights, values)
            total = out[:, LANES:]
            parts.append(out[:, :LANES] / total)
            lse = jnp.where(lane == head, top + jnp.log(total), lse)
        ctx_ref[:, at] = jnp.where(lane < HEAD_DIM, parts[0], parts[1]).astype(LOW)
    lse_ref[...] = lse
    leave(lse_ref, ctx_ref)


def put_pieces(value, refs):
    size = refs[0].shape[0]
    for place, ref in enumerate(refs):
        ref[...] = value[place * size : (place + 1) * size].astype(LOW)


def summed(parts):
    count = len(parts) // 2
    return jnp.concatenate(
        [own[...].astype(F32) + far[...].astype(F32) for own, far in zip(parts[:count], parts[count:])], axis=0
    )


def first_attention(levels, x, wq, wk, wv, boxes, pages, table, wo, q, k, v, lse, ctx, ext, *parts):
    states = x[...]
    q[...] = (dot(states, wq[...]).astype(LOW).astype(F32) * SCALE).astype(LOW)
    k[...] = dot(states, wk[...]).astype(LOW)
    v[...] = dot(states, wv[...]).astype(LOW)
    leave(q, k, v)
    rows, cols = token_marks(boxes, pages)
    marks = query_marks(cols, levels)
    tables = [table[head] for head in range(table.shape[0])]
    for head in range(q.shape[1] // HEAD_DIM):
        ext[:, head * LANES : (head + 1) * LANES] = dot(
            marks, bias_rows(tables, head, levels)
        ).astype(LOW)
    leave(ext)
    mask = page_mask(cols[:, 2:3], rows[2:3, :])
    attend(q, k, v, ext, key_marks(cols, levels), mask, lse, ctx)
    put_pieces(dot(ctx[...], wo[...]), parts)


def next_states(*refs):
    parts, refs = refs[: 2 * FORE], refs[2 * FORE :]
    mixed, gain, shift, combined, hidden, rounded, *shares = refs
    xhat, _ = normalized(mixed[...])
    total = xhat * gain[0:1, :] + shift[0:1, :] + summed(parts)
    combined[...] = total
    leave(combined)
    xhat, _ = normalized(total)
    state = xhat * gain[1:2, :] + shift[1:2, :]
    hidden[...] = state
    rounded[...] = state.astype(LOW)
    size = shares[0].shape[0]
    first = lax.axis_index("mp") * (size * len(shares))
    for place, share in enumerate(shares):
        share[...] = rounded[pl.ds(pl.multiple_of(first + place * size, size), size), :]


def next_queries(rounded, wq, q):
    q[...] = (dot(rounded[...], wq[...]).astype(LOW).astype(F32) * SCALE).astype(LOW)


def copy_weights(wk, wv, out):
    out[0] = wk[...]
    out[1] = wv[...]


def next_attention(count, *refs):
    near, far, refs = refs[:count], refs[count : 2 * count], refs[2 * count :]
    weights, q, boxes, pages, wo, k, v, lse, ctx, *parts = refs
    size = near[0].shape[0]
    here = lax.axis_index("mp") * (size * count)
    there = size * count - here
    for start, pieces in ((here, near), (there, far)):
        for place, states in enumerate(pieces):
            at = pl.ds(pl.multiple_of(start + place * size, size), size)
            k[at, :] = dot(states[...], weights[0]).astype(LOW)
            v[at, :] = dot(states[...], weights[1]).astype(LOW)
    rows, cols = token_marks(boxes, pages)
    mask = page_mask(cols[:, 2:3], rows[3:4, :])
    attend(q, k, v, None, None, mask, lse, ctx)
    put_pieces(dot(ctx[...], wo[...]), parts)


def normal_cdf(values):
    return 0.5 * (1.0 + lax.erf(values * (0.5**0.5)))


def feed_forward(chunks, *refs):
    parts, refs = refs[: 2 * FORE], refs[2 * FORE :]
    hidden, gain, shift, refs = refs[0], refs[1], refs[2], refs[3:]
    ups, downs, refs = refs[:chunks], refs[chunks : 2 * chunks], refs[2 * chunks :]
    mixed, middle, refs = refs[0], refs[1], refs[2:]
    upward, active, outs = refs[:chunks], refs[chunks : 2 * chunks], refs[2 * chunks :]
    total = hidden[...].astype(F32) + summed(parts)
    mixed[...] = total
    xhat, _ = normalized(total)
    low = (xhat * gain[0:1, :] + shift[0:1, :]).astype(LOW)
    middle[...] = low
    leave(mixed, middle)
    acc = None
    for index in range(chunks):
        up = dot(low, ups[index][...])
        upward[index][...] = up.astype(LOW)
        act = (up * normal_cdf(up)).astype(LOW)
        active[index][...] = act
        leave(upward[index], active[index])
        piece = dot(act, downs[index][...])
        acc = piece if acc is None else acc + piece
    put_pieces(acc, outs)


def down_back(order, chunks, grad, combined, gain, active, refs):
    grad_comb, down_cot, dgain, dshift, *outs, held, moved = refs
    xhat, rstd = normalized(combined)
    grad_in, dgain[...], dshift[...] = norm_back(grad, xhat, rstd, gain)
    grad_comb[...] = grad_in
    down_cot[...] = grad_in.astype(LOW)
    multiply(order, [(down_cot, [(ref, False) for ref in active])], outs, [held, moved])


def last_down_back(order, chunks, *refs):
    parts, refs = refs[: 2 * FORE], refs[2 * FORE :]
    mixed, gain, shift, cot, refs = *refs[:4], refs[4:]
    active, output, refs = refs[:chunks], refs[chunks], refs[chunks + 1 :]
    xhat, _ = normalized(mixed[...])
    combined = xhat * gain[0:1, :] + shift[0:1, :] + summed(parts)
    xhat, _ = normalized(combined)
    output[...] = (xhat * gain[1:2, :] + shift[1:2, :]).astype(LOW)
    leave(output)
    down_back(order, chunks, cot[...].astype(F32), combined, gain[1:2, :], active, refs)


def first_down_back(order, chunks, *refs):
    parts, refs = refs[: 2 * BACK], refs[2 * BACK :]
    grad_mixed, combined, gain, refs = *refs[:3], refs[3:]
    active, refs = refs[:chunks], refs[chunks:]
    grad = grad_mixed[...] + summed(parts)
    down_back(order, chunks, grad, combined[...], gain[1:2, :], active, refs)


def up_back(chunks, down_cot, *refs):
    upward, ups, downs, refs = refs[:chunks], refs[chunks : 2 * chunks], refs[2 * chunks : 3 * chunks], refs[3 * chunks :]
    grad_up, outs = refs[:chunks], refs[chunks:]
    low = down_cot[...]
    acc = None
    for index in range(chunks):
        back = dot_nt(low, downs[index][...])
        up = upward[index][...].astype(F32)
        slope = normal_cdf(up) + up * (jnp.exp(-0.5 * up * up) * 0.3989422804014327)
        gup = (back * slope).astype(LOW)
        grad_up[index][...] = gup
        piece = dot_nt(gup, ups[index][...])
        acc = piece if acc is None else acc + piece
    put_pieces(acc, outs)


def mixed_back(parts, grad_comb, mixed, gain, wo, grad_mixed, out_cot, dgain, dshift):
    grad = grad_comb[...] + summed(parts)
    xhat, rstd = normalized(mixed[...])
    grad_in, dgain[...], dshift[...] = norm_back(grad, xhat, rstd, gain[0:1, :])
    grad_mixed[...] = grad_in
    low = grad_in.astype(LOW)
    out_cot[...] = low
    return dot_nt(low, wo[...]).astype(LOW)


def heads_back(levels, page_row, pairs, gctx, q, k, v, lse, ctx, ext, boxes, pages, gq, gkt, gvt, dtable):
    seq = q.shape[0]
    rows, cols = token_marks(boxes, pages)
    mask = page_mask(cols[:, 2:3], rows[page_row : page_row + 1, :])
    halves = half_masks()
    lane = iota((seq, LANES), 1)
    if ext is not None:
        key_ext = key_marks(cols, levels)
        place = lane.astype(F32)
        back_ext = (
            (place == levels - cols[:, 0:1]) | (place == levels + HEAD_DIM - cols[:, 1:2])
        ).astype(F32).astype(LOW)
        line = iota((LANES, seq), 0).astype(F32)
        marks_t = ((line == rows[0:1, :]) | (line == rows[1:2, :] + HEAD_DIM)).astype(F32).astype(LOW)
        dtable[...] = jnp.zeros(dtable.shape, F32)
    for slot, pair in enumerate(pairs):
        at = slice(pair * LANES, (pair + 1) * LANES)
        queries, keys, values = q[:, at], k[:, at], v[:, at]
        gc = gctx[:, at]
        product = gc.astype(F32) * ctx[:, at].astype(F32)
        gc_t = jnp.transpose(gc)
        q_t = jnp.transpose(queries)
        keys_left = keys if ext is None else jnp.concatenate([keys, key_ext], axis=1)
        keys_right = keys if ext is None else jnp.concatenate([keys, back_ext], axis=1)
        parts = []
        for half in range(2):
            head = 2 * pair + half
            rows_at = slice(half * HEAD_DIM, (half + 1) * HEAD_DIM)
            out_at = slice(slot * LANES + half * HEAD_DIM, slot * LANES + (half + 1) * HEAD_DIM)
            left = queries * halves[half]
            if ext is not None:
                left = jnp.concatenate([left, ext[:, head * LANES : (head + 1) * LANES]], axis=1)
            scores = dot_nt(left, keys_left) + mask
            probs = jnp.exp(scores - lse[:, head : head + 1])
            delta = jnp.sum(
                jnp.where((lane < HEAD_DIM) == (half == 0), product, 0.0), -1, keepdims=True
            )
            grad_scores = probs * (dot_nt(gc * halves[half], values) - delta)
            score_cot = grad_scores.astype(LOW)
            gvt[out_at, :] = dot(gc_t[rows_at, :], probs.astype(LOW)).astype(LOW)
            gkt[out_at, :] = dot(q_t[rows_at, :], score_cot).astype(LOW)
            out = dot(score_cot, keys_right)
            parts.append(out[:, :LANES])
            if ext is not None:
                spread = out[:, LANES:]
                upper = spread.astype(LOW)
                lower = (spread - upper.astype(F32)).astype(LOW)
                block = dot(marks_t, upper) + dot(marks_t, lower)
                small = iota((40, LANES), 1)
                for dim in range(2):
                    piece = block[dim * HEAD_DIM : dim * HEAD_DIM + 40, :]
                    if dim:
                        piece = pltpu.roll(piece, HEAD_DIM, 1)
                    piece = jnp.where(small <= levels, piece, 0.0)
                    piece = pltpu.roll(piece, 0, 1, stride=1, stride_axis=0)
                    line = jnp.sum(piece, 0, keepdims=True)
                    over = pltpu.roll(line, LANES - 1, 1)
                    column = iota((1, LANES), 1)
                    line = jnp.where(column == 2 * levels - 1, line + over, line)
                    dtable[dim, head : head + 1, :] = line
        gq[:, slot * LANES : (slot + 1) * LANES] = (jnp.where(lane < HEAD_DIM, parts[0], parts[1]) * SCALE).astype(LOW)


def next_attention_back(*refs):
    parts, refs = refs[: 2 * BACK], refs[2 * BACK :]
    grad_comb, mixed, gain, wo, q, k, v, lse, ctx, boxes, pages, *outs = refs
    grad_mixed, out_cot, gq, gkt, gvt, dgain, dshift = outs
    gctx = mixed_back(parts, grad_comb, mixed, gain, wo, grad_mixed, out_cot, dgain, dshift)
    heads_back(0, 3, range(q.shape[1] // LANES), gctx, q, k, v, lse, ctx, None, boxes, pages, gq, gkt, gvt, None)


def first_attention_back(levels, *refs):
    parts, refs = refs[: 2 * BACK], refs[2 * BACK :]
    grad_comb, mixed, gain, wo, q, k, v, lse, ctx, ext, boxes, pages, wq, wk, wv, *outs = refs
    grad_mixed, out_cot, dgain, dshift, gq, gkt, gvt, dtable, part = outs
    gctx = mixed_back(parts, grad_comb, mixed, gain, wo, grad_mixed, out_cot, dgain, dshift)
    heads_back(levels, 2, range(q.shape[1] // LANES), gctx, q, k, v, lse, ctx, ext, boxes, pages, gq, gkt, gvt, dtable)
    input_back(gq, gkt, gvt, wq, wk, wv, part)


def input_back(gq, gkt, gvt, wq, wk, wv, *parts):
    put_pieces(
        dot_nt(gq[...], wq[...])
        + dot_nt(jnp.transpose(gkt[...]), wk[...])
        + dot_nt(jnp.transpose(gvt[...]), wv[...]),
        parts,
    )


def halving_order(bits):
    count = len(bits)
    flips = [
        sum(bit for place, bit in enumerate(bits) if block >> (count - 1 - place) & 1)
        for block in range(1 << count)
    ]
    return [lambda here, flip=flip: here ^ flip for flip in flips]


def arranged(order, source, held, moved):
    held[...] = jnp.transpose(source[...])
    if order == "plain":
        return held
    size = held.shape[0] // len(order)
    here = lax.axis_index("dp")
    for block, flip in enumerate(order):
        at = pl.multiple_of(flip(here) * size, size)
        moved[block * size : (block + 1) * size, :] = held[pl.ds(at, size), :]
    return moved


def multiply(order, groups, outs, scratch):
    column = 0
    for place, (source, rights) in enumerate(groups):
        left = arranged(order, source, scratch[2 * place], scratch[2 * place + 1])
        for right, flipped in rights:
            wide = right.shape[0] if flipped else right.shape[1]
            step = wide if flipped else min(512, wide)
            for start in range(0, wide, step):
                for index in reversed(range(len(outs))):
                    size = outs[index].shape[0]
                    rows = left[index * size : (index + 1) * size, :]
                    if flipped:
                        block = dot_nt(rows, right[start : start + step, :])
                    else:
                        block = dot(rows, right[:, start : start + step])
                    outs[index][:, column + start : column + start + step] = block.astype(LOW)
            column += wide


def put_vectors(order, lines, table, outs, column, turned, buckets):
    count, rest = len(lines), LANES - len(lines)
    rows = [line[...] for line in lines] + [jnp.zeros((rest, lines[0].shape[1]), F32)]
    turned[...] = jnp.transpose(jnp.concatenate(rows, axis=0))
    rows = [jnp.zeros((count, LANES), F32), table[0], table[1]]
    rows += [jnp.zeros((rest - 2 * table.shape[1], LANES), F32)]
    buckets[...] = jnp.transpose(jnp.concatenate(rows, axis=0))
    here = lax.axis_index("dp")
    size = turned.shape[0] // len(order)
    some = 2 * (LANES // 4) // len(order)
    per_out = len(order) // len(outs)
    for block, flip in enumerate(order):
        index = flip(here)
        part = turned[pl.ds(pl.multiple_of(index * size, size), size), :]
        first = part[:some] + buckets[pl.ds(pl.multiple_of(index * some, some), some), :]
        at = (block % per_out) * size
        outs[block // per_out][at : at + size, column : column + LANES] = jnp.concatenate(
            [first, part[some:]], axis=0
        ).astype(LOW)


def weight_products(order, plan, parts, lines, *refs):
    groups, position = [], 0
    for kinds in plan:
        stop = position + 1 + len(kinds)
        groups.append((refs[position], list(zip(refs[position + 1 : stop], kinds))))
        position = stop
    extras, refs = refs[position : position + lines], refs[position + lines :]
    outs, scratch = refs[:parts], refs[parts:]
    multiply(order, groups, outs, scratch)
    if lines:
        put_vectors(order, extras[:-1], extras[-1], outs, outs[0].shape[1] - LANES, *scratch[-2:])


def weight_gradients(order, groups, after=(), extras=()):
    plan, args, columns = [], [], LANES if extras else 0
    for left, rights in groups:
        plan.append([flipped for _, flipped in rights])
        args.append(left)
        for right, flipped in rights:
            args.append(right)
            columns += right.shape[0] if flipped else right.shape[1]
    seq, d_model = groups[0][0].shape
    parts = 1 if order == "plain" else 2
    scratch = [pltpu.VMEM((d_model, seq), LOW)] * (2 * len(groups))
    if extras:
        scratch += [pltpu.VMEM((d_model, LANES), F32), pltpu.VMEM((LANES, LANES), F32)]
    return call(
        functools.partial(weight_products, order, plan, parts, len(extras)),
        [((d_model // parts, columns), LOW)] * parts,
        *args, *extras, after=after, scratch=scratch,
    )


def merge_kernel(kept, got, keep, send):
    half = keep.shape[0]
    keep[...] = (kept[:half, :].astype(F32) + got[:half, :].astype(F32)).astype(LOW)
    leave(keep)
    send[...] = (kept[half:, :].astype(F32) + got[half:, :].astype(F32)).astype(LOW)


def merge(kept, got, after=(), last=False):
    half = ((kept.shape[0] // 2, kept.shape[1]), LOW)
    return call(merge_kernel, [(*half, SAVE) if last else half, half], kept, got, after=after)


def join_kernel(*refs):
    keep, send = refs[-2:]
    half, column = keep.shape[0], 0
    for kept, got in zip(refs[:-2:2], refs[1:-2:2]):
        at = slice(column, column + kept.shape[1])
        keep[:, at] = (kept[:half, :].astype(F32) + got[:half, :].astype(F32)).astype(LOW)
        send[:, at] = (kept[half:, :].astype(F32) + got[half:, :].astype(F32)).astype(LOW)
        column = at.stop


def join(*pairs, after=()):
    rows, columns = pairs[0][0].shape[0] // 2, sum(pair[0].shape[1] for pair in pairs)
    return call(join_kernel, [((rows, columns), LOW)] * 2, *[a for pair in pairs for a in pair], after=after)


def finish_kernel(plan, count, width, extra, *refs):
    token, ins = refs[-1], []
    token[...] = jnp.zeros(token.shape, F32)
    refs = list(refs)
    for targets, paired in plan:
        ins.append([refs.pop(0) for _ in range(2 if paired else 1)])
    read = lambda group, at: sum(ref[:, at].astype(F32) for ref in group)
    for group, (targets, _) in zip(ins, plan):
        for block, target in enumerate(targets):
            if target is None:
                continue
            out, layer = target
            refs[out][layer] = read(group, slice(block * width, (block + 1) * width))
    if extra is not None:
        size, columns = ins[extra][0].shape
        total = read(ins[extra], slice(columns - LANES, columns))
        total = jnp.concatenate([total, jnp.zeros((LANES - size, LANES), F32)], axis=0)
        refs[count][...] = jnp.transpose(total)


def finish(plan, groups, count, width, extra=None, after=(), fresh=False):
    size = groups[0][0].shape[0]
    outs = [((2, size, width), F32, SAVE)] * count
    if extra is not None:
        outs.append(((LANES, LANES), F32, FREE))
    plan = [(targets, len(group) > 1) for targets, group in zip(plan, groups)]
    results = call(
        functools.partial(finish_kernel, plan, count, width, extra), [*outs, TOKEN],
        *[Held(a) if isinstance(a, jax.Array) and not (fresh and place == 0) else a for place, group in enumerate(groups) for a in group],
        after=after,
    )
    return [out.array if isinstance(out, Held) else out for out in results]


def input_sum(*refs):
    *parts, grad, out, token = refs
    out[...] = grad[...] + summed(parts)
    token[...] = jnp.zeros(token.shape, F32)


def pack_kernel(*refs):
    table, out = refs[-2], refs[-1]
    lines = len(refs) - 2
    for place in range(lines):
        out[place : place + 1, :] = refs[place][...]
    rows = table.shape[1]
    rest = jnp.zeros((rows, out.shape[1] - LANES), F32)
    for dim in range(2):
        at = slice(lines + dim * rows, lines + (dim + 1) * rows)
        out[at, :] = jnp.concatenate([table[dim], rest], axis=1)


def other(block, axis):
    return lax.ppermute(block, axis, [(0, 1), (1, 0)])


def body(inputs, w_query, w_key, w_value, w_out, w_up, w_down, norm_gain, norm_shift, box_table, boxes, pages, cotangent):
    _, rows_here, seq, d_model = inputs.shape
    assert rows_here == 1
    width = w_query.shape[3]
    hidden_width = w_up.shape[3]
    heads = width // HEAD_DIM
    levels = box_table.shape[3] // 2
    n_dp = lax.axis_size("dp")
    me = lax.axis_index("dp")
    bits = [1 << place for place in range(n_dp.bit_length() - 1)]
    pairs = n_dp == 8 and d_model % (16 * n_dp) == 0
    far_bits = bits[1:] + bits[:1]
    near_first, far_first = [halving_order(b) if pairs else "plain" for b in (bits, far_bits)]

    cuts = [slice(at, at + 512) for at in range(0, hidden_width, 512)]
    chunks = len(cuts)

    def ff_weights(layer):
        return [Held(w_up, 0, layer, None, cut) for cut in cuts] + [Held(w_down, 0, layer, cut) for cut in cuts]

    def flip(block, bit):
        return lax.ppermute(block, "dp", [(i, i ^ bit) for i in range(n_dp)])

    def exchange(*parts):
        return [*parts, *(other(part, "mp") for part in parts)]

    wide = ((seq, d_model), F32)
    thin = ((seq, d_model), LOW)
    fore = [((seq // FORE, d_model), LOW)] * FORE
    back = [((seq // BACK, d_model), LOW)] * BACK
    proj = ((seq, width), LOW)
    turned = [((width, seq), LOW)] * 2
    ff = [((seq, 512), LOW)] * chunks
    stats = ((seq, LANES), F32)
    vec = ((1, d_model), F32)
    halves = [((d_model // 2, hidden_width), LOW)] * 2 if pairs else [((d_model, hidden_width), LOW)]
    flat = [pltpu.VMEM((d_model, seq), LOW)] * 2
    saved = lambda *shapes: [(*shape, SAVE) for shape in shapes]
    x = Held(inputs, 0, 0)
    box = Held(boxes, 0, None, 0)
    page = Held(pages, None, 0)
    table = Held(jnp.transpose(box_table[0], (1, 0, 2)))
    norms = [[Held(array, 0, layer) for array in (norm_gain, norm_shift)] for layer in range(2)]

    (mine,) = call(
        copy_weights, [((2, d_model, width), LOW)], Held(w_key, 0, 1), Held(w_value, 0, 1)
    )
    far_weights = other(mine, "stream")
    q0, k0, v0, lse0, ctx0, ext0, *rest = call(
        functools.partial(first_attention, levels),
        [*saved(proj, proj, proj, stats, proj, ((seq, heads * LANES), LOW)), *fore],
        x, Held(w_query, 0, 0), Held(w_key, 0, 0), Held(w_value, 0, 0), box, page, table, Held(w_out, 0, 0),
        after=[mine], fetch=[*ff_weights(0), x],
    )
    parts, ff_w, x_here = rest[:FORE], rest[FORE:-1], rest[-1]
    mixed_here, middle0, *rest = call(
        functools.partial(feed_forward, chunks),
        [(*wide, BOTH), *saved(thin, *ff, *ff), *fore],
        *exchange(*parts), x_here, *norms[0], *ff_w, fetch=[Held(w_query, 0, 1)],
    )
    upward0, active0, parts = rest[:chunks], rest[chunks : 2 * chunks], rest[2 * chunks : -2]
    mixed0, wq1 = rest[-2:]
    combined0, hidden1, rounded1, *shares = call(
        next_states, [*saved(wide), wide, thin, *fore[:2]],
        *exchange(*parts), mixed_here, *norms[0],
    )
    near = [other(share, "stream") for share in shares]
    q1, wo1 = call(next_queries, [proj], rounded1, wq1, fetch=[Held(w_out, 0, 1)])
    far = [other(share, "mp") for share in near]
    k1, v1, lse1, ctx1, *rest = call(
        functools.partial(next_attention, len(near)), [proj, proj, stats, proj, *fore],
        *near, *far, far_weights, q1, box, page, wo1, after=[q1], fetch=ff_weights(1),
    )
    parts, ff_w = rest[:FORE], rest[FORE:]
    mixed1, middle1, *rest = call(
        functools.partial(feed_forward, chunks), [wide, thin, *ff, *ff, *fore],
        *exchange(*parts), hidden1, *norms[1], *ff_w, fetch=[Held(cotangent, 0, 0)],
    )
    upward1, active1, parts, cot = rest[:chunks], rest[chunks : 2 * chunks], rest[2 * chunks : -1], rest[-1]

    output, grad_comb, down_cot, dgain11, dshift11, *down1 = call(
        functools.partial(last_down_back, near_first, chunks), [(*thin, SAVE), wide, thin, vec, vec, *halves],
        *exchange(*parts), mixed1, *norms[1], cot, *active1, scratch=flat,
    )
    if pairs:
        got_down1 = flip(down1[1], bits[0])
    rest = call(functools.partial(up_back, chunks), [*ff, *back], down_cot, *upward1, *ff_w, after=down1[-1:])
    grad_up, parts = rest[:chunks], rest[chunks:]
    up1 = weight_gradients(far_first, [(middle1, [(ref, False) for ref in grad_up])])
    if pairs:
        got_up1 = flip(up1[1], far_bits[0])
    grad_mixed, out_cot, gq, *rest = call(
        next_attention_back, [wide, thin, proj, *turned, vec, vec],
        *exchange(*parts), grad_comb, mixed1, norms[1][0], wo1, q1, k1, v1, lse1, ctx1, box, page, after=up1[-1:],
    )
    gkv, (dgain10, dshift10) = [other(ref, "stream") for ref in rest[:2]], rest[2:]
    qo1 = weight_gradients(near_first, [(rounded1, [(gq, False)]), (out_cot, [(ctx1, False)])])
    before = qo1[-1:]
    if pairs:
        got_qo1 = flip(qo1[1], bits[0])
        down1 = merge(down1[0], got_down1, after=qo1[1:])
        got_down1 = flip(down1[1], bits[1])
        before = down1[1:]
    parts = call(
        input_back, back, gq, *gkv, Held(w_query, 0, 1), Held(w_key, 0, 1), Held(w_value, 0, 1), after=before
    )
    kv1 = weight_gradients(near_first, [(rounded1, [(ref, True) for ref in gkv])], after=parts[:1])
    before = kv1[-1:]
    if pairs:
        got_kv1 = flip(kv1[1], bits[0])
        up1 = merge(up1[0], got_up1, after=[kv1[1], got_qo1])
        got_up1 = flip(up1[1], far_bits[1])
        before = up1[1:]

    grad_comb, down_cot, dgain01, dshift01, *rest = call(
        functools.partial(first_down_back, near_first, chunks), [wide, thin, vec, vec, *halves],
        *exchange(*parts), grad_mixed, combined0, norms[0][0], *active0, scratch=flat, after=before, fetch=ff_weights(0),
    )
    down0, ff_w = rest[: len(halves)], rest[len(halves) :]
    if pairs:
        got_down0 = flip(down0[1], bits[0])
    rest = call(functools.partial(up_back, chunks), [*ff, *back], down_cot, *upward0, *ff_w, after=down0[-1:])
    grad_up, parts = rest[:chunks], rest[chunks:]
    before = []
    if pairs:
        at1 = join((qo1[0], got_qo1), (kv1[0], got_kv1), after=[parts[0], got_down1])
        got_at1 = flip(at1[1], bits[1])
        down1 = merge(down1[0], got_down1, after=at1[1:], last=True)
        got_down1 = flip(down1[1], bits[2])
        before = down1[1:]
    grad_mixed, out_cot, dgain00, dshift00, gq, gkt, gvt, dtable, part = call(
        functools.partial(first_attention_back, levels),
        [wide, thin, vec, vec, proj, *turned, ((2, 8, LANES), F32), thin],
        *exchange(*parts), grad_comb, mixed0, norms[0][0], Held(w_out, 0, 0),
        q0, k0, v0, lse0, ctx0, ext0, box, page, Held(w_query, 0, 0), Held(w_key, 0, 0), Held(w_value, 0, 0), after=before,
    )
    vectors = [dgain00, dgain01, dgain10, dgain11, dshift00, dshift01, dshift10, dshift11]
    before = [dgain00, got_up1] if pairs else [dgain00]
    up0 = weight_gradients(near_first, [(middle0, [(ref, False) for ref in grad_up])], after=before)
    before = up0[-1:]
    if pairs:
        got_up0 = flip(up0[1], bits[0])
        at1 = merge(at1[0], got_at1, after=[up0[1], got_down0], last=True)
        got_at1 = flip(at1[1], bits[2])
        down0 = merge(down0[0], got_down0, after=at1[1:])
        got_down0 = flip(down0[1], bits[1])
        before = down0[1:]
    kv0 = weight_gradients(
        near_first, [(x, [(gkt, True), (gvt, True)])], after=before, extras=[*vectors, dtable] if pairs else ()
    )
    qo0 = weight_gradients(near_first, [(x, [(gq, False)]), (out_cot, [(ctx0, False)])], after=kv0[-1:])

    before = qo0[-1:]
    if pairs:
        got_kv0, got_qo0 = (flip(block[1], bits[0]) for block in (kv0, qo0))
        down0 = merge(down0[0], got_down0, after=[qo0[1], got_at1, got_down1], last=True)
        got_down0 = flip(down0[1], bits[2])

        up0 = merge(up0[0], got_up0, after=down0[1:])
        got_up0 = flip(up0[1], bits[1])

        kv0 = merge(kv0[0], got_kv0, after=[up0[1], got_up0, got_down0])
        got_kv0 = flip(kv0[1], bits[1])
        up0 = merge(up0[0], got_up0, after=kv0[1:], last=True)
        got_up0 = flip(up0[1], bits[2])
        up1 = merge(up1[0], got_up1, after=up0[1:], last=True)
        got_up1 = flip(up1[1], far_bits[2])
        before = up1[1:]
    grad_inputs, token = call(
        input_sum, [(*wide, SAVE), TOKEN], *exchange(part), grad_mixed, after=before,
    )
    before = [token]
    if pairs:
        qo0 = merge(qo0[0], got_qo0, after=[token, got_kv0])
        got_qo0 = flip(qo0[1], bits[1])
        kv0 = merge(kv0[0], got_kv0, after=qo0[1:], last=True)
        got_kv0 = flip(kv0[1], bits[2])
        before = kv0[1:]
        down0, up0, down1, up1, at1 = (
            (down0[0], got_down0), (up0[0], got_up0), (down1[0], got_down1), (up1[0], got_up1), (at1[0], got_at1)
        )
    else:
        (small,) = call(pack_kernel, [((24, d_model), F32)], *vectors, dtable)
        small = lax.psum(small, "dp")
        at1 = [jnp.concatenate([qo1[0], kv1[0]], axis=1)]
        down0, up0, down1, up1, kv0, qo0, at1 = (
            (lax.psum_scatter(g[0], "dp", scatter_dimension=0, tiled=True),)
            for g in (down0, up0, down1, up1, kv0, qo0, at1)
        )
    grad_down, grad_up, token = finish(
        [[(0, 0)], [(0, 1)], [(1, 0)], [(1, 1)]], [down0, down1, up0, up1], 2, hidden_width, after=before
    )
    if pairs:
        qo0 = merge(qo0[0], got_qo0, after=[token], last=True)
        got_qo0 = flip(qo0[1], bits[2])
        token = qo0[1]
        kv0, qo0 = (kv0[0], got_kv0), (qo0[0], got_qo0)
    grad_k, grad_v, *rest, token = finish(
        [[(0, 0), (1, 0)], [None, None, (0, 1), (1, 1)]], [kv0, at1], 2, width, 0 if pairs else None, after=[token], fresh=pairs
    )
    grad_q, grad_o, _ = finish([[(0, 0), (1, 0)], [(0, 1), (1, 1), None, None]], [qo0, at1], 2, width, after=[token], fresh=pairs)
    cut = d_model // n_dp
    some = 2 * levels // n_dp
    if pairs:
        vectors, grad_table = rest[0][:8, :cut], rest[0][8:24, :some]
    else:
        vectors = lax.dynamic_slice_in_dim(small[:8], me * cut, cut, 1)
        grad_table = lax.dynamic_slice_in_dim(small[8:], me * some, some, 1)
    vectors = vectors.reshape(2, 2, 2, cut)
    grad_table = grad_table.reshape(1, 2, 8, some)[:, :, :heads]
    flipped = lambda block: jnp.transpose(block, (0, 2, 1))[None]
    return (
        output.array[None, None],
        grad_inputs.array[None, None],
        grad_q[None],
        grad_k[None],
        grad_v[None],
        flipped(grad_o),
        grad_up[None],
        flipped(grad_down),
        vectors[:1],
        vectors[1:],
        grad_table,
    )


def solution(mesh):
    in_specs = (
        P("stream", "dp", None, None),
        P("stream", None, None, "mp"),
        P("stream", None, None, "mp"),
        P("stream", None, None, "mp"),
        P("stream", None, "mp", None),
        P("stream", None, None, "mp"),
        P("stream", None, "mp", None),
        P("stream", None, None, None),
        P("stream", None, None, None),
        P("stream", None, "mp", None),
        P("stream", None, "dp", None),
        P(None, "dp", None),
        P("stream", "dp", None, None),
    )
    out_specs = (
        P("stream", "dp", None, None),
        P("stream", "dp", None, None),
        P("stream", None, "dp", "mp"),
        P("stream", None, "dp", "mp"),
        P("stream", None, "dp", "mp"),
        P("stream", None, "mp", "dp"),
        P("stream", None, "dp", "mp"),
        P("stream", None, "mp", "dp"),
        P("stream", None, None, "dp"),
        P("stream", None, None, "dp"),
        P("stream", None, "mp", "dp"),
    )
    return jax.shard_map(body, mesh=mesh, in_specs=in_specs, out_specs=out_specs, check_vma=False)
```

```python
import functools

import jax
import jax.numpy as jnp
from jax import lax
from jax.experimental import pallas as pl
from jax.experimental.pallas import tpu as pltpu
from jax.sharding import PartitionSpec as P

HEAD_DIM = 64
EPSILON = 1e-05
MASKED = -1e30
LOW = jnp.bfloat16
F32 = jnp.float32
LANES = 128
SCALE = HEAD_DIM ** (-0.5)


def dot(left, right):
    return lax.dot_general(left, right, (((1,), (0,)), ((), ())), preferred_element_type=F32)


def dot_nt(left, right):
    return lax.dot_general(left, right, (((1,), (1,)), ((), ())), preferred_element_type=F32)


def iota(shape, dim):
    return lax.broadcasted_iota(jnp.int32, shape, dim)


def normalized(values):
    center = values - jnp.mean(values, -1, keepdims=True)
    rstd = lax.rsqrt(jnp.mean(center * center, -1, keepdims=True) + EPSILON)
    return center * rstd, rstd


def norm_back(grad, xhat, rstd, gain):
    scaled = grad * gain
    grad_in = rstd * (
        scaled
        - jnp.mean(scaled, -1, keepdims=True)
        - xhat * jnp.mean(scaled * xhat, -1, keepdims=True)
    )
    return grad_in, jnp.sum(grad * xhat, 0, keepdims=True), jnp.sum(grad, 0, keepdims=True)


class Held:
    def __init__(self, array, *index):
        self.array, self.dtype = array, array.dtype
        self.index = tuple(slice(None) if i is None else i for i in index)
        plain = tuple(0 if callable(i) else i for i in self.index)
        self.shape = jax.eval_shape(lambda: jnp.zeros(array.shape, jnp.int8)[plain]).shape

    def part(self, ref):
        return ref.at[tuple(i() if callable(i) else i for i in self.index)] if self.index else ref


class Arriving:
    def __init__(self, source, target, semaphore):
        self.copy = pltpu.make_async_copy(source, target, semaphore)
        self.copy.start()
        self.target, self.waited = target, False
        self.shape, self.dtype = target.shape, target.dtype

    def arrive(self):
        if not self.waited:
            self.copy.wait()
        self.waited = True

    def __getitem__(self, at):
        self.arrive()
        return self.target[at]


class Leaving:
    def __init__(self, source, target, semaphore):
        self.copy = pltpu.make_async_copy(source, target, semaphore)
        self.source, self.left = source, False
        self.shape, self.dtype = source.shape, source.dtype

    def leave(self):
        if not self.left:
            self.copy.start()
        self.left = True

    def __getitem__(self, at):
        return self.source[at]

    def __setitem__(self, at, value):
        self.source[at] = value


def leave(*refs):
    for ref in refs:
        if isinstance(ref, Leaving):
            ref.leave()


SAVE = "save"
BOTH = "both"
FREE = "free"
FORE = 4
BACK = 2
TOKEN = ((8, LANES), F32)


def call(kernel, outs, *args, after=(), fetch=(), scratch=(), vmem=24, time=0.0):
    arrays, specs, held = [], [], []
    for place, arg in enumerate(args):
        if isinstance(arg, Held):
            specs.append(pl.BlockSpec(memory_space=pltpu.HBM))
            arrays.append(pltpu.with_memory_space_constraint(arg.array, pltpu.HBM))
            held.append((place, arg))
        else:
            specs.append(pl.BlockSpec(memory_space=pltpu.VMEM))
            arrays.append(pltpu.with_memory_space_constraint(arg, pltpu.VMEM))
    arrays += list(after)
    specs += [pl.BlockSpec(memory_space=pl.ANY)] * len(after)
    for arg in fetch:
        specs.append(pl.BlockSpec(memory_space=pltpu.HBM))
        arrays.append(pltpu.with_memory_space_constraint(arg.array, pltpu.HBM))
    kinds = [out[2] if len(out) > 2 else None for out in outs]
    saved = [place for place, kind in enumerate(kinds) if kind == SAVE]
    both = [place for place, kind in enumerate(kinds) if kind == BOTH]
    out_shape, out_specs = [], []
    for out, kind in zip(outs, kinds):
        make = {None: pltpu.VMEM, BOTH: pltpu.VMEM, SAVE: pltpu.HBM, FREE: jax.ShapeDtypeStruct}[kind]
        out_shape.append(make(out[0], out[1]))
        out_specs.append(pl.BlockSpec(memory_space=pltpu.HBM if kind == SAVE else pltpu.VMEM))
    for place in both:
        out_shape.append(pltpu.HBM(*outs[place][:2]))
        out_specs.append(pl.BlockSpec(memory_space=pltpu.HBM))
    for arg in fetch:
        out_shape.append(pltpu.VMEM(arg.shape, arg.dtype))
        out_specs.append(pl.BlockSpec(memory_space=pltpu.VMEM))
    count, waits, fetched, n_outs, n_own = len(args), len(after), len(fetch), len(outs), len(scratch)
    buffers = [pltpu.VMEM(arg.shape, arg.dtype) for _, arg in held]
    buffers += [pltpu.VMEM(*outs[place][:2]) for place in saved]
    moves = len(buffers) + len(both) + fetched

    def run(*refs):
        refs = list(refs)
        take = lambda size: [refs.pop(0) for _ in range(size)]
        ins, _, sources, results = take(count), take(waits), take(fetched), take(n_outs)
        copies, fetches, own, targets = take(len(both)), take(fetched), take(n_own), take(len(buffers))
        semaphores = [refs[0].at[order] for order in range(moves)] if moves else []
        for place, arg in held:
            ins[place] = Arriving(arg.part(ins[place]), targets.pop(0), semaphores.pop(0))
        for place in saved:
            results[place] = Leaving(targets.pop(0), results[place], semaphores.pop(0))
        for place in both:
            results[place] = Leaving(results[place], copies.pop(0), semaphores.pop(0))
        coming = [Arriving(arg.part(ref), out, semaphores.pop(0)) for arg, ref, out in zip(fetch, sources, fetches)]
        kernel(*ins, *results, *own)
        for place, _ in held:
            ins[place].arrive()
        for ref in coming:
            ref.arrive()
        for place in saved + both:
            results[place].leave()
        for place in saved + both:
            results[place].copy.wait()

    results = pl.pallas_call(
        run,
        out_shape=out_shape,
        in_specs=specs,
        out_specs=out_specs,
        scratch_shapes=list(scratch) + buffers + ([pltpu.SemaphoreType.DMA((moves,))] if moves else []),
        compiler_params=pltpu.CompilerParams(vmem_limit_bytes=vmem * 1024 * 1024),
        cost_estimate=pl.CostEstimate(flops=int(1e5 + time * 1e9), bytes_accessed=1, transcendentals=0),
    )(*arrays)
    wrapped = [Held(r) if place in saved else r for place, r in enumerate(results[:n_outs])]
    wrapped += [Held(r) for r in results[n_outs : n_outs + len(both)]]
    return wrapped + list(results[n_outs + len(both) :])


def token_marks(boxes, pages):
    first = lax.axis_index("stream") == 0
    own = jnp.where(first, pages[0:1, :], pages[1:2, :])
    far = jnp.where(first, pages[1:2, :], pages[0:1, :])
    rows = jnp.concatenate([boxes[...], own, far, boxes[...], own, far], axis=0).astype(F32)
    return rows, jnp.transpose(rows)


def page_mask(cols, rows):
    return jnp.where(cols == rows, 0.0, MASKED).astype(F32)


def key_marks(cols, levels):
    lane = iota((cols.shape[0], LANES), 1)
    want = (levels - lane % levels).astype(F32)
    picked = jnp.where((lane // levels) % 2 == 0, cols[:, 0:1], cols[:, 1:2])
    return (picked == want).astype(F32).astype(LOW)


def query_marks(cols, levels):
    lane = iota((cols.shape[0], LANES), 1).astype(F32)
    hit = (lane == levels - cols[:, 0:1]) | (lane == levels + 40 - cols[:, 1:2])
    return hit.astype(F32).astype(LOW)


def bias_rows(table, head, levels):
    lane = iota((40, LANES), 1)
    blocks = []
    for dim in range(2):
        line = table[head][dim : dim + 1, :]
        line = jnp.concatenate(
            [line, jnp.broadcast_to(line[:, -1:], (1, LANES - line.shape[1]))], axis=1
        )
        base = jnp.broadcast_to(pltpu.roll(line, LANES - levels, 1), (40, LANES))
        spread = pltpu.roll(base, 0, 1, stride=1, stride_axis=0)
        spread = jnp.where(lane < levels, spread - spread[:, levels : levels + 1], 0.0)
        upper = spread.astype(LOW).astype(F32)
        lower = spread - upper
        blocks.append(
            pltpu.roll(upper, dim * levels, 1) + pltpu.roll(lower, (2 + dim) * levels, 1)
            if dim
            else upper + pltpu.roll(lower, 2 * levels, 1)
        )
    blocks.append(jnp.zeros((LANES - 80, LANES), F32))
    return jnp.concatenate(blocks, axis=0).astype(LOW)


def half_masks():
    lane = iota((1, LANES), 1)
    first = (lane < HEAD_DIM).astype(F32).astype(LOW)
    return first, (1 - first.astype(F32)).astype(LOW)


def attend(q_ref, k_ref, v_ref, ext_ref, key_ext, mask, lse_ref, ctx_ref):
    seq, width = q_ref.shape
    halves = half_masks()
    lane = iota((seq, LANES), 1)
    ones = jnp.ones((seq, LANES), LOW)
    lse = jnp.zeros((seq, LANES), F32)
    for pair in range(width // LANES):
        at = slice(pair * LANES, (pair + 1) * LANES)
        queries, keys = q_ref[:, at], k_ref[:, at]
        if key_ext is not None:
            keys = jnp.concatenate([keys, key_ext], axis=1)
        values = jnp.concatenate([v_ref[:, at], ones], axis=1)
        parts = []
        for half in range(2):
            head = 2 * pair + half
            left = queries * halves[half]
            if key_ext is not None:
                left = jnp.concatenate([left, ext_ref[:, head * LANES : (head + 1) * LANES]], axis=1)
            scores = dot_nt(left, keys) + mask
            top = jnp.max(scores, -1, keepdims=True)
            weights = jnp.exp(scores - top).astype(LOW)
            out = dot(weights, values)
            total = out[:, LANES:]
            parts.append(out[:, :LANES] / total)
            lse = jnp.where(lane == head, top + jnp.log(total), lse)
        ctx_ref[:, at] = jnp.where(lane < HEAD_DIM, parts[0], parts[1]).astype(LOW)
    lse_ref[...] = lse
    leave(lse_ref, ctx_ref)


def put_pieces(value, refs):
    size = refs[0].shape[0]
    for place, ref in enumerate(refs):
        ref[...] = value[place * size : (place + 1) * size].astype(LOW)


def summed(parts):
    count = len(parts) // 2
    return jnp.concatenate(
        [own[...].astype(F32) + far[...].astype(F32) for own, far in zip(parts[:count], parts[count:])], axis=0
    )


def first_attention(levels, boxes, pages, table, x, wq, wk, wv, wo, q, k, v, lse, ctx, ext, *parts):
    rows, cols = token_marks(boxes, pages)
    marks = query_marks(cols, levels)
    tables = [table[head] for head in range(table.shape[0])]
    for head in range(q.shape[1] // HEAD_DIM):
        ext[:, head * LANES : (head + 1) * LANES] = dot(
            marks, bias_rows(tables, head, levels)
        ).astype(LOW)
    leave(ext)
    mask = page_mask(cols[:, 2:3], rows[2:3, :])
    key_ext = key_marks(cols, levels)
    states = x[...]
    q[...] = (dot(states, wq[...]).astype(LOW).astype(F32) * SCALE).astype(LOW)
    k[...] = dot(states, wk[...]).astype(LOW)
    v[...] = dot(states, wv[...]).astype(LOW)
    leave(q, k, v)
    attend(q, k, v, ext, key_ext, mask, lse, ctx)
    put_pieces(dot(ctx[...], wo[...]), parts)


def next_states(*refs):
    parts, refs = refs[: 2 * FORE], refs[2 * FORE :]
    mixed, gain, shift, combined, hidden, rounded = refs
    xhat, _ = normalized(mixed[...])
    total = xhat * gain[0:1, :] + shift[0:1, :] + summed(parts)
    combined[...] = total
    leave(combined)
    xhat, _ = normalized(total)
    state = xhat * gain[1:2, :] + shift[1:2, :]
    hidden[...] = state
    rounded[...] = state.astype(LOW)


def shared_states(*refs):
    parts, refs = refs[: 2 * FORE], refs[2 * FORE :]
    mixed, gain, shift, *shares = refs
    here = lax.axis_index("mp")
    count, size = len(shares), shares[0].shape[0]
    for place, share in enumerate(shares):
        late = count + place
        pick = lambda group: jnp.where(here == 0, group[place][...], group[late][...]).astype(F32)
        start = pl.multiple_of((here * count + place) * size, size)
        xhat, _ = normalized(mixed[pl.ds(start, size), :])
        total = xhat * gain[0:1, :] + shift[0:1, :] + (pick(parts[:FORE]) + pick(parts[FORE:]))
        xhat, _ = normalized(total)
        share[...] = (xhat * gain[1:2, :] + shift[1:2, :]).astype(LOW)


def next_queries(rounded, wq, q):
    q[...] = (dot(rounded[...], wq[...]).astype(LOW).astype(F32) * SCALE).astype(LOW)


def copy_weights(wk, wv, out):
    out[...] = jnp.where(lax.axis_index("dp") % 2 == 0, wk[...], wv[...])


def next_attention(count, *refs):
    near, far, refs = refs[:count], refs[count : 2 * count], refs[2 * count :]
    near_weights, far_weights, q, boxes, pages, wo, k, v, lse, ctx, *parts = refs
    even = lax.axis_index("dp") % 2 == 0
    size = near[0].shape[0]
    here = lax.axis_index("mp") * (size * count)
    there = size * count - here
    for start, pieces in ((here, near), (there, far)):
        for place, states in enumerate(pieces):
            at = pl.ds(pl.multiple_of(start + place * size, size), size)
            first = dot(states[...], near_weights[...])
            second = dot(states[...], far_weights[...])
            k[at, :] = jnp.where(even, first, second).astype(LOW)
            v[at, :] = jnp.where(even, second, first).astype(LOW)
    rows, cols = token_marks(boxes, pages)
    mask = page_mask(cols[:, 2:3], rows[3:4, :])
    attend(q, k, v, None, None, mask, lse, ctx)
    put_pieces(dot(ctx[...], wo[...]), parts)


def normal_cdf(values):
    return 0.5 * (1.0 + lax.erf(values * (0.5**0.5)))


def feed_forward(chunks, *refs):
    parts, refs = refs[: 2 * FORE], refs[2 * FORE :]
    hidden, gain, shift, refs = refs[0], refs[1], refs[2], refs[3:]
    ups, downs, refs = refs[:chunks], refs[chunks : 2 * chunks], refs[2 * chunks :]
    mixed, middle, refs = refs[0], refs[1], refs[2:]
    upward, active, outs = refs[:chunks], refs[chunks : 2 * chunks], refs[2 * chunks :]
    total = hidden[...].astype(F32) + summed(parts)
    mixed[...] = total
    xhat, _ = normalized(total)
    low = (xhat * gain[0:1, :] + shift[0:1, :]).astype(LOW)
    middle[...] = low
    leave(mixed, middle)
    acc = None
    for index in range(chunks):
        up = dot(low, ups[index][...])
        upward[index][...] = up.astype(LOW)
        act = (up * normal_cdf(up)).astype(LOW)
        active[index][...] = act
        leave(upward[index], active[index])
        piece = dot(act, downs[index][...])
        acc = piece if acc is None else acc + piece
    put_pieces(acc, outs)


def down_back(order, chunks, grad, combined, gain, active, refs):
    grad_comb, down_cot, dgain, dshift, *outs, held, moved = refs
    xhat, rstd = normalized(combined)
    grad_in, dgain[...], dshift[...] = norm_back(grad, xhat, rstd, gain)
    grad_comb[...] = grad_in
    down_cot[...] = grad_in.astype(LOW)
    multiply(order, [(down_cot, [(ref, False) for ref in active])], outs, [held, moved])


def last_down_back(order, chunks, *refs):
    parts, refs = refs[: 2 * FORE], refs[2 * FORE :]
    mixed, gain, shift, cot, refs = *refs[:4], refs[4:]
    active, output, refs = refs[:chunks], refs[chunks], refs[chunks + 1 :]
    xhat, _ = normalized(mixed[...])
    combined = xhat * gain[0:1, :] + shift[0:1, :] + summed(parts)
    xhat, _ = normalized(combined)
    output[...] = (xhat * gain[1:2, :] + shift[1:2, :]).astype(LOW)
    leave(output)
    down_back(order, chunks, cot[...].astype(F32), combined, gain[1:2, :], active, refs)


def first_down_back(order, chunks, *refs):
    parts, refs = refs[: 2 * BACK], refs[2 * BACK :]
    grad_mixed, combined, gain, refs = *refs[:3], refs[3:]
    active, refs = refs[:chunks], refs[chunks:]
    grad = grad_mixed[...] + summed(parts)
    down_back(order, chunks, grad, combined[...], gain[1:2, :], active, refs)


def up_back(chunks, down_cot, *refs):
    upward, ups, downs, refs = refs[:chunks], refs[chunks : 2 * chunks], refs[2 * chunks : 3 * chunks], refs[3 * chunks :]
    grad_up, outs = refs[:chunks], refs[chunks:]
    low = down_cot[...]
    acc = None
    for index in range(chunks):
        back = dot_nt(low, downs[index][...])
        up = upward[index][...].astype(F32)
        slope = normal_cdf(up) + up * (jnp.exp(-0.5 * up * up) * 0.3989422804014327)
        gup = (back * slope).astype(LOW)
        grad_up[index][...] = gup
        piece = dot_nt(gup, ups[index][...])
        acc = piece if acc is None else acc + piece
    put_pieces(acc, outs)


def mixed_back(parts, grad_comb, mixed, gain, wo, grad_mixed, out_cot, dgain, dshift):
    grad = grad_comb[...] + summed(parts)
    xhat, rstd = normalized(mixed[...])
    grad_in, dgain[...], dshift[...] = norm_back(grad, xhat, rstd, gain[0:1, :])
    grad_mixed[...] = grad_in
    low = grad_in.astype(LOW)
    out_cot[...] = low
    return dot_nt(low, wo[...]).astype(LOW)


def heads_back(levels, page_row, pairs, gctx, q, k, v, lse, ctx, ext, boxes, pages, gq, gkt, gvt, dtable):
    seq = q.shape[0]
    rows, cols = token_marks(boxes, pages)
    mask = page_mask(cols[:, 2:3], rows[page_row : page_row + 1, :])
    halves = half_masks()
    lane = iota((seq, LANES), 1)
    if ext is not None:
        key_ext = key_marks(cols, levels)
        place = lane.astype(F32)
        back_ext = (
            (place == levels - cols[:, 0:1]) | (place == levels + HEAD_DIM - cols[:, 1:2])
        ).astype(F32).astype(LOW)
        line = iota((LANES, seq), 0).astype(F32)
        marks_t = ((line == rows[0:1, :]) | (line == rows[1:2, :] + HEAD_DIM)).astype(F32).astype(LOW)
        dtable[...] = jnp.zeros(dtable.shape, F32)
    for slot, pair in enumerate(pairs):
        at = slice(pair * LANES, (pair + 1) * LANES)
        queries, keys, values = q[:, at], k[:, at], v[:, at]
        gc = gctx[:, at]
        product = gc.astype(F32) * ctx[:, at].astype(F32)
        gc_t = jnp.transpose(gc)
        q_t = jnp.transpose(queries)
        keys_left = keys if ext is None else jnp.concatenate([keys, key_ext], axis=1)
        keys_right = keys if ext is None else jnp.concatenate([keys, back_ext], axis=1)
        parts = []
        for half in range(2):
            head = 2 * pair + half
            rows_at = slice(half * HEAD_DIM, (half + 1) * HEAD_DIM)
            out_at = slice(slot * LANES + half * HEAD_DIM, slot * LANES + (half + 1) * HEAD_DIM)
            left = queries * halves[half]
            if ext is not None:
                left = jnp.concatenate([left, ext[:, head * LANES : (head + 1) * LANES]], axis=1)
            scores = dot_nt(left, keys_left) + mask
            probs = jnp.exp(scores - lse[:, head : head + 1])
            delta = jnp.sum(
                jnp.where((lane < HEAD_DIM) == (half == 0), product, 0.0), -1, keepdims=True
            )
            grad_scores = probs * (dot_nt(gc * halves[half], values) - delta)
            score_cot = grad_scores.astype(LOW)
            gvt[out_at, :] = dot(gc_t[rows_at, :], probs.astype(LOW)).astype(LOW)
            gkt[out_at, :] = dot(q_t[rows_at, :], score_cot).astype(LOW)
            out = dot(score_cot, keys_right)
            parts.append(out[:, :LANES])
            if ext is not None:
                spread = out[:, LANES:]
                upper = spread.astype(LOW)
                lower = (spread - upper.astype(F32)).astype(LOW)
                block = dot(marks_t, upper) + dot(marks_t, lower)
                small = iota((40, LANES), 1)
                for dim in range(2):
                    piece = block[dim * HEAD_DIM : dim * HEAD_DIM + 40, :]
                    if dim:
                        piece = pltpu.roll(piece, HEAD_DIM, 1)
                    piece = jnp.where(small <= levels, piece, 0.0)
                    piece = pltpu.roll(piece, 0, 1, stride=1, stride_axis=0)
                    line = jnp.sum(piece, 0, keepdims=True)
                    over = pltpu.roll(line, LANES - 1, 1)
                    column = iota((1, LANES), 1)
                    line = jnp.where(column == 2 * levels - 1, line + over, line)
                    dtable[dim, head : head + 1, :] = line
        gq[:, slot * LANES : (slot + 1) * LANES] = (jnp.where(lane < HEAD_DIM, parts[0], parts[1]) * SCALE).astype(LOW)


def next_attention_back(*refs):
    parts, refs = refs[: 2 * BACK], refs[2 * BACK :]
    grad_comb, mixed, gain, wo, q, k, v, lse, ctx, boxes, pages, *outs = refs
    grad_mixed, out_cot, gq, gkt, gvt, dgain, dshift = outs
    gctx = mixed_back(parts, grad_comb, mixed, gain, wo, grad_mixed, out_cot, dgain, dshift)
    heads_back(0, 3, range(q.shape[1] // LANES), gctx, q, k, v, lse, ctx, None, boxes, pages, gq, gkt, gvt, None)


def first_attention_back(levels, *refs):
    parts, refs = refs[: 2 * BACK], refs[2 * BACK :]
    grad_comb, mixed, gain, wo, q, k, v, lse, ctx, ext, boxes, pages, wq, wk, wv, *outs = refs
    grad_mixed, out_cot, dgain, dshift, gq, gkt, gvt, dtable, part = outs
    gctx = mixed_back(parts, grad_comb, mixed, gain, wo, grad_mixed, out_cot, dgain, dshift)
    heads_back(levels, 2, range(q.shape[1] // LANES), gctx, q, k, v, lse, ctx, ext, boxes, pages, gq, gkt, gvt, dtable)
    input_back(gq, gkt, gvt, wq, wk, wv, part)


def input_back(gq, gkt, gvt, wq, wk, wv, *parts):
    put_pieces(
        dot_nt(gq[...], wq[...])
        + dot_nt(jnp.transpose(gkt[...]), wk[...])
        + dot_nt(jnp.transpose(gvt[...]), wv[...]),
        parts,
    )


def halving_order(bits):
    count = len(bits)
    flips = [
        sum(bit for place, bit in enumerate(bits) if block >> (count - 1 - place) & 1)
        for block in range(1 << count)
    ]
    return [lambda here, flip=flip: here ^ flip for flip in flips]


def arranged(order, source, held, moved):
    held[...] = jnp.transpose(source[...])
    if order == "plain":
        return held
    size = held.shape[0] // len(order)
    here = lax.axis_index("dp")
    for block, flip in enumerate(order):
        at = pl.multiple_of(flip(here) * size, size)
        moved[block * size : (block + 1) * size, :] = held[pl.ds(at, size), :]
    return moved


def multiply(order, groups, outs, scratch):
    column = 0
    for place, (source, rights) in enumerate(groups):
        left = arranged(order, source, scratch[2 * place], scratch[2 * place + 1])
        for right, flipped in rights:
            wide = right.shape[0] if flipped else right.shape[1]
            step = wide if flipped else min(512, wide)
            for start in range(0, wide, step):
                for index in reversed(range(len(outs))):
                    size = outs[index].shape[0]
                    rows = left[index * size : (index + 1) * size, :]
                    if flipped:
                        block = dot_nt(rows, right[start : start + step, :])
                    else:
                        block = dot(rows, right[:, start : start + step])
                    outs[index][:, column + start : column + start + step] = block.astype(LOW)
            column += wide


def put_vectors(order, lines, table, outs, column, turned, buckets):
    count, rest = len(lines), LANES - len(lines)
    rows = [line[...] for line in lines] + [jnp.zeros((rest, lines[0].shape[1]), F32)]
    turned[...] = jnp.transpose(jnp.concatenate(rows, axis=0))
    rows = [jnp.zeros((count, LANES), F32), table[0], table[1]]
    rows += [jnp.zeros((rest - 2 * table.shape[1], LANES), F32)]
    buckets[...] = jnp.transpose(jnp.concatenate(rows, axis=0))
    here = lax.axis_index("dp")
    size = turned.shape[0] // len(order)
    some = 2 * (LANES // 4) // len(order)
    per_out = len(order) // len(outs)
    for block, flip in enumerate(order):
        index = flip(here)
        part = turned[pl.ds(pl.multiple_of(index * size, size), size), :]
        first = part[:some] + buckets[pl.ds(pl.multiple_of(index * some, some), some), :]
        at = (block % per_out) * size
        outs[block // per_out][at : at + size, column : column + LANES] = jnp.concatenate(
            [first, part[some:]], axis=0
        ).astype(LOW)


def weight_products(order, plan, parts, lines, *refs):
    groups, position = [], 0
    for kinds in plan:
        stop = position + 1 + len(kinds)
        groups.append((refs[position], list(zip(refs[position + 1 : stop], kinds))))
        position = stop
    extras, refs = refs[position : position + lines], refs[position + lines :]
    outs, scratch = refs[:parts], refs[parts:]
    multiply(order, groups, outs, scratch)
    if lines:
        put_vectors(order, extras[:-1], extras[-1], outs, outs[0].shape[1] - LANES, *scratch[-2:])


def weight_gradients(order, groups, after=(), extras=()):
    plan, args, columns = [], [], LANES if extras else 0
    for left, rights in groups:
        plan.append([flipped for _, flipped in rights])
        args.append(left)
        for right, flipped in rights:
            args.append(right)
            columns += right.shape[0] if flipped else right.shape[1]
    seq, d_model = groups[0][0].shape
    parts = 1 if order == "plain" else 2
    scratch = [pltpu.VMEM((d_model, seq), LOW)] * (2 * len(groups))
    if extras:
        scratch += [pltpu.VMEM((d_model, LANES), F32), pltpu.VMEM((LANES, LANES), F32)]
    return call(
        functools.partial(weight_products, order, plan, parts, len(extras)),
        [((d_model // parts, columns), LOW)] * parts,
        *args, *extras, after=after, scratch=scratch,
    )


def merge_kernel(kept, got, keep, send):
    half = keep.shape[0]
    keep[...] = (kept[:half, :].astype(F32) + got[:half, :].astype(F32)).astype(LOW)
    leave(keep)
    send[...] = (kept[half:, :].astype(F32) + got[half:, :].astype(F32)).astype(LOW)


def merge(kept, got, after=(), last=False):
    half = ((kept.shape[0] // 2, kept.shape[1]), LOW)
    return call(merge_kernel, [(*half, SAVE) if last else half, half], kept, got, after=after)


def join_kernel(*refs):
    keep, send = refs[-2:]
    half, column = keep.shape[0], 0
    for kept, got in zip(refs[:-2:2], refs[1:-2:2]):
        at = slice(column, column + kept.shape[1])
        keep[:, at] = (kept[:half, :].astype(F32) + got[:half, :].astype(F32)).astype(LOW)
        send[:, at] = (kept[half:, :].astype(F32) + got[half:, :].astype(F32)).astype(LOW)
        column = at.stop


def join(*pairs, after=()):
    rows, columns = pairs[0][0].shape[0] // 2, sum(pair[0].shape[1] for pair in pairs)
    return call(join_kernel, [((rows, columns), LOW)] * 2, *[a for pair in pairs for a in pair], after=after)


def finish_kernel(plan, count, width, extra, *refs):
    token, ins = refs[-1], []
    token[...] = jnp.zeros(token.shape, F32)
    refs = list(refs)
    for targets, paired in plan:
        ins.append([refs.pop(0) for _ in range(2 if paired else 1)])
    read = lambda group, at: sum(ref[:, at].astype(F32) for ref in group)
    for group, (targets, _) in zip(ins, plan):
        for block, target in enumerate(targets):
            if target is None:
                continue
            out, layer = target
            refs[out][layer] = read(group, slice(block * width, (block + 1) * width))
    if extra is not None:
        size, columns = ins[extra][0].shape
        total = read(ins[extra], slice(columns - LANES, columns))
        total = jnp.concatenate([total, jnp.zeros((LANES - size, LANES), F32)], axis=0)
        refs[count][...] = jnp.transpose(total)


def finish(plan, groups, count, width, extra=None, after=(), fresh=False):
    size = groups[0][0].shape[0]
    outs = [((2, size, width), F32, SAVE)] * count
    if extra is not None:
        outs.append(((LANES, LANES), F32, FREE))
    plan = [(targets, len(group) > 1) for targets, group in zip(plan, groups)]
    results = call(
        functools.partial(finish_kernel, plan, count, width, extra), [*outs, TOKEN],
        *[Held(a) if isinstance(a, jax.Array) and not (fresh and place == 0) else a for place, group in enumerate(groups) for a in group],
        after=after,
    )
    return [out.array if isinstance(out, Held) else out for out in results]


def input_sum(*refs):
    *parts, grad, out, token = refs
    out[...] = grad[...] + summed(parts)
    token[...] = jnp.zeros(token.shape, F32)


def pack_kernel(*refs):
    table, out = refs[-2], refs[-1]
    lines = len(refs) - 2
    for place in range(lines):
        out[place : place + 1, :] = refs[place][...]
    rows = table.shape[1]
    rest = jnp.zeros((rows, out.shape[1] - LANES), F32)
    for dim in range(2):
        at = slice(lines + dim * rows, lines + (dim + 1) * rows)
        out[at, :] = jnp.concatenate([table[dim], rest], axis=1)


def other(block, axis):
    return lax.ppermute(block, axis, [(0, 1), (1, 0)])


def body(inputs, w_query, w_key, w_value, w_out, w_up, w_down, norm_gain, norm_shift, box_table, boxes, pages, cotangent):
    _, rows_here, seq, d_model = inputs.shape
    assert rows_here == 1
    width = w_query.shape[3]
    hidden_width = w_up.shape[3]
    heads = width // HEAD_DIM
    levels = box_table.shape[3] // 2
    n_dp = lax.axis_size("dp")
    me = lax.axis_index("dp")
    bits = [1 << place for place in range(n_dp.bit_length() - 1)]
    pairs = n_dp == 8 and d_model % (16 * n_dp) == 0
    far_bits = bits[1:] + bits[:1]
    near_first, far_first = [halving_order(b) if pairs else "plain" for b in (bits, far_bits)]

    cuts = [slice(at, at + 512) for at in range(0, hidden_width, 512)]
    chunks = len(cuts)

    def ff_weights(layer):
        return [Held(w_up, 0, layer, None, cut) for cut in cuts] + [Held(w_down, 0, layer, cut) for cut in cuts]

    def flip(block, bit):
        return lax.ppermute(block, "dp", [(i, i ^ bit) for i in range(n_dp)])

    def exchange(*parts):
        return [*parts, *(other(part, "mp") for part in parts)]

    wide = ((seq, d_model), F32)
    thin = ((seq, d_model), LOW)
    fore = [((seq // FORE, d_model), LOW)] * FORE
    back = [((seq // BACK, d_model), LOW)] * BACK
    proj = ((seq, width), LOW)
    turned = [((width, seq), LOW)] * 2
    ff = [((seq, 512), LOW)] * chunks
    stats = ((seq, LANES), F32)
    vec = ((1, d_model), F32)
    halves = [((d_model // 2, hidden_width), LOW)] * 2 if pairs else [((d_model, hidden_width), LOW)]
    flat = [pltpu.VMEM((d_model, seq), LOW)] * 2
    saved = lambda *shapes: [(*shape, SAVE) for shape in shapes]
    x = Held(inputs, 0, 0)
    box = Held(boxes, 0, None, 0)
    page = Held(pages, None, 0)
    table = Held(jnp.transpose(box_table[0], (1, 0, 2)))
    norms = [[Held(array, 0, layer) for array in (norm_gain, norm_shift)] for layer in range(2)]

    assert n_dp % 2 == 0
    (mine,) = call(
        copy_weights, [((d_model, width), LOW)], Held(w_key, 0, 1), Held(w_value, 0, 1)
    )
    near_weights = other(mine, "stream")
    far_weights = flip(near_weights, 1)
    q0, k0, v0, lse0, ctx0, ext0, *rest = call(
        functools.partial(first_attention, levels),
        [*saved(proj, proj, proj, stats, proj, ((seq, heads * LANES), LOW)), *fore],
        box, page, table, x, Held(w_query, 0, 0), Held(w_key, 0, 0), Held(w_value, 0, 0), Held(w_out, 0, 0),
        after=[mine], fetch=[*ff_weights(0), x],
    )
    parts, ff_w, x_here = rest[:FORE], rest[FORE:-1], rest[-1]
    mixed_here, middle0, *rest = call(
        functools.partial(feed_forward, chunks),
        [wide, thin, *ff, *ff, *fore],
        *exchange(*parts), x_here, *norms[0], *ff_w, fetch=[Held(w_query, 0, 1)],
    )
    upward0, active0, parts = rest[:chunks], rest[chunks : 2 * chunks], rest[2 * chunks : -1]
    mixed0, wq1 = mixed_here, rest[-1]
    sums = exchange(*parts)
    shares = call(shared_states, fore[:2], *sums, mixed_here, *norms[0])
    near = [other(share, "stream") for share in shares]
    combined0, hidden1, rounded1 = call(
        next_states, [*saved(wide), wide, thin], *sums, mixed_here, *norms[0], after=shares[:1],
    )
    q1, wo1 = call(next_queries, [proj], rounded1, wq1, fetch=[Held(w_out, 0, 1)])
    *near, q1 = lax.optimization_barrier((*near, q1))
    far = [other(share, "mp") for share in near]
    k1, v1, lse1, ctx1, *rest = call(
        functools.partial(next_attention, len(near)), [proj, proj, stats, proj, *fore],
        *near, *far, near_weights, far_weights, q1, box, page, wo1, after=[q1], fetch=ff_weights(1),
    )
    parts, ff_w = rest[:FORE], rest[FORE:]
    mixed1, middle1, *rest = call(
        functools.partial(feed_forward, chunks), [wide, thin, *ff, *ff, *fore],
        *exchange(*parts), hidden1, *norms[1], *ff_w, fetch=[Held(cotangent, 0, 0)],
    )
    upward1, active1, parts, cot = rest[:chunks], rest[chunks : 2 * chunks], rest[2 * chunks : -1], rest[-1]

    output, grad_comb, down_cot, dgain11, dshift11, *down1 = call(
        functools.partial(last_down_back, near_first, chunks), [(*thin, SAVE), wide, thin, vec, vec, *halves],
        *exchange(*parts), mixed1, *norms[1], cot, *active1, scratch=flat,
    )
    if pairs:
        got_down1 = flip(down1[1], bits[0])
    rest = call(functools.partial(up_back, chunks), [*ff, *back], down_cot, *upward1, *ff_w, after=down1[-1:])
    grad_up, parts = rest[:chunks], rest[chunks:]
    up1 = weight_gradients(far_first, [(middle1, [(ref, False) for ref in grad_up])])
    if pairs:
        got_up1 = flip(up1[1], far_bits[0])
    grad_mixed, out_cot, gq, *rest = call(
        next_attention_back, [wide, thin, proj, *turned, vec, vec],
        *exchange(*parts), grad_comb, mixed1, norms[1][0], wo1, q1, k1, v1, lse1, ctx1, box, page, after=up1[-1:],
    )
    gkv, (dgain10, dshift10) = [other(ref, "stream") for ref in rest[:2]], rest[2:]
    qo1 = weight_gradients(near_first, [(rounded1, [(gq, False)]), (out_cot, [(ctx1, False)])])
    before = qo1[-1:]
    if pairs:
        got_qo1 = flip(qo1[1], bits[0])
        down1 = merge(down1[0], got_down1, after=qo1[1:])
        got_down1 = flip(down1[1], bits[1])
        before = down1[1:]
    parts = call(
        input_back, back, gq, *gkv, Held(w_query, 0, 1), Held(w_key, 0, 1), Held(w_value, 0, 1), after=before
    )
    kv1 = weight_gradients(near_first, [(rounded1, [(ref, True) for ref in gkv])], after=parts[:1])
    before = kv1[-1:]
    if pairs:
        got_kv1 = flip(kv1[1], bits[0])
        up1 = merge(up1[0], got_up1, after=[kv1[1], got_qo1])
        got_up1 = flip(up1[1], far_bits[1])
        before = up1[1:]

    grad_comb, down_cot, dgain01, dshift01, *rest = call(
        functools.partial(first_down_back, near_first, chunks), [wide, thin, vec, vec, *halves],
        *exchange(*parts), grad_mixed, combined0, norms[0][0], *active0, scratch=flat, after=before, fetch=ff_weights(0),
    )
    down0, ff_w = rest[: len(halves)], rest[len(halves) :]
    if pairs:
        got_down0 = flip(down0[1], bits[0])
    rest = call(functools.partial(up_back, chunks), [*ff, *back], down_cot, *upward0, *ff_w, after=down0[-1:])
    grad_up, parts = rest[:chunks], rest[chunks:]
    before = []
    if pairs:
        at1 = join((qo1[0], got_qo1), (kv1[0], got_kv1), after=[parts[0], got_down1])
        got_at1 = flip(at1[1], bits[1])
        down1 = merge(down1[0], got_down1, after=at1[1:], last=True)
        got_down1 = flip(down1[1], bits[2])
        before = down1[1:]
    grad_mixed, out_cot, dgain00, dshift00, gq, gkt, gvt, dtable, part = call(
        functools.partial(first_attention_back, levels),
        [wide, thin, vec, vec, proj, *turned, ((2, 8, LANES), F32), thin],
        *exchange(*parts), grad_comb, mixed0, norms[0][0], Held(w_out, 0, 0),
        q0, k0, v0, lse0, ctx0, ext0, box, page, Held(w_query, 0, 0), Held(w_key, 0, 0), Held(w_value, 0, 0), after=before,
    )
    vectors = [dgain00, dgain01, dgain10, dgain11, dshift00, dshift01, dshift10, dshift11]
    before = [dgain00, got_up1] if pairs else [dgain00]
    up0 = weight_gradients(near_first, [(middle0, [(ref, False) for ref in grad_up])], after=before)
    before = up0[-1:]
    if pairs:
        got_up0 = flip(up0[1], bits[0])
        at1 = merge(at1[0], got_at1, after=[up0[1], got_down0], last=True)
        got_at1 = flip(at1[1], bits[2])
        down0 = merge(down0[0], got_down0, after=at1[1:])
        got_down0 = flip(down0[1], bits[1])
        before = down0[1:]
    kv0 = weight_gradients(
        near_first, [(x, [(gkt, True), (gvt, True)])], after=before, extras=[*vectors, dtable] if pairs else ()
    )
    qo0 = weight_gradients(near_first, [(x, [(gq, False)]), (out_cot, [(ctx0, False)])], after=kv0[-1:])

    before = qo0[-1:]
    if pairs:
        got_kv0, got_qo0 = (flip(block[1], bits[0]) for block in (kv0, qo0))
        down0 = merge(down0[0], got_down0, after=[qo0[1], got_at1, got_down1], last=True)
        got_down0 = flip(down0[1], bits[2])

        up0 = merge(up0[0], got_up0, after=down0[1:])
        got_up0 = flip(up0[1], bits[1])

        kv0 = merge(kv0[0], got_kv0, after=[up0[1], got_up0, got_down0])
        got_kv0 = flip(kv0[1], bits[1])
        up0 = merge(up0[0], got_up0, after=kv0[1:], last=True)
        got_up0 = flip(up0[1], bits[2])
        up1 = merge(up1[0], got_up1, after=up0[1:], last=True)
        got_up1 = flip(up1[1], far_bits[2])
        before = up1[1:]
    grad_inputs, token = call(
        input_sum, [(*wide, SAVE), TOKEN], *exchange(part), grad_mixed, after=before,
    )
    before = [token]
    if pairs:
        qo0 = merge(qo0[0], got_qo0, after=[token, got_kv0])
        got_qo0 = flip(qo0[1], bits[1])
        kv0 = merge(kv0[0], got_kv0, after=qo0[1:], last=True)
        got_kv0 = flip(kv0[1], bits[2])
        before = kv0[1:]
        down0, up0, down1, up1, at1 = (
            (down0[0], got_down0), (up0[0], got_up0), (down1[0], got_down1), (up1[0], got_up1), (at1[0], got_at1)
        )
    else:
        (small,) = call(pack_kernel, [((24, d_model), F32)], *vectors, dtable)
        small = lax.psum(small, "dp")
        at1 = [jnp.concatenate([qo1[0], kv1[0]], axis=1)]
        down0, up0, down1, up1, kv0, qo0, at1 = (
            (lax.psum_scatter(g[0], "dp", scatter_dimension=0, tiled=True),)
            for g in (down0, up0, down1, up1, kv0, qo0, at1)
        )
    grad_down, grad_up, token = finish(
        [[(0, 0)], [(0, 1)], [(1, 0)], [(1, 1)]], [down0, down1, up0, up1], 2, hidden_width, after=before
    )
    if pairs:
        qo0 = merge(qo0[0], got_qo0, after=[token], last=True)
        got_qo0 = flip(qo0[1], bits[2])
        token = qo0[1]
        kv0, qo0 = (kv0[0], got_kv0), (qo0[0], got_qo0)
    grad_k, grad_v, *rest, token = finish(
        [[(0, 0), (1, 0)], [None, None, (0, 1), (1, 1)]], [kv0, at1], 2, width, 0 if pairs else None, after=[token], fresh=pairs
    )
    grad_q, grad_o, _ = finish([[(0, 0), (1, 0)], [(0, 1), (1, 1), None, None]], [qo0, at1], 2, width, after=[token], fresh=pairs)
    cut = d_model // n_dp
    some = 2 * levels // n_dp
    if pairs:
        vectors, grad_table = rest[0][:8, :cut], rest[0][8:24, :some]
    else:
        vectors = lax.dynamic_slice_in_dim(small[:8], me * cut, cut, 1)
        grad_table = lax.dynamic_slice_in_dim(small[8:], me * some, some, 1)
    vectors = vectors.reshape(2, 2, 2, cut)
    grad_table = grad_table.reshape(1, 2, 8, some)[:, :, :heads]
    flipped = lambda block: jnp.transpose(block, (0, 2, 1))[None]
    return (
        output.array[None, None],
        grad_inputs.array[None, None],
        grad_q[None],
        grad_k[None],
        grad_v[None],
        flipped(grad_o),
        grad_up[None],
        flipped(grad_down),
        vectors[:1],
        vectors[1:],
        grad_table,
    )


def solution(mesh):
    in_specs = (
        P("stream", "dp", None, None),
        P("stream", None, None, "mp"),
        P("stream", None, None, "mp"),
        P("stream", None, None, "mp"),
        P("stream", None, "mp", None),
        P("stream", None, None, "mp"),
        P("stream", None, "mp", None),
        P("stream", None, None, None),
        P("stream", None, None, None),
        P("stream", None, "mp", None),
        P("stream", None, "dp", None),
        P(None, "dp", None),
        P("stream", "dp", None, None),
    )
    out_specs = (
        P("stream", "dp", None, None),
        P("stream", "dp", None, None),
        P("stream", None, "dp", "mp"),
        P("stream", None, "dp", "mp"),
        P("stream", None, "dp", "mp"),
        P("stream", None, "mp", "dp"),
        P("stream", None, "dp", "mp"),
        P("stream", None, "mp", "dp"),
        P("stream", None, None, "dp"),
        P("stream", None, None, "dp"),
        P("stream", None, "mp", "dp"),
    )
    return jax.shard_map(body, mesh=mesh, in_specs=in_specs, out_specs=out_specs, check_vma=False)
```

```python
import functools

import jax
import jax.numpy as jnp
from jax import lax
from jax.experimental import pallas as pl
from jax.experimental.pallas import tpu as pltpu
from jax.sharding import PartitionSpec as P

HEAD_DIM = 64
EPSILON = 1e-05
MASKED = -1e30
LOW = jnp.bfloat16
F32 = jnp.float32
LANES = 128
SCALE = HEAD_DIM ** (-0.5)


def dot(left, right):
    return lax.dot_general(left, right, (((1,), (0,)), ((), ())), preferred_element_type=F32)


def dot_nt(left, right):
    return lax.dot_general(left, right, (((1,), (1,)), ((), ())), preferred_element_type=F32)


def iota(shape, dim):
    return lax.broadcasted_iota(jnp.int32, shape, dim)


def normalized(values):
    center = values - jnp.mean(values, -1, keepdims=True)
    rstd = lax.rsqrt(jnp.mean(center * center, -1, keepdims=True) + EPSILON)
    return center * rstd, rstd


def norm_back(grad, xhat, rstd, gain):
    scaled = grad * gain
    grad_in = rstd * (
        scaled
        - jnp.mean(scaled, -1, keepdims=True)
        - xhat * jnp.mean(scaled * xhat, -1, keepdims=True)
    )
    return grad_in, jnp.sum(grad * xhat, 0, keepdims=True), jnp.sum(grad, 0, keepdims=True)


class Held:
    def __init__(self, array, *index):
        self.array, self.dtype = array, array.dtype
        self.index = tuple(slice(None) if i is None else i for i in index)
        plain = tuple(0 if callable(i) else i for i in self.index)
        self.shape = jax.eval_shape(lambda: jnp.zeros(array.shape, jnp.int8)[plain]).shape

    def part(self, ref):
        return ref.at[tuple(i() if callable(i) else i for i in self.index)] if self.index else ref


class Arriving:
    def __init__(self, source, target, semaphore):
        self.copy = pltpu.make_async_copy(source, target, semaphore)
        self.copy.start()
        self.target, self.waited = target, False
        self.shape, self.dtype = target.shape, target.dtype

    def arrive(self):
        if not self.waited:
            self.copy.wait()
        self.waited = True

    def __getitem__(self, at):
        self.arrive()
        return self.target[at]


class Leaving:
    def __init__(self, source, target, semaphore):
        self.copy = pltpu.make_async_copy(source, target, semaphore)
        self.source, self.left = source, False
        self.shape, self.dtype = source.shape, source.dtype

    def leave(self):
        if not self.left:
            self.copy.start()
        self.left = True

    def __getitem__(self, at):
        return self.source[at]

    def __setitem__(self, at, value):
        self.source[at] = value


def leave(*refs):
    for ref in refs:
        if isinstance(ref, Leaving):
            ref.leave()


SAVE = "save"
BOTH = "both"
FREE = "free"
FORE = 4
BACK = 2
TOKEN = ((8, LANES), F32)


def call(kernel, outs, *args, after=(), fetch=(), scratch=(), vmem=24, time=0.0):
    arrays, specs, held = [], [], []
    for place, arg in enumerate(args):
        if isinstance(arg, Held):
            specs.append(pl.BlockSpec(memory_space=pltpu.HBM))
            arrays.append(pltpu.with_memory_space_constraint(arg.array, pltpu.HBM))
            held.append((place, arg))
        else:
            specs.append(pl.BlockSpec(memory_space=pltpu.VMEM))
            arrays.append(pltpu.with_memory_space_constraint(arg, pltpu.VMEM))
    arrays += list(after)
    specs += [pl.BlockSpec(memory_space=pl.ANY)] * len(after)
    for arg in fetch:
        specs.append(pl.BlockSpec(memory_space=pltpu.HBM))
        arrays.append(pltpu.with_memory_space_constraint(arg.array, pltpu.HBM))
    kinds = [out[2] if len(out) > 2 else None for out in outs]
    saved = [place for place, kind in enumerate(kinds) if kind == SAVE]
    both = [place for place, kind in enumerate(kinds) if kind == BOTH]
    out_shape, out_specs = [], []
    for out, kind in zip(outs, kinds):
        make = {None: pltpu.VMEM, BOTH: pltpu.VMEM, SAVE: pltpu.HBM, FREE: jax.ShapeDtypeStruct}[kind]
        out_shape.append(make(out[0], out[1]))
        out_specs.append(pl.BlockSpec(memory_space=pltpu.HBM if kind == SAVE else pltpu.VMEM))
    for place in both:
        out_shape.append(pltpu.HBM(*outs[place][:2]))
        out_specs.append(pl.BlockSpec(memory_space=pltpu.HBM))
    for arg in fetch:
        out_shape.append(pltpu.VMEM(arg.shape, arg.dtype))
        out_specs.append(pl.BlockSpec(memory_space=pltpu.VMEM))
    count, waits, fetched, n_outs, n_own = len(args), len(after), len(fetch), len(outs), len(scratch)
    buffers = [pltpu.VMEM(arg.shape, arg.dtype) for _, arg in held]
    buffers += [pltpu.VMEM(*outs[place][:2]) for place in saved]
    moves = len(buffers) + len(both) + fetched

    def run(*refs):
        refs = list(refs)
        take = lambda size: [refs.pop(0) for _ in range(size)]
        ins, _, sources, results = take(count), take(waits), take(fetched), take(n_outs)
        copies, fetches, own, targets = take(len(both)), take(fetched), take(n_own), take(len(buffers))
        semaphores = [refs[0].at[order] for order in range(moves)] if moves else []
        for place, arg in held:
            ins[place] = Arriving(arg.part(ins[place]), targets.pop(0), semaphores.pop(0))
        for place in saved:
            results[place] = Leaving(targets.pop(0), results[place], semaphores.pop(0))
        for place in both:
            results[place] = Leaving(results[place], copies.pop(0), semaphores.pop(0))
        coming = [Arriving(arg.part(ref), out, semaphores.pop(0)) for arg, ref, out in zip(fetch, sources, fetches)]
        kernel(*ins, *results, *own)
        for place, _ in held:
            ins[place].arrive()
        for ref in coming:
            ref.arrive()
        for place in saved + both:
            results[place].leave()
        for place in saved + both:
            results[place].copy.wait()

    results = pl.pallas_call(
        run,
        out_shape=out_shape,
        in_specs=specs,
        out_specs=out_specs,
        scratch_shapes=list(scratch) + buffers + ([pltpu.SemaphoreType.DMA((moves,))] if moves else []),
        compiler_params=pltpu.CompilerParams(vmem_limit_bytes=vmem * 1024 * 1024),
        cost_estimate=pl.CostEstimate(flops=int(1e5 + time * 1e9), bytes_accessed=1, transcendentals=0),
    )(*arrays)
    wrapped = [Held(r) if place in saved else r for place, r in enumerate(results[:n_outs])]
    wrapped += [Held(r) for r in results[n_outs : n_outs + len(both)]]
    return wrapped + list(results[n_outs + len(both) :])


def token_marks(boxes, pages):
    first = lax.axis_index("stream") == 0
    own = jnp.where(first, pages[0:1, :], pages[1:2, :])
    far = jnp.where(first, pages[1:2, :], pages[0:1, :])
    rows = jnp.concatenate([boxes[...], own, far, boxes[...], own, far], axis=0).astype(F32)
    return rows, jnp.transpose(rows)


def page_mask(cols, rows):
    return jnp.where(cols == rows, 0.0, MASKED).astype(F32)


def key_marks(cols, levels):
    lane = iota((cols.shape[0], LANES), 1)
    want = (levels - lane % levels).astype(F32)
    picked = jnp.where((lane // levels) % 2 == 0, cols[:, 0:1], cols[:, 1:2])
    return (picked == want).astype(F32).astype(LOW)


def query_marks(cols, levels):
    lane = iota((cols.shape[0], LANES), 1).astype(F32)
    hit = (lane == levels - cols[:, 0:1]) | (lane == levels + 40 - cols[:, 1:2])
    return hit.astype(F32).astype(LOW)


def bias_rows(table, head, levels):
    lane = iota((40, LANES), 1)
    blocks = []
    for dim in range(2):
        line = table[head][dim : dim + 1, :]
        line = jnp.concatenate(
            [line, jnp.broadcast_to(line[:, -1:], (1, LANES - line.shape[1]))], axis=1
        )
        base = jnp.broadcast_to(pltpu.roll(line, LANES - levels, 1), (40, LANES))
        spread = pltpu.roll(base, 0, 1, stride=1, stride_axis=0)
        spread = jnp.where(lane < levels, spread - spread[:, levels : levels + 1], 0.0)
        upper = spread.astype(LOW).astype(F32)
        lower = spread - upper
        blocks.append(
            pltpu.roll(upper, dim * levels, 1) + pltpu.roll(lower, (2 + dim) * levels, 1)
            if dim
            else upper + pltpu.roll(lower, 2 * levels, 1)
        )
    blocks.append(jnp.zeros((LANES - 80, LANES), F32))
    return jnp.concatenate(blocks, axis=0).astype(LOW)


def half_masks():
    lane = iota((1, LANES), 1)
    first = (lane < HEAD_DIM).astype(F32).astype(LOW)
    return first, (1 - first.astype(F32)).astype(LOW)


def attend(q_ref, k_ref, v_ref, ext_ref, key_ext, mask, lse_ref, ctx_ref):
    seq, width = q_ref.shape
    halves = half_masks()
    lane = iota((seq, LANES), 1)
    ones = jnp.ones((seq, LANES), LOW)
    lse = jnp.zeros((seq, LANES), F32)
    for pair in range(width // LANES):
        at = slice(pair * LANES, (pair + 1) * LANES)
        queries, keys = q_ref[:, at], k_ref[:, at]
        if key_ext is not None:
            keys = jnp.concatenate([keys, key_ext], axis=1)
        values = jnp.concatenate([v_ref[:, at], ones], axis=1)
        parts = []
        for half in range(2):
            head = 2 * pair + half
            left = queries * halves[half]
            if key_ext is not None:
                left = jnp.concatenate([left, ext_ref[:, head * LANES : (head + 1) * LANES]], axis=1)
            scores = dot_nt(left, keys) + mask
            top = jnp.max(scores, -1, keepdims=True)
            weights = jnp.exp(scores - top).astype(LOW)
            out = dot(weights, values)
            total = out[:, LANES:]
            parts.append(out[:, :LANES] / total)
            lse = jnp.where(lane == head, top + jnp.log(total), lse)
        ctx_ref[:, at] = jnp.where(lane < HEAD_DIM, parts[0], parts[1]).astype(LOW)
    lse_ref[...] = lse
    leave(lse_ref, ctx_ref)


def put_pieces(value, refs):
    size = refs[0].shape[0]
    for place, ref in enumerate(refs):
        ref[...] = value[place * size : (place + 1) * size].astype(LOW)


def summed(parts):
    count = len(parts) // 2
    return jnp.concatenate(
        [own[...].astype(F32) + far[...].astype(F32) for own, far in zip(parts[:count], parts[count:])], axis=0
    )


def first_attention(levels, boxes, pages, table, x, wq, wk, wv, wo, q, k, v, lse, ctx, ext, *parts):
    rows, cols = token_marks(boxes, pages)
    marks = query_marks(cols, levels)
    tables = [table[head] for head in range(table.shape[0])]
    for head in range(q.shape[1] // HEAD_DIM):
        ext[:, head * LANES : (head + 1) * LANES] = dot(
            marks, bias_rows(tables, head, levels)
        ).astype(LOW)
    leave(ext)
    mask = page_mask(cols[:, 2:3], rows[2:3, :])
    key_ext = key_marks(cols, levels)
    states = x[...]
    q[...] = (dot(states, wq[...]).astype(LOW).astype(F32) * SCALE).astype(LOW)
    k[...] = dot(states, wk[...]).astype(LOW)
    v[...] = dot(states, wv[...]).astype(LOW)
    leave(q, k, v)
    attend(q, k, v, ext, key_ext, mask, lse, ctx)
    put_pieces(dot(ctx[...], wo[...]), parts)


def next_states(*refs):
    parts, refs = refs[: 2 * FORE], refs[2 * FORE :]
    mixed, gain, shift, combined, hidden, rounded = refs
    xhat, _ = normalized(mixed[...])
    total = xhat * gain[0:1, :] + shift[0:1, :] + summed(parts)
    combined[...] = total
    leave(combined)
    xhat, _ = normalized(total)
    state = xhat * gain[1:2, :] + shift[1:2, :]
    hidden[...] = state
    rounded[...] = state.astype(LOW)


def shared_states(*refs):
    parts, refs = refs[: 2 * FORE], refs[2 * FORE :]
    mixed, gain, shift, *shares = refs
    here = lax.axis_index("mp")
    count, size = len(shares), shares[0].shape[0]
    for place, share in enumerate(shares):
        late = count + place
        pick = lambda group: jnp.where(here == 0, group[place][...], group[late][...]).astype(F32)
        start = pl.multiple_of((here * count + place) * size, size)
        xhat, _ = normalized(mixed[pl.ds(start, size), :])
        total = xhat * gain[0:1, :] + shift[0:1, :] + (pick(parts[:FORE]) + pick(parts[FORE:]))
        xhat, _ = normalized(total)
        share[...] = (xhat * gain[1:2, :] + shift[1:2, :]).astype(LOW)


def next_queries(rounded, wq, q):
    q[...] = (dot(rounded[...], wq[...]).astype(LOW).astype(F32) * SCALE).astype(LOW)


def fetch_kernel(wk, wv, out, semaphore):
    even = lax.axis_index("dp") % 2 == 0
    for wanted, source in ((even, wk), (jnp.logical_not(even), wv)):

        @pl.when(wanted)
        def _(source=source):
            copy = pltpu.make_async_copy(source.at[0, 1], out, semaphore)
            copy.start()
            copy.wait()


def fetch_weights(wk, wv):
    hbm = lambda array: pltpu.with_memory_space_constraint(array, pltpu.HBM)
    return pl.pallas_call(
        fetch_kernel,
        out_shape=pltpu.VMEM(wk.shape[2:], wk.dtype),
        in_specs=[pl.BlockSpec(memory_space=pltpu.HBM)] * 2,
        out_specs=pl.BlockSpec(memory_space=pltpu.VMEM),
        scratch_shapes=[pltpu.SemaphoreType.DMA],
        cost_estimate=pl.CostEstimate(flops=int(1e5), bytes_accessed=1, transcendentals=0),
    )(hbm(wk), hbm(wv))


def next_attention(count, *refs):
    near, far, refs = refs[:count], refs[count : 2 * count], refs[2 * count :]
    near_weights, far_weights, q, boxes, pages, wo, k, v, lse, ctx, *parts = refs
    even = lax.axis_index("dp") % 2 == 0
    size = near[0].shape[0]
    here = lax.axis_index("mp") * (size * count)
    there = size * count - here
    for start, pieces in ((here, near), (there, far)):
        for place, states in enumerate(pieces):
            at = pl.ds(pl.multiple_of(start + place * size, size), size)
            first = dot(states[...], near_weights[...])
            second = dot(states[...], far_weights[...])
            k[at, :] = jnp.where(even, first, second).astype(LOW)
            v[at, :] = jnp.where(even, second, first).astype(LOW)
    rows, cols = token_marks(boxes, pages)
    mask = page_mask(cols[:, 2:3], rows[3:4, :])
    attend(q, k, v, None, None, mask, lse, ctx)
    put_pieces(dot(ctx[...], wo[...]), parts)


def normal_cdf(values):
    return 0.5 * (1.0 + lax.erf(values * (0.5**0.5)))


def feed_forward(chunks, *refs):
    parts, refs = refs[: 2 * FORE], refs[2 * FORE :]
    hidden, gain, shift, refs = refs[0], refs[1], refs[2], refs[3:]
    ups, downs, refs = refs[:chunks], refs[chunks : 2 * chunks], refs[2 * chunks :]
    mixed, middle, refs = refs[0], refs[1], refs[2:]
    upward, active, outs = refs[:chunks], refs[chunks : 2 * chunks], refs[2 * chunks :]
    total = hidden[...].astype(F32) + summed(parts)
    mixed[...] = total
    xhat, _ = normalized(total)
    low = (xhat * gain[0:1, :] + shift[0:1, :]).astype(LOW)
    middle[...] = low
    leave(mixed, middle)
    acc = None
    for index in range(chunks):
        up = dot(low, ups[index][...])
        upward[index][...] = up.astype(LOW)
        act = (up * normal_cdf(up)).astype(LOW)
        active[index][...] = act
        leave(upward[index], active[index])
        piece = dot(act, downs[index][...])
        acc = piece if acc is None else acc + piece
    put_pieces(acc, outs)


def down_back(order, chunks, grad, combined, gain, active, refs):
    grad_comb, down_cot, dgain, dshift, *outs, held, moved = refs
    xhat, rstd = normalized(combined)
    grad_in, dgain[...], dshift[...] = norm_back(grad, xhat, rstd, gain)
    grad_comb[...] = grad_in
    down_cot[...] = grad_in.astype(LOW)
    multiply(order, [(down_cot, [(ref, False) for ref in active])], outs, [held, moved])


def last_down_back(order, chunks, *refs):
    parts, refs = refs[: 2 * FORE], refs[2 * FORE :]
    mixed, gain, shift, cot, refs = *refs[:4], refs[4:]
    active, output, refs = refs[:chunks], refs[chunks], refs[chunks + 1 :]
    xhat, _ = normalized(mixed[...])
    combined = xhat * gain[0:1, :] + shift[0:1, :] + summed(parts)
    xhat, _ = normalized(combined)
    output[...] = (xhat * gain[1:2, :] + shift[1:2, :]).astype(LOW)
    leave(output)
    down_back(order, chunks, cot[...].astype(F32), combined, gain[1:2, :], active, refs)


def first_down_back(order, chunks, *refs):
    parts, refs = refs[: 2 * BACK], refs[2 * BACK :]
    grad_mixed, combined, gain, refs = *refs[:3], refs[3:]
    active, refs = refs[:chunks], refs[chunks:]
    grad = grad_mixed[...] + summed(parts)
    down_back(order, chunks, grad, combined[...], gain[1:2, :], active, refs)


def up_back(chunks, down_cot, *refs):
    upward, ups, downs, refs = refs[:chunks], refs[chunks : 2 * chunks], refs[2 * chunks : 3 * chunks], refs[3 * chunks :]
    grad_up, outs = refs[:chunks], refs[chunks:]
    low = down_cot[...]
    acc = None
    for index in range(chunks):
        back = dot_nt(low, downs[index][...])
        up = upward[index][...].astype(F32)
        slope = normal_cdf(up) + up * (jnp.exp(-0.5 * up * up) * 0.3989422804014327)
        gup = (back * slope).astype(LOW)
        grad_up[index][...] = gup
        piece = dot_nt(gup, ups[index][...])
        acc = piece if acc is None else acc + piece
    put_pieces(acc, outs)


def mixed_back(parts, grad_comb, mixed, gain, wo, grad_mixed, out_cot, dgain, dshift):
    grad = grad_comb[...] + summed(parts)
    xhat, rstd = normalized(mixed[...])
    grad_in, dgain[...], dshift[...] = norm_back(grad, xhat, rstd, gain[0:1, :])
    grad_mixed[...] = grad_in
    low = grad_in.astype(LOW)
    out_cot[...] = low
    return dot_nt(low, wo[...]).astype(LOW)


def heads_back(levels, page_row, pairs, gctx, q, k, v, lse, ctx, ext, boxes, pages, gq, gkt, gvt, dtable):
    seq = q.shape[0]
    rows, cols = token_marks(boxes, pages)
    mask = page_mask(cols[:, 2:3], rows[page_row : page_row + 1, :])
    halves = half_masks()
    lane = iota((seq, LANES), 1)
    if ext is not None:
        key_ext = key_marks(cols, levels)
        place = lane.astype(F32)
        back_ext = (
            (place == levels - cols[:, 0:1]) | (place == levels + HEAD_DIM - cols[:, 1:2])
        ).astype(F32).astype(LOW)
        line = iota((LANES, seq), 0).astype(F32)
        marks_t = ((line == rows[0:1, :]) | (line == rows[1:2, :] + HEAD_DIM)).astype(F32).astype(LOW)
        dtable[...] = jnp.zeros(dtable.shape, F32)
    for slot, pair in enumerate(pairs):
        at = slice(pair * LANES, (pair + 1) * LANES)
        queries, keys, values = q[:, at], k[:, at], v[:, at]
        gc = gctx[:, at]
        product = gc.astype(F32) * ctx[:, at].astype(F32)
        gc_t = jnp.transpose(gc)
        q_t = jnp.transpose(queries)
        keys_left = keys if ext is None else jnp.concatenate([keys, key_ext], axis=1)
        keys_right = keys if ext is None else jnp.concatenate([keys, back_ext], axis=1)
        parts = []
        for half in range(2):
            head = 2 * pair + half
            rows_at = slice(half * HEAD_DIM, (half + 1) * HEAD_DIM)
            out_at = slice(slot * LANES + half * HEAD_DIM, slot * LANES + (half + 1) * HEAD_DIM)
            left = queries * halves[half]
            if ext is not None:
                left = jnp.concatenate([left, ext[:, head * LANES : (head + 1) * LANES]], axis=1)
            scores = dot_nt(left, keys_left) + mask
            probs = jnp.exp(scores - lse[:, head : head + 1])
            delta = jnp.sum(
                jnp.where((lane < HEAD_DIM) == (half == 0), product, 0.0), -1, keepdims=True
            )
            grad_scores = probs * (dot_nt(gc * halves[half], values) - delta)
            score_cot = grad_scores.astype(LOW)
            gvt[out_at, :] = dot(gc_t[rows_at, :], probs.astype(LOW)).astype(LOW)
            gkt[out_at, :] = dot(q_t[rows_at, :], score_cot).astype(LOW)
            out = dot(score_cot, keys_right)
            parts.append(out[:, :LANES])
            if ext is not None:
                spread = out[:, LANES:]
                upper = spread.astype(LOW)
                lower = (spread - upper.astype(F32)).astype(LOW)
                block = dot(marks_t, upper) + dot(marks_t, lower)
                small = iota((40, LANES), 1)
                for dim in range(2):
                    piece = block[dim * HEAD_DIM : dim * HEAD_DIM + 40, :]
                    if dim:
                        piece = pltpu.roll(piece, HEAD_DIM, 1)
                    piece = jnp.where(small <= levels, piece, 0.0)
                    piece = pltpu.roll(piece, 0, 1, stride=1, stride_axis=0)
                    line = jnp.sum(piece, 0, keepdims=True)
                    over = pltpu.roll(line, LANES - 1, 1)
                    column = iota((1, LANES), 1)
                    line = jnp.where(column == 2 * levels - 1, line + over, line)
                    dtable[dim, head : head + 1, :] = line
        gq[:, slot * LANES : (slot + 1) * LANES] = (jnp.where(lane < HEAD_DIM, parts[0], parts[1]) * SCALE).astype(LOW)


def next_attention_back(*refs):
    parts, refs = refs[: 2 * BACK], refs[2 * BACK :]
    grad_comb, mixed, gain, wo, q, k, v, lse, ctx, boxes, pages, *outs = refs
    grad_mixed, out_cot, gq, gkt, gvt, dgain, dshift = outs
    gctx = mixed_back(parts, grad_comb, mixed, gain, wo, grad_mixed, out_cot, dgain, dshift)
    heads_back(0, 3, range(q.shape[1] // LANES), gctx, q, k, v, lse, ctx, None, boxes, pages, gq, gkt, gvt, None)


def first_attention_back(levels, *refs):
    parts, refs = refs[: 2 * BACK], refs[2 * BACK :]
    grad_comb, mixed, gain, wo, q, k, v, lse, ctx, ext, boxes, pages, wq, wk, wv, *outs = refs
    grad_mixed, out_cot, dgain, dshift, gq, gkt, gvt, dtable, part = outs
    gctx = mixed_back(parts, grad_comb, mixed, gain, wo, grad_mixed, out_cot, dgain, dshift)
    heads_back(levels, 2, range(q.shape[1] // LANES), gctx, q, k, v, lse, ctx, ext, boxes, pages, gq, gkt, gvt, dtable)
    input_back(gq, gkt, gvt, wq, wk, wv, part)


def input_back(gq, gkt, gvt, wq, wk, wv, *parts):
    put_pieces(
        dot_nt(gq[...], wq[...])
        + dot_nt(jnp.transpose(gkt[...]), wk[...])
        + dot_nt(jnp.transpose(gvt[...]), wv[...]),
        parts,
    )


def halving_order(bits):
    count = len(bits)
    flips = [
        sum(bit for place, bit in enumerate(bits) if block >> (count - 1 - place) & 1)
        for block in range(1 << count)
    ]
    return [lambda here, flip=flip: here ^ flip for flip in flips]


def arranged(order, source, held, moved):
    held[...] = jnp.transpose(source[...])
    if order == "plain":
        return held
    size = held.shape[0] // len(order)
    here = lax.axis_index("dp")
    for block, flip in enumerate(order):
        at = pl.multiple_of(flip(here) * size, size)
        moved[block * size : (block + 1) * size, :] = held[pl.ds(at, size), :]
    return moved


def multiply(order, groups, outs, scratch):
    column = 0
    for place, (source, rights) in enumerate(groups):
        left = arranged(order, source, scratch[2 * place], scratch[2 * place + 1])
        for right, flipped in rights:
            wide = right.shape[0] if flipped else right.shape[1]
            step = wide if flipped else min(512, wide)
            for start in range(0, wide, step):
                for index in reversed(range(len(outs))):
                    size = outs[index].shape[0]
                    rows = left[index * size : (index + 1) * size, :]
                    if flipped:
                        block = dot_nt(rows, right[start : start + step, :])
                    else:
                        block = dot(rows, right[:, start : start + step])
                    outs[index][:, column + start : column + start + step] = block.astype(LOW)
            column += wide


def put_vectors(order, lines, table, outs, column, turned, buckets):
    count, rest = len(lines), LANES - len(lines)
    rows = [line[...] for line in lines] + [jnp.zeros((rest, lines[0].shape[1]), F32)]
    turned[...] = jnp.transpose(jnp.concatenate(rows, axis=0))
    rows = [jnp.zeros((count, LANES), F32), table[0], table[1]]
    rows += [jnp.zeros((rest - 2 * table.shape[1], LANES), F32)]
    buckets[...] = jnp.transpose(jnp.concatenate(rows, axis=0))
    here = lax.axis_index("dp")
    size = turned.shape[0] // len(order)
    some = 2 * (LANES // 4) // len(order)
    per_out = len(order) // len(outs)
    for block, flip in enumerate(order):
        index = flip(here)
        part = turned[pl.ds(pl.multiple_of(index * size, size), size), :]
        first = part[:some] + buckets[pl.ds(pl.multiple_of(index * some, some), some), :]
        at = (block % per_out) * size
        outs[block // per_out][at : at + size, column : column + LANES] = jnp.concatenate(
            [first, part[some:]], axis=0
        ).astype(LOW)


def weight_products(order, plan, parts, lines, *refs):
    groups, position = [], 0
    for kinds in plan:
        stop = position + 1 + len(kinds)
        groups.append((refs[position], list(zip(refs[position + 1 : stop], kinds))))
        position = stop
    extras, refs = refs[position : position + lines], refs[position + lines :]
    outs, scratch = refs[:parts], refs[parts:]
    multiply(order, groups, outs, scratch)
    if lines:
        put_vectors(order, extras[:-1], extras[-1], outs, outs[0].shape[1] - LANES, *scratch[-2:])


def weight_gradients(order, groups, after=(), extras=()):
    plan, args, columns = [], [], LANES if extras else 0
    for left, rights in groups:
        plan.append([flipped for _, flipped in rights])
        args.append(left)
        for right, flipped in rights:
            args.append(right)
            columns += right.shape[0] if flipped else right.shape[1]
    seq, d_model = groups[0][0].shape
    parts = 1 if order == "plain" else 2
    scratch = [pltpu.VMEM((d_model, seq), LOW)] * (2 * len(groups))
    if extras:
        scratch += [pltpu.VMEM((d_model, LANES), F32), pltpu.VMEM((LANES, LANES), F32)]
    return call(
        functools.partial(weight_products, order, plan, parts, len(extras)),
        [((d_model // parts, columns), LOW)] * parts,
        *args, *extras, after=after, scratch=scratch,
    )


def merge_kernel(kept, got, keep, send):
    half = keep.shape[0]
    keep[...] = (kept[:half, :].astype(F32) + got[:half, :].astype(F32)).astype(LOW)
    leave(keep)
    send[...] = (kept[half:, :].astype(F32) + got[half:, :].astype(F32)).astype(LOW)


def merge(kept, got, after=(), last=False):
    half = ((kept.shape[0] // 2, kept.shape[1]), LOW)
    return call(merge_kernel, [(*half, SAVE) if last else half, half], kept, got, after=after)


def join_kernel(*refs):
    keep, send = refs[-2:]
    half, column = keep.shape[0], 0
    for kept, got in zip(refs[:-2:2], refs[1:-2:2]):
        at = slice(column, column + kept.shape[1])
        keep[:, at] = (kept[:half, :].astype(F32) + got[:half, :].astype(F32)).astype(LOW)
        send[:, at] = (kept[half:, :].astype(F32) + got[half:, :].astype(F32)).astype(LOW)
        column = at.stop


def join(*pairs, after=()):
    rows, columns = pairs[0][0].shape[0] // 2, sum(pair[0].shape[1] for pair in pairs)
    return call(join_kernel, [((rows, columns), LOW)] * 2, *[a for pair in pairs for a in pair], after=after)


def finish_kernel(plan, count, width, extra, *refs):
    token, ins = refs[-1], []
    token[...] = jnp.zeros(token.shape, F32)
    refs = list(refs)
    for targets, paired in plan:
        ins.append([refs.pop(0) for _ in range(2 if paired else 1)])
    read = lambda group, at: sum(ref[:, at].astype(F32) for ref in group)
    for group, (targets, _) in zip(ins, plan):
        for block, target in enumerate(targets):
            if target is None:
                continue
            out, layer = target
            refs[out][layer] = read(group, slice(block * width, (block + 1) * width))
    if extra is not None:
        size, columns = ins[extra][0].shape
        total = read(ins[extra], slice(columns - LANES, columns))
        total = jnp.concatenate([total, jnp.zeros((LANES - size, LANES), F32)], axis=0)
        refs[count][...] = jnp.transpose(total)


def finish(plan, groups, count, width, extra=None, after=(), fresh=False):
    size = groups[0][0].shape[0]
    outs = [((2, size, width), F32, SAVE)] * count
    if extra is not None:
        outs.append(((LANES, LANES), F32, FREE))
    plan = [(targets, len(group) > 1) for targets, group in zip(plan, groups)]
    results = call(
        functools.partial(finish_kernel, plan, count, width, extra), [*outs, TOKEN],
        *[Held(a) if isinstance(a, jax.Array) and not (fresh and place == 0) else a for place, group in enumerate(groups) for a in group],
        after=after,
    )
    return [out.array if isinstance(out, Held) else out for out in results]


def sum_kernel(*refs):
    *parts, out = refs
    at = slice(0, out.shape[1])
    out[...] = sum(part[:, at].astype(F32) for part in parts)


def last_kernel(layer1, *refs):
    *parts, first, second = refs
    width = first.shape[2]
    for place, out in enumerate((first, second)):
        at = slice(place * width, (place + 1) * width)
        out[0] = sum(part[:, at].astype(F32) for part in parts)
        out[1] = layer1[:, at]
        leave(out)


def input_sum(*refs):
    *parts, grad, out, token = refs
    out[...] = grad[...] + summed(parts)
    token[...] = jnp.zeros(token.shape, F32)


def pack_kernel(*refs):
    table, out = refs[-2], refs[-1]
    lines = len(refs) - 2
    for place in range(lines):
        out[place : place + 1, :] = refs[place][...]
    rows = table.shape[1]
    rest = jnp.zeros((rows, out.shape[1] - LANES), F32)
    for dim in range(2):
        at = slice(lines + dim * rows, lines + (dim + 1) * rows)
        out[at, :] = jnp.concatenate([table[dim], rest], axis=1)


def other(block, axis):
    return lax.ppermute(block, axis, [(0, 1), (1, 0)])


def body(inputs, w_query, w_key, w_value, w_out, w_up, w_down, norm_gain, norm_shift, box_table, boxes, pages, cotangent):
    _, rows_here, seq, d_model = inputs.shape
    assert rows_here == 1
    width = w_query.shape[3]
    hidden_width = w_up.shape[3]
    heads = width // HEAD_DIM
    levels = box_table.shape[3] // 2
    n_dp = lax.axis_size("dp")
    me = lax.axis_index("dp")
    bits = [1 << place for place in range(n_dp.bit_length() - 1)]
    pairs = n_dp == 8 and d_model % (16 * n_dp) == 0
    far_bits = bits[1:] + bits[:1]
    near_first, far_first = [halving_order(b) if pairs else "plain" for b in (bits, far_bits)]

    cuts = [slice(at, at + 512) for at in range(0, hidden_width, 512)]
    chunks = len(cuts)

    def ff_weights(layer):
        return [Held(w_up, 0, layer, None, cut) for cut in cuts] + [Held(w_down, 0, layer, cut) for cut in cuts]

    def flip(block, bit):
        return lax.ppermute(block, "dp", [(i, i ^ bit) for i in range(n_dp)])

    def exchange(*parts):
        return [*parts, *(other(part, "mp") for part in parts)]

    wide = ((seq, d_model), F32)
    thin = ((seq, d_model), LOW)
    fore = [((seq // FORE, d_model), LOW)] * FORE
    back = [((seq // BACK, d_model), LOW)] * BACK
    proj = ((seq, width), LOW)
    turned = [((width, seq), LOW)] * 2
    ff = [((seq, 512), LOW)] * chunks
    stats = ((seq, LANES), F32)
    vec = ((1, d_model), F32)
    halves = [((d_model // 2, hidden_width), LOW)] * 2 if pairs else [((d_model, hidden_width), LOW)]
    flat = [pltpu.VMEM((d_model, seq), LOW)] * 2
    saved = lambda *shapes: [(*shape, SAVE) for shape in shapes]
    x = Held(inputs, 0, 0)
    box = Held(boxes, 0, None, 0)
    page = Held(pages, None, 0)
    table = Held(jnp.transpose(box_table[0], (1, 0, 2)))
    norms = [[Held(array, 0, layer) for array in (norm_gain, norm_shift)] for layer in range(2)]

    assert n_dp % 2 == 0
    mine = fetch_weights(w_key, w_value)
    near_weights = other(mine, "stream")
    far_weights = flip(near_weights, 1)
    q0, k0, v0, lse0, ctx0, ext0, *rest = call(
        functools.partial(first_attention, levels),
        [*saved(proj, proj, proj, stats, proj, ((seq, heads * LANES), LOW)), *fore],
        box, page, table, x, Held(w_query, 0, 0), Held(w_key, 0, 0), Held(w_value, 0, 0), Held(w_out, 0, 0),
        after=[mine], fetch=[*ff_weights(0), x],
    )
    parts, ff_w, x_here = rest[:FORE], rest[FORE:-1], rest[-1]
    mixed_here, middle0, *rest = call(
        functools.partial(feed_forward, chunks),
        [wide, thin, *ff, *ff, *fore],
        *exchange(*parts), x_here, *norms[0], *ff_w, fetch=[Held(w_query, 0, 1)],
    )
    upward0, active0, parts = rest[:chunks], rest[chunks : 2 * chunks], rest[2 * chunks : -1]
    mixed0, wq1 = mixed_here, rest[-1]
    sums = exchange(*parts)
    shares = call(shared_states, fore[:2], *sums, mixed_here, *norms[0])
    near = [other(share, "stream") for share in shares]
    combined0, hidden1, rounded1 = call(
        next_states, [*saved(wide), wide, thin], *sums, mixed_here, *norms[0], after=shares[:1],
    )
    q1, wo1 = call(next_queries, [proj], rounded1, wq1, fetch=[Held(w_out, 0, 1)])
    *near, q1 = lax.optimization_barrier((*near, q1))
    far = [other(share, "mp") for share in near]
    k1, v1, lse1, ctx1, *rest = call(
        functools.partial(next_attention, len(near)), [proj, proj, stats, proj, *fore],
        *near, *far, near_weights, far_weights, q1, box, page, wo1, after=[q1], fetch=ff_weights(1),
    )
    parts, ff_w = rest[:FORE], rest[FORE:]
    mixed1, middle1, *rest = call(
        functools.partial(feed_forward, chunks), [wide, thin, *ff, *ff, *fore],
        *exchange(*parts), hidden1, *norms[1], *ff_w, fetch=[Held(cotangent, 0, 0)],
    )
    upward1, active1, parts, cot = rest[:chunks], rest[chunks : 2 * chunks], rest[2 * chunks : -1], rest[-1]

    output, grad_comb, down_cot, dgain11, dshift11, *down1 = call(
        functools.partial(last_down_back, near_first, chunks), [(*thin, SAVE), wide, thin, vec, vec, *halves],
        *exchange(*parts), mixed1, *norms[1], cot, *active1, scratch=flat,
    )
    if pairs:
        got_down1 = flip(down1[1], bits[0])
    rest = call(functools.partial(up_back, chunks), [*ff, *back], down_cot, *upward1, *ff_w, after=down1[-1:])
    grad_up, parts = rest[:chunks], rest[chunks:]
    up1 = weight_gradients(far_first, [(middle1, [(ref, False) for ref in grad_up])])
    if pairs:
        got_up1 = flip(up1[1], far_bits[0])
    grad_mixed, out_cot, gq, *rest = call(
        next_attention_back, [wide, thin, proj, *turned, vec, vec],
        *exchange(*parts), grad_comb, mixed1, norms[1][0], wo1, q1, k1, v1, lse1, ctx1, box, page, after=up1[-1:],
    )
    gkv, (dgain10, dshift10) = [other(ref, "stream") for ref in rest[:2]], rest[2:]
    qo1 = weight_gradients(near_first, [(rounded1, [(gq, False)]), (out_cot, [(ctx1, False)])])
    before = qo1[-1:]
    if pairs:
        got_qo1 = flip(qo1[1], bits[0])
        down1 = merge(down1[0], got_down1, after=qo1[1:])
        got_down1 = flip(down1[1], bits[1])
        before = down1[1:]
    parts = call(
        input_back, back, gq, *gkv, Held(w_query, 0, 1), Held(w_key, 0, 1), Held(w_value, 0, 1), after=before
    )
    kv1 = weight_gradients(near_first, [(rounded1, [(ref, True) for ref in gkv])], after=parts[:1])
    before = kv1[-1:]
    if pairs:
        got_kv1 = flip(kv1[1], bits[0])
        up1 = merge(up1[0], got_up1, after=[kv1[1], got_qo1])
        got_up1 = flip(up1[1], far_bits[1])
        before = up1[1:]

    grad_comb, down_cot, dgain01, dshift01, *rest = call(
        functools.partial(first_down_back, near_first, chunks), [wide, thin, vec, vec, *halves],
        *exchange(*parts), grad_mixed, combined0, norms[0][0], *active0, scratch=flat, after=before, fetch=ff_weights(0),
    )
    down0, ff_w = rest[: len(halves)], rest[len(halves) :]
    if pairs:
        got_down0 = flip(down0[1], bits[0])
    rest = call(functools.partial(up_back, chunks), [*ff, *back], down_cot, *upward0, *ff_w, after=down0[-1:])
    grad_up, parts = rest[:chunks], rest[chunks:]
    before = []
    if pairs:
        at1 = join((qo1[0], got_qo1), (kv1[0], got_kv1), after=[parts[0], got_down1])
        got_at1 = flip(at1[1], bits[1])
        down1 = merge(down1[0], got_down1, after=at1[1:], last=True)
        got_down1 = flip(down1[1], bits[2])
        before = down1[1:]
    grad_mixed, out_cot, dgain00, dshift00, gq, gkt, gvt, dtable, part = call(
        functools.partial(first_attention_back, levels),
        [wide, thin, vec, vec, proj, *turned, ((2, 8, LANES), F32), thin],
        *exchange(*parts), grad_comb, mixed0, norms[0][0], Held(w_out, 0, 0),
        q0, k0, v0, lse0, ctx0, ext0, box, page, Held(w_query, 0, 0), Held(w_key, 0, 0), Held(w_value, 0, 0), after=before,
    )
    vectors = [dgain00, dgain01, dgain10, dgain11, dshift00, dshift01, dshift10, dshift11]
    before = [dgain00, got_up1] if pairs else [dgain00]
    up0 = weight_gradients(near_first, [(middle0, [(ref, False) for ref in grad_up])], after=before)
    before = up0[-1:]
    if pairs:
        got_up0 = flip(up0[1], bits[0])
        at1 = merge(at1[0], got_at1, after=[up0[1], got_down0], last=True)
        got_at1 = flip(at1[1], bits[2])
        down0 = merge(down0[0], got_down0, after=at1[1:])
        got_down0 = flip(down0[1], bits[1])
        before = down0[1:]
    kv0 = weight_gradients(
        near_first, [(x, [(gkt, True), (gvt, True)])], after=before, extras=[*vectors, dtable] if pairs else ()
    )
    qo0 = weight_gradients(near_first, [(x, [(gq, False)]), (out_cot, [(ctx0, False)])], after=kv0[-1:])

    before = qo0[-1:]
    if pairs:
        got_kv0, got_qo0 = (flip(block[1], bits[0]) for block in (kv0, qo0))
        down0 = merge(down0[0], got_down0, after=[qo0[1], got_at1, got_down1], last=True)
        got_down0 = flip(down0[1], bits[2])

        up0 = merge(up0[0], got_up0, after=down0[1:])
        got_up0 = flip(up0[1], bits[1])

        kv0 = merge(kv0[0], got_kv0, after=[up0[1], got_up0, got_down0])
        got_kv0 = flip(kv0[1], bits[1])
        up0 = merge(up0[0], got_up0, after=kv0[1:], last=True)
        got_up0 = flip(up0[1], bits[2])
        up1 = merge(up1[0], got_up1, after=up0[1:], last=True)
        got_up1 = flip(up1[1], far_bits[2])
        before = up1[1:]
    grad_inputs, token = call(
        input_sum, [(*wide, SAVE), TOKEN], *exchange(part), grad_mixed, after=before,
    )
    before = [token]
    if pairs:
        qo0 = merge(qo0[0], got_qo0, after=[token, got_kv0])
        got_qo0 = flip(qo0[1], bits[1])
        kv0 = merge(kv0[0], got_kv0, after=qo0[1:], last=True)
        got_kv0 = flip(kv0[1], bits[2])
        before = kv0[1:]
        down0, up0, down1, up1, at1 = (
            (down0[0], got_down0), (up0[0], got_up0), (down1[0], got_down1), (up1[0], got_up1), (at1[0], got_at1)
        )
    else:
        (small,) = call(pack_kernel, [((24, d_model), F32)], *vectors, dtable)
        small = lax.psum(small, "dp")
        at1 = [jnp.concatenate([qo1[0], kv1[0]], axis=1)]
        down0, up0, down1, up1, kv0, qo0, at1 = (
            (lax.psum_scatter(g[0], "dp", scatter_dimension=0, tiled=True),)
            for g in (down0, up0, down1, up1, kv0, qo0, at1)
        )
    grad_down, grad_up, token = finish(
        [[(0, 0)], [(0, 1)], [(1, 0)], [(1, 1)]], [down0, down1, up0, up1], 2, hidden_width, after=before
    )
    if pairs:
        qo0 = merge(qo0[0], got_qo0, after=[token], last=True)
        got_qo0 = flip(qo0[1], bits[2])
        token = qo0[1]
        kv0, qo0 = (kv0[0], got_kv0), (qo0[0], got_qo0)
    grad_k, grad_v, *rest, token = finish(
        [[(0, 0), (1, 0)], [None, None, (0, 1), (1, 1)]], [kv0, at1], 2, width, 0 if pairs else None, after=[token], fresh=pairs
    )
    (layer1,) = call(sum_kernel, [((d_model // n_dp, 2 * width), F32)], *(Held(a) if isinstance(a, jax.Array) else a for a in at1), after=[token])
    grad_q, grad_o = call(
        last_kernel, [((2, d_model // n_dp, width), F32, SAVE)] * 2, layer1, *qo0
    )
    grad_q, grad_o = grad_q.array, grad_o.array
    cut = d_model // n_dp
    some = 2 * levels // n_dp
    if pairs:
        vectors, grad_table = rest[0][:8, :cut], rest[0][8:24, :some]
    else:
        vectors = lax.dynamic_slice_in_dim(small[:8], me * cut, cut, 1)
        grad_table = lax.dynamic_slice_in_dim(small[8:], me * some, some, 1)
    vectors = vectors.reshape(2, 2, 2, cut)
    grad_table = grad_table.reshape(1, 2, 8, some)[:, :, :heads]
    flipped = lambda block: jnp.transpose(block, (0, 2, 1))[None]
    return (
        output.array[None, None],
        grad_inputs.array[None, None],
        grad_q[None],
        grad_k[None],
        grad_v[None],
        flipped(grad_o),
        grad_up[None],
        flipped(grad_down),
        vectors[:1],
        vectors[1:],
        grad_table,
    )


def solution(mesh):
    in_specs = (
        P("stream", "dp", None, None),
        P("stream", None, None, "mp"),
        P("stream", None, None, "mp"),
        P("stream", None, None, "mp"),
        P("stream", None, "mp", None),
        P("stream", None, None, "mp"),
        P("stream", None, "mp", None),
        P("stream", None, None, None),
        P("stream", None, None, None),
        P("stream", None, "mp", None),
        P("stream", None, "dp", None),
        P(None, "dp", None),
        P("stream", "dp", None, None),
    )
    out_specs = (
        P("stream", "dp", None, None),
        P("stream", "dp", None, None),
        P("stream", None, "dp", "mp"),
        P("stream", None, "dp", "mp"),
        P("stream", None, "dp", "mp"),
        P("stream", None, "mp", "dp"),
        P("stream", None, "dp", "mp"),
        P("stream", None, "mp", "dp"),
        P("stream", None, None, "dp"),
        P("stream", None, None, "dp"),
        P("stream", None, "mp", "dp"),
    )
    return jax.shard_map(body, mesh=mesh, in_specs=in_specs, out_specs=out_specs, check_vma=False)
```

```python
import functools

import jax
import jax.numpy as jnp
from jax import lax
from jax.experimental import pallas as pl
from jax.experimental.pallas import tpu as pltpu
from jax.sharding import PartitionSpec as P

HEAD_DIM = 64
EPSILON = 1e-05
MASKED = -1e30
LOW = jnp.bfloat16
F32 = jnp.float32
LANES = 128
SCALE = HEAD_DIM ** (-0.5)


def dot(left, right):
    return lax.dot_general(left, right, (((1,), (0,)), ((), ())), preferred_element_type=F32)


def dot_nt(left, right):
    return lax.dot_general(left, right, (((1,), (1,)), ((), ())), preferred_element_type=F32)


def iota(shape, dim):
    return lax.broadcasted_iota(jnp.int32, shape, dim)


def normalized(values):
    center = values - jnp.mean(values, -1, keepdims=True)
    rstd = lax.rsqrt(jnp.mean(center * center, -1, keepdims=True) + EPSILON)
    return center * rstd, rstd


def norm_back(grad, xhat, rstd, gain):
    scaled = grad * gain
    grad_in = rstd * (
        scaled
        - jnp.mean(scaled, -1, keepdims=True)
        - xhat * jnp.mean(scaled * xhat, -1, keepdims=True)
    )
    return grad_in, jnp.sum(grad * xhat, 0, keepdims=True), jnp.sum(grad, 0, keepdims=True)


class Held:
    def __init__(self, array, *index):
        self.array, self.dtype = array, array.dtype
        self.index = tuple(slice(None) if i is None else i for i in index)
        plain = tuple(0 if callable(i) else i for i in self.index)
        self.shape = jax.eval_shape(lambda: jnp.zeros(array.shape, jnp.int8)[plain]).shape

    def part(self, ref):
        return ref.at[tuple(i() if callable(i) else i for i in self.index)] if self.index else ref


class Arriving:
    def __init__(self, source, target, semaphore):
        self.copy = pltpu.make_async_copy(source, target, semaphore)
        self.copy.start()
        self.target, self.waited = target, False
        self.shape, self.dtype = target.shape, target.dtype

    def arrive(self):
        if not self.waited:
            self.copy.wait()
        self.waited = True

    def __getitem__(self, at):
        self.arrive()
        return self.target[at]


class Leaving:
    def __init__(self, source, target, semaphore):
        self.copy = pltpu.make_async_copy(source, target, semaphore)
        self.source, self.left = source, False
        self.shape, self.dtype = source.shape, source.dtype

    def leave(self):
        if not self.left:
            self.copy.start()
        self.left = True

    def __getitem__(self, at):
        return self.source[at]

    def __setitem__(self, at, value):
        self.source[at] = value


def leave(*refs):
    for ref in refs:
        if isinstance(ref, Leaving):
            ref.leave()


SAVE = "save"
BOTH = "both"
FREE = "free"
FORE = 4
BACK = 2
TOKEN = ((8, LANES), F32)


def call(kernel, outs, *args, after=(), fetch=(), scratch=(), vmem=24, time=0.0):
    arrays, specs, held = [], [], []
    for place, arg in enumerate(args):
        if isinstance(arg, Held):
            specs.append(pl.BlockSpec(memory_space=pltpu.HBM))
            arrays.append(pltpu.with_memory_space_constraint(arg.array, pltpu.HBM))
            held.append((place, arg))
        else:
            specs.append(pl.BlockSpec(memory_space=pltpu.VMEM))
            arrays.append(pltpu.with_memory_space_constraint(arg, pltpu.VMEM))
    arrays += list(after)
    specs += [pl.BlockSpec(memory_space=pl.ANY)] * len(after)
    for arg in fetch:
        specs.append(pl.BlockSpec(memory_space=pltpu.HBM))
        arrays.append(pltpu.with_memory_space_constraint(arg.array, pltpu.HBM))
    kinds = [out[2] if len(out) > 2 else None for out in outs]
    saved = [place for place, kind in enumerate(kinds) if kind == SAVE]
    both = [place for place, kind in enumerate(kinds) if kind == BOTH]
    out_shape, out_specs = [], []
    for out, kind in zip(outs, kinds):
        make = {None: pltpu.VMEM, BOTH: pltpu.VMEM, SAVE: pltpu.HBM, FREE: jax.ShapeDtypeStruct}[kind]
        out_shape.append(make(out[0], out[1]))
        out_specs.append(pl.BlockSpec(memory_space=pltpu.HBM if kind == SAVE else pltpu.VMEM))
    for place in both:
        out_shape.append(pltpu.HBM(*outs[place][:2]))
        out_specs.append(pl.BlockSpec(memory_space=pltpu.HBM))
    for arg in fetch:
        out_shape.append(pltpu.VMEM(arg.shape, arg.dtype))
        out_specs.append(pl.BlockSpec(memory_space=pltpu.VMEM))
    count, waits, fetched, n_outs, n_own = len(args), len(after), len(fetch), len(outs), len(scratch)
    buffers = [pltpu.VMEM(arg.shape, arg.dtype) for _, arg in held]
    buffers += [pltpu.VMEM(*outs[place][:2]) for place in saved]
    moves = len(buffers) + len(both) + fetched

    def run(*refs):
        refs = list(refs)
        take = lambda size: [refs.pop(0) for _ in range(size)]
        ins, _, sources, results = take(count), take(waits), take(fetched), take(n_outs)
        copies, fetches, own, targets = take(len(both)), take(fetched), take(n_own), take(len(buffers))
        semaphores = [refs[0].at[order] for order in range(moves)] if moves else []
        for place, arg in held:
            ins[place] = Arriving(arg.part(ins[place]), targets.pop(0), semaphores.pop(0))
        for place in saved:
            results[place] = Leaving(targets.pop(0), results[place], semaphores.pop(0))
        for place in both:
            results[place] = Leaving(results[place], copies.pop(0), semaphores.pop(0))
        coming = [Arriving(arg.part(ref), out, semaphores.pop(0)) for arg, ref, out in zip(fetch, sources, fetches)]
        kernel(*ins, *results, *own)
        for place, _ in held:
            ins[place].arrive()
        for ref in coming:
            ref.arrive()
        for place in saved + both:
            results[place].leave()
        for place in saved + both:
            results[place].copy.wait()

    results = pl.pallas_call(
        run,
        out_shape=out_shape,
        in_specs=specs,
        out_specs=out_specs,
        scratch_shapes=list(scratch) + buffers + ([pltpu.SemaphoreType.DMA((moves,))] if moves else []),
        compiler_params=pltpu.CompilerParams(vmem_limit_bytes=vmem * 1024 * 1024),
        cost_estimate=pl.CostEstimate(flops=int(1e5 + time * 1e9), bytes_accessed=1, transcendentals=0),
    )(*arrays)
    wrapped = [Held(r) if place in saved else r for place, r in enumerate(results[:n_outs])]
    wrapped += [Held(r) for r in results[n_outs : n_outs + len(both)]]
    return wrapped + list(results[n_outs + len(both) :])


def token_marks(boxes, pages):
    first = lax.axis_index("stream") == 0
    own = jnp.where(first, pages[0:1, :], pages[1:2, :])
    far = jnp.where(first, pages[1:2, :], pages[0:1, :])
    rows = jnp.concatenate([boxes[...], own, far, boxes[...], own, far], axis=0).astype(F32)
    return rows, jnp.transpose(rows)


def page_mask(cols, rows):
    return jnp.where(cols == rows, 0.0, MASKED).astype(F32)


def key_marks(cols, levels):
    lane = iota((cols.shape[0], LANES), 1)
    want = (levels - lane % levels).astype(F32)
    picked = jnp.where((lane // levels) % 2 == 0, cols[:, 0:1], cols[:, 1:2])
    return (picked == want).astype(F32).astype(LOW)


def query_marks(cols, levels):
    lane = iota((cols.shape[0], LANES), 1).astype(F32)
    hit = (lane == levels - cols[:, 0:1]) | (lane == levels + 40 - cols[:, 1:2])
    return hit.astype(F32).astype(LOW)


def bias_rows(table, head, levels):
    lane = iota((40, LANES), 1)
    blocks = []
    for dim in range(2):
        line = table[head][dim : dim + 1, :]
        line = jnp.concatenate(
            [line, jnp.broadcast_to(line[:, -1:], (1, LANES - line.shape[1]))], axis=1
        )
        base = jnp.broadcast_to(pltpu.roll(line, LANES - levels, 1), (40, LANES))
        spread = pltpu.roll(base, 0, 1, stride=1, stride_axis=0)
        spread = jnp.where(lane < levels, spread - spread[:, levels : levels + 1], 0.0)
        upper = spread.astype(LOW).astype(F32)
        lower = spread - upper
        blocks.append(
            pltpu.roll(upper, dim * levels, 1) + pltpu.roll(lower, (2 + dim) * levels, 1)
            if dim
            else upper + pltpu.roll(lower, 2 * levels, 1)
        )
    blocks.append(jnp.zeros((LANES - 80, LANES), F32))
    return jnp.concatenate(blocks, axis=0).astype(LOW)


def half_masks():
    lane = iota((1, LANES), 1)
    first = (lane < HEAD_DIM).astype(F32).astype(LOW)
    return first, (1 - first.astype(F32)).astype(LOW)


def attend(q_ref, k_ref, v_ref, ext_ref, key_ext, mask, lse_ref, ctx_ref):
    seq, width = q_ref.shape
    halves = half_masks()
    lane = iota((seq, LANES), 1)
    ones = jnp.ones((seq, LANES), LOW)
    lse = jnp.zeros((seq, LANES), F32)
    for pair in range(width // LANES):
        at = slice(pair * LANES, (pair + 1) * LANES)
        queries, keys = q_ref[:, at], k_ref[:, at]
        if key_ext is not None:
            keys = jnp.concatenate([keys, key_ext], axis=1)
        values = jnp.concatenate([v_ref[:, at], ones], axis=1)
        parts = []
        for half in range(2):
            head = 2 * pair + half
            left = queries * halves[half]
            if key_ext is not None:
                left = jnp.concatenate([left, ext_ref[:, head * LANES : (head + 1) * LANES]], axis=1)
            scores = dot_nt(left, keys) + mask
            top = jnp.max(scores, -1, keepdims=True)
            weights = jnp.exp(scores - top).astype(LOW)
            out = dot(weights, values)
            total = out[:, LANES:]
            parts.append(out[:, :LANES] / total)
            lse = jnp.where(lane == head, top + jnp.log(total), lse)
        ctx_ref[:, at] = jnp.where(lane < HEAD_DIM, parts[0], parts[1]).astype(LOW)
    lse_ref[...] = lse
    leave(lse_ref, ctx_ref)


def put_pieces(value, refs):
    size = refs[0].shape[0]
    for place, ref in enumerate(refs):
        ref[...] = value[place * size : (place + 1) * size].astype(LOW)


def summed(parts):
    count = len(parts) // 2
    return jnp.concatenate(
        [own[...].astype(F32) + far[...].astype(F32) for own, far in zip(parts[:count], parts[count:])], axis=0
    )


def first_attention(levels, boxes, pages, table, x, wq, wk, wv, wo, q, k, v, lse, ctx, ext, *parts):
    rows, cols = token_marks(boxes, pages)
    marks = query_marks(cols, levels)
    tables = [table[head] for head in range(table.shape[0])]
    for head in range(q.shape[1] // HEAD_DIM):
        ext[:, head * LANES : (head + 1) * LANES] = dot(
            marks, bias_rows(tables, head, levels)
        ).astype(LOW)
    leave(ext)
    mask = page_mask(cols[:, 2:3], rows[2:3, :])
    key_ext = key_marks(cols, levels)
    states = x[...]
    q[...] = (dot(states, wq[...]).astype(LOW).astype(F32) * SCALE).astype(LOW)
    k[...] = dot(states, wk[...]).astype(LOW)
    v[...] = dot(states, wv[...]).astype(LOW)
    leave(q, k, v)
    attend(q, k, v, ext, key_ext, mask, lse, ctx)
    put_pieces(dot(ctx[...], wo[...]), parts)


def next_states(*refs):
    parts, refs = refs[: 2 * FORE], refs[2 * FORE :]
    mixed, gain, shift, combined, hidden, rounded = refs
    xhat, _ = normalized(mixed[...])
    total = xhat * gain[0:1, :] + shift[0:1, :] + summed(parts)
    combined[...] = total
    leave(combined)
    xhat, _ = normalized(total)
    state = xhat * gain[1:2, :] + shift[1:2, :]
    hidden[...] = state
    rounded[...] = state.astype(LOW)


def shared_states(*refs):
    parts, refs = refs[: 2 * FORE], refs[2 * FORE :]
    mixed, gain, shift, *shares = refs
    here = lax.axis_index("mp")
    count, size = len(shares), shares[0].shape[0]
    for place, share in enumerate(shares):
        late = count + place
        pick = lambda group: jnp.where(here == 0, group[place][...], group[late][...]).astype(F32)
        start = pl.multiple_of((here * count + place) * size, size)
        xhat, _ = normalized(mixed[pl.ds(start, size), :])
        total = xhat * gain[0:1, :] + shift[0:1, :] + (pick(parts[:FORE]) + pick(parts[FORE:]))
        xhat, _ = normalized(total)
        share[...] = (xhat * gain[1:2, :] + shift[1:2, :]).astype(LOW)


def next_queries(rounded, wq, q):
    q[...] = (dot(rounded[...], wq[...]).astype(LOW).astype(F32) * SCALE).astype(LOW)


def fetch_kernel(wk, wv, out, semaphore):
    even = lax.axis_index("dp") % 2 == 0
    for wanted, source in ((even, wk), (jnp.logical_not(even), wv)):

        @pl.when(wanted)
        def _(source=source):
            copy = pltpu.make_async_copy(source.at[0, 1], out, semaphore)
            copy.start()
            copy.wait()


def fetch_weights(wk, wv):
    hbm = lambda array: pltpu.with_memory_space_constraint(array, pltpu.HBM)
    return pl.pallas_call(
        fetch_kernel,
        out_shape=pltpu.VMEM(wk.shape[2:], wk.dtype),
        in_specs=[pl.BlockSpec(memory_space=pltpu.HBM)] * 2,
        out_specs=pl.BlockSpec(memory_space=pltpu.VMEM),
        scratch_shapes=[pltpu.SemaphoreType.DMA],
        cost_estimate=pl.CostEstimate(flops=int(1e5), bytes_accessed=1, transcendentals=0),
    )(hbm(wk), hbm(wv))


def next_attention(count, *refs):
    near, far, refs = refs[:count], refs[count : 2 * count], refs[2 * count :]
    near_weights, far_weights, q, boxes, pages, wo, k, v, lse, ctx, *parts = refs
    even = lax.axis_index("dp") % 2 == 0
    size = near[0].shape[0]
    here = lax.axis_index("mp") * (size * count)
    there = size * count - here
    for start, pieces in ((here, near), (there, far)):
        for place, states in enumerate(pieces):
            at = pl.ds(pl.multiple_of(start + place * size, size), size)
            first = dot(states[...], near_weights[...])
            second = dot(states[...], far_weights[...])
            k[at, :] = jnp.where(even, first, second).astype(LOW)
            v[at, :] = jnp.where(even, second, first).astype(LOW)
    rows, cols = token_marks(boxes, pages)
    mask = page_mask(cols[:, 2:3], rows[3:4, :])
    attend(q, k, v, None, None, mask, lse, ctx)
    put_pieces(dot(ctx[...], wo[...]), parts)


def normal_cdf(values):
    return 0.5 * (1.0 + lax.erf(values * (0.5**0.5)))


def feed_forward(chunks, *refs):
    parts, refs = refs[: 2 * FORE], refs[2 * FORE :]
    hidden, gain, shift, refs = refs[0], refs[1], refs[2], refs[3:]
    ups, downs, refs = refs[:chunks], refs[chunks : 2 * chunks], refs[2 * chunks :]
    mixed, middle, refs = refs[0], refs[1], refs[2:]
    upward, active, outs = refs[:chunks], refs[chunks : 2 * chunks], refs[2 * chunks :]
    total = hidden[...].astype(F32) + summed(parts)
    mixed[...] = total
    xhat, _ = normalized(total)
    low = (xhat * gain[0:1, :] + shift[0:1, :]).astype(LOW)
    middle[...] = low
    leave(mixed, middle)
    acc = None
    for index in range(chunks):
        up = dot(low, ups[index][...])
        upward[index][...] = up.astype(LOW)
        act = (up * normal_cdf(up)).astype(LOW)
        active[index][...] = act
        leave(upward[index], active[index])
        piece = dot(act, downs[index][...])
        acc = piece if acc is None else acc + piece
    put_pieces(acc, outs)


def down_back(order, chunks, grad, combined, gain, active, refs):
    grad_comb, down_cot, dgain, dshift, *outs, held, moved = refs
    plain = order == "plain" or outs[0].shape == outs[1].shape
    xhat, rstd = normalized(combined)
    grad_in, dgain[...], dshift[...] = norm_back(grad, xhat, rstd, gain)
    grad_comb[...] = grad_in
    down_cot[...] = grad_in.astype(LOW)
    if plain:
        multiply(order, [(down_cot, [(ref, False) for ref in active])], outs, [held, moved])
        return
    own, sent = outs
    rows = arranged(order, down_cot, held, moved)
    half, column = sent.shape[0], 0
    own[...] = rows[:half, :]
    for ref in active:
        at = slice(column, column + ref.shape[1])
        sent[:, at] = dot(rows[half:, :], ref[...]).astype(LOW)
        column = at.stop


def kept_products(rows, *refs):
    *active, out = refs
    column = 0
    for ref in active:
        at = slice(column, column + ref.shape[1])
        out[:, at] = dot(rows[...], ref[...]).astype(LOW)
        column = at.stop


def last_down_back(order, chunks, *refs):
    parts, refs = refs[: 2 * FORE], refs[2 * FORE :]
    mixed, gain, shift, cot, refs = *refs[:4], refs[4:]
    active, output, refs = refs[:chunks], refs[chunks], refs[chunks + 1 :]
    xhat, _ = normalized(mixed[...])
    combined = xhat * gain[0:1, :] + shift[0:1, :] + summed(parts)
    xhat, _ = normalized(combined)
    output[...] = (xhat * gain[1:2, :] + shift[1:2, :]).astype(LOW)
    leave(output)
    down_back(order, chunks, cot[...].astype(F32), combined, gain[1:2, :], active, refs)


def first_down_back(order, chunks, *refs):
    parts, refs = refs[: 2 * BACK], refs[2 * BACK :]
    grad_mixed, combined, gain, refs = *refs[:3], refs[3:]
    active, refs = refs[:chunks], refs[chunks:]
    grad = grad_mixed[...] + summed(parts)
    down_back(order, chunks, grad, combined[...], gain[1:2, :], active, refs)


def up_back(chunks, down_cot, *refs):
    upward, ups, downs, refs = refs[:chunks], refs[chunks : 2 * chunks], refs[2 * chunks : 3 * chunks], refs[3 * chunks :]
    grad_up, outs = refs[:chunks], refs[chunks:]
    low = down_cot[...]
    acc = None
    for index in range(chunks):
        back = dot_nt(low, downs[index][...])
        up = upward[index][...].astype(F32)
        slope = normal_cdf(up) + up * (jnp.exp(-0.5 * up * up) * 0.3989422804014327)
        gup = (back * slope).astype(LOW)
        grad_up[index][...] = gup
        piece = dot_nt(gup, ups[index][...])
        acc = piece if acc is None else acc + piece
    put_pieces(acc, outs)


def mixed_back(parts, grad_comb, mixed, gain, wo, grad_mixed, out_cot, dgain, dshift):
    grad = grad_comb[...] + summed(parts)
    xhat, rstd = normalized(mixed[...])
    grad_in, dgain[...], dshift[...] = norm_back(grad, xhat, rstd, gain[0:1, :])
    grad_mixed[...] = grad_in
    low = grad_in.astype(LOW)
    out_cot[...] = low
    return dot_nt(low, wo[...]).astype(LOW)


def heads_back(levels, page_row, pairs, gctx, q, k, v, lse, ctx, ext, boxes, pages, gq, gkt, gvt, dtable):
    seq = q.shape[0]
    rows, cols = token_marks(boxes, pages)
    mask = page_mask(cols[:, 2:3], rows[page_row : page_row + 1, :])
    halves = half_masks()
    lane = iota((seq, LANES), 1)
    if ext is not None:
        key_ext = key_marks(cols, levels)
        place = lane.astype(F32)
        back_ext = (
            (place == levels - cols[:, 0:1]) | (place == levels + HEAD_DIM - cols[:, 1:2])
        ).astype(F32).astype(LOW)
        line = iota((LANES, seq), 0).astype(F32)
        marks_t = ((line == rows[0:1, :]) | (line == rows[1:2, :] + HEAD_DIM)).astype(F32).astype(LOW)
        dtable[...] = jnp.zeros(dtable.shape, F32)
    for slot, pair in enumerate(pairs):
        at = slice(pair * LANES, (pair + 1) * LANES)
        queries, keys, values = q[:, at], k[:, at], v[:, at]
        gc = gctx[:, at]
        product = gc.astype(F32) * ctx[:, at].astype(F32)
        gc_t = jnp.transpose(gc)
        q_t = jnp.transpose(queries)
        keys_left = keys if ext is None else jnp.concatenate([keys, key_ext], axis=1)
        keys_right = keys if ext is None else jnp.concatenate([keys, back_ext], axis=1)
        parts = []
        for half in range(2):
            head = 2 * pair + half
            rows_at = slice(half * HEAD_DIM, (half + 1) * HEAD_DIM)
            out_at = slice(slot * LANES + half * HEAD_DIM, slot * LANES + (half + 1) * HEAD_DIM)
            left = queries * halves[half]
            if ext is not None:
                left = jnp.concatenate([left, ext[:, head * LANES : (head + 1) * LANES]], axis=1)
            scores = dot_nt(left, keys_left) + mask
            probs = jnp.exp(scores - lse[:, head : head + 1])
            delta = jnp.sum(
                jnp.where((lane < HEAD_DIM) == (half == 0), product, 0.0), -1, keepdims=True
            )
            grad_scores = probs * (dot_nt(gc * halves[half], values) - delta)
            score_cot = grad_scores.astype(LOW)
            gvt[out_at, :] = dot(gc_t[rows_at, :], probs.astype(LOW)).astype(LOW)
            gkt[out_at, :] = dot(q_t[rows_at, :], score_cot).astype(LOW)
            out = dot(score_cot, keys_right)
            parts.append(out[:, :LANES])
            if ext is not None:
                spread = out[:, LANES:]
                upper = spread.astype(LOW)
                lower = (spread - upper.astype(F32)).astype(LOW)
                block = dot(marks_t, upper) + dot(marks_t, lower)
                small = iota((40, LANES), 1)
                for dim in range(2):
                    piece = block[dim * HEAD_DIM : dim * HEAD_DIM + 40, :]
                    if dim:
                        piece = pltpu.roll(piece, HEAD_DIM, 1)
                    piece = jnp.where(small <= levels, piece, 0.0)
                    piece = pltpu.roll(piece, 0, 1, stride=1, stride_axis=0)
                    line = jnp.sum(piece, 0, keepdims=True)
                    over = pltpu.roll(line, LANES - 1, 1)
                    column = iota((1, LANES), 1)
                    line = jnp.where(column == 2 * levels - 1, line + over, line)
                    dtable[dim, head : head + 1, :] = line
        gq[:, slot * LANES : (slot + 1) * LANES] = (jnp.where(lane < HEAD_DIM, parts[0], parts[1]) * SCALE).astype(LOW)


def next_attention_back(*refs):
    parts, refs = refs[: 2 * BACK], refs[2 * BACK :]
    grad_comb, mixed, gain, wo, q, k, v, lse, ctx, boxes, pages, *outs = refs
    grad_mixed, out_cot, gq, gkt, gvt, dgain, dshift = outs
    gctx = mixed_back(parts, grad_comb, mixed, gain, wo, grad_mixed, out_cot, dgain, dshift)
    heads_back(0, 3, range(q.shape[1] // LANES), gctx, q, k, v, lse, ctx, None, boxes, pages, gq, gkt, gvt, None)


def first_attention_back(levels, *refs):
    parts, refs = refs[: 2 * BACK], refs[2 * BACK :]
    grad_comb, mixed, gain, wo, q, k, v, lse, ctx, ext, boxes, pages, wq, wk, wv, *outs = refs
    grad_mixed, out_cot, dgain, dshift, gq, gkt, gvt, dtable, part = outs
    gctx = mixed_back(parts, grad_comb, mixed, gain, wo, grad_mixed, out_cot, dgain, dshift)
    heads_back(levels, 2, range(q.shape[1] // LANES), gctx, q, k, v, lse, ctx, ext, boxes, pages, gq, gkt, gvt, dtable)
    input_back(gq, gkt, gvt, wq, wk, wv, part)


def input_back(gq, gkt, gvt, wq, wk, wv, *parts):
    put_pieces(
        dot_nt(gq[...], wq[...])
        + dot_nt(jnp.transpose(gkt[...]), wk[...])
        + dot_nt(jnp.transpose(gvt[...]), wv[...]),
        parts,
    )


def halving_order(bits):
    count = len(bits)
    flips = [
        sum(bit for place, bit in enumerate(bits) if block >> (count - 1 - place) & 1)
        for block in range(1 << count)
    ]
    return [lambda here, flip=flip: here ^ flip for flip in flips]


def arranged(order, source, held, moved):
    held[...] = jnp.transpose(source[...])
    if order == "plain":
        return held
    size = held.shape[0] // len(order)
    here = lax.axis_index("dp")
    for block, flip in enumerate(order):
        at = pl.multiple_of(flip(here) * size, size)
        moved[block * size : (block + 1) * size, :] = held[pl.ds(at, size), :]
    return moved


def multiply(order, groups, outs, scratch):
    column = 0
    for place, (source, rights) in enumerate(groups):
        left = arranged(order, source, scratch[2 * place], scratch[2 * place + 1])
        for right, flipped in rights:
            wide = right.shape[0] if flipped else right.shape[1]
            step = wide if flipped else min(512, wide)
            for start in range(0, wide, step):
                for index in reversed(range(len(outs))):
                    size = outs[index].shape[0]
                    rows = left[index * size : (index + 1) * size, :]
                    if flipped:
                        block = dot_nt(rows, right[start : start + step, :])
                    else:
                        block = dot(rows, right[:, start : start + step])
                    outs[index][:, column + start : column + start + step] = block.astype(LOW)
            column += wide


def put_vectors(order, lines, table, outs, column, turned, buckets):
    count, rest = len(lines), LANES - len(lines)
    rows = [line[...] for line in lines] + [jnp.zeros((rest, lines[0].shape[1]), F32)]
    turned[...] = jnp.transpose(jnp.concatenate(rows, axis=0))
    rows = [jnp.zeros((count, LANES), F32), table[0], table[1]]
    rows += [jnp.zeros((rest - 2 * table.shape[1], LANES), F32)]
    buckets[...] = jnp.transpose(jnp.concatenate(rows, axis=0))
    here = lax.axis_index("dp")
    size = turned.shape[0] // len(order)
    some = 2 * (LANES // 4) // len(order)
    per_out = len(order) // len(outs)
    for block, flip in enumerate(order):
        index = flip(here)
        part = turned[pl.ds(pl.multiple_of(index * size, size), size), :]
        first = part[:some] + buckets[pl.ds(pl.multiple_of(index * some, some), some), :]
        at = (block % per_out) * size
        outs[block // per_out][at : at + size, column : column + LANES] = jnp.concatenate(
            [first, part[some:]], axis=0
        ).astype(LOW)


def weight_products(order, plan, parts, lines, *refs):
    groups, position = [], 0
    for kinds in plan:
        stop = position + 1 + len(kinds)
        groups.append((refs[position], list(zip(refs[position + 1 : stop], kinds))))
        position = stop
    extras, refs = refs[position : position + lines], refs[position + lines :]
    outs, scratch = refs[:parts], refs[parts:]
    multiply(order, groups, outs, scratch)
    if lines:
        put_vectors(order, extras[:-1], extras[-1], outs, outs[0].shape[1] - LANES, *scratch[-2:])


def weight_gradients(order, groups, after=(), extras=()):
    plan, args, columns = [], [], LANES if extras else 0
    for left, rights in groups:
        plan.append([flipped for _, flipped in rights])
        args.append(left)
        for right, flipped in rights:
            args.append(right)
            columns += right.shape[0] if flipped else right.shape[1]
    seq, d_model = groups[0][0].shape
    parts = 1 if order == "plain" else 2
    scratch = [pltpu.VMEM((d_model, seq), LOW)] * (2 * len(groups))
    if extras:
        scratch += [pltpu.VMEM((d_model, LANES), F32), pltpu.VMEM((LANES, LANES), F32)]
    return call(
        functools.partial(weight_products, order, plan, parts, len(extras)),
        [((d_model // parts, columns), LOW)] * parts,
        *args, *extras, after=after, scratch=scratch,
    )


def merge_kernel(kept, got, keep, send):
    half = keep.shape[0]
    keep[...] = (kept[:half, :].astype(F32) + got[:half, :].astype(F32)).astype(LOW)
    leave(keep)
    send[...] = (kept[half:, :].astype(F32) + got[half:, :].astype(F32)).astype(LOW)


def merge(kept, got, after=(), last=False):
    half = ((kept.shape[0] // 2, kept.shape[1]), LOW)
    return call(merge_kernel, [(*half, SAVE) if last else half, half], kept, got, after=after)


def join_kernel(*refs):
    keep, send = refs[-2:]
    half, column = keep.shape[0], 0
    for kept, got in zip(refs[:-2:2], refs[1:-2:2]):
        at = slice(column, column + kept.shape[1])
        keep[:, at] = (kept[:half, :].astype(F32) + got[:half, :].astype(F32)).astype(LOW)
        send[:, at] = (kept[half:, :].astype(F32) + got[half:, :].astype(F32)).astype(LOW)
        column = at.stop


def join(*pairs, after=()):
    rows, columns = pairs[0][0].shape[0] // 2, sum(pair[0].shape[1] for pair in pairs)
    return call(join_kernel, [((rows, columns), LOW)] * 2, *[a for pair in pairs for a in pair], after=after)


def finish_kernel(plan, count, width, extra, *refs):
    token, ins = refs[-1], []
    token[...] = jnp.zeros(token.shape, F32)
    refs = list(refs)
    for targets, paired in plan:
        ins.append([refs.pop(0) for _ in range(2 if paired else 1)])
    read = lambda group, at: sum(ref[:, at].astype(F32) for ref in group)
    for group, (targets, _) in zip(ins, plan):
        for block, target in enumerate(targets):
            if target is None:
                continue
            out, layer = target
            refs[out][layer] = read(group, slice(block * width, (block + 1) * width))
    if extra is not None:
        size, columns = ins[extra][0].shape
        total = read(ins[extra], slice(columns - LANES, columns))
        total = jnp.concatenate([total, jnp.zeros((LANES - size, LANES), F32)], axis=0)
        refs[count][...] = jnp.transpose(total)


def finish(plan, groups, count, width, extra=None, after=(), fresh=False):
    size = groups[0][0].shape[0]
    outs = [((2, size, width), F32, SAVE)] * count
    if extra is not None:
        outs.append(((LANES, LANES), F32, FREE))
    plan = [(targets, len(group) > 1) for targets, group in zip(plan, groups)]
    results = call(
        functools.partial(finish_kernel, plan, count, width, extra), [*outs, TOKEN],
        *[Held(a) if isinstance(a, jax.Array) and not (fresh and place == 0) else a for place, group in enumerate(groups) for a in group],
        after=after,
    )
    return [out.array if isinstance(out, Held) else out for out in results]


def sum_kernel(*refs):
    *parts, out = refs
    at = slice(0, out.shape[1])
    out[...] = sum(part[:, at].astype(F32) for part in parts)


def last_kernel(layer1, *refs):
    *parts, first, second = refs
    width = first.shape[2]
    for place, out in enumerate((first, second)):
        at = slice(place * width, (place + 1) * width)
        out[0] = sum(part[:, at].astype(F32) for part in parts)
        out[1] = layer1[:, at]
        leave(out)


def input_sum(*refs):
    *parts, grad, out, token = refs
    out[...] = grad[...] + summed(parts)
    token[...] = jnp.zeros(token.shape, F32)


def pack_kernel(*refs):
    table, out = refs[-2], refs[-1]
    lines = len(refs) - 2
    for place in range(lines):
        out[place : place + 1, :] = refs[place][...]
    rows = table.shape[1]
    rest = jnp.zeros((rows, out.shape[1] - LANES), F32)
    for dim in range(2):
        at = slice(lines + dim * rows, lines + (dim + 1) * rows)
        out[at, :] = jnp.concatenate([table[dim], rest], axis=1)


def other(block, axis):
    return lax.ppermute(block, axis, [(0, 1), (1, 0)])


def body(inputs, w_query, w_key, w_value, w_out, w_up, w_down, norm_gain, norm_shift, box_table, boxes, pages, cotangent):
    _, rows_here, seq, d_model = inputs.shape
    assert rows_here == 1
    width = w_query.shape[3]
    hidden_width = w_up.shape[3]
    heads = width // HEAD_DIM
    levels = box_table.shape[3] // 2
    n_dp = lax.axis_size("dp")
    me = lax.axis_index("dp")
    bits = [1 << place for place in range(n_dp.bit_length() - 1)]
    pairs = n_dp == 8 and d_model % (16 * n_dp) == 0
    far_bits = bits[1:] + bits[:1]
    near_first, far_first = [halving_order(b) if pairs else "plain" for b in (bits, far_bits)]

    cuts = [slice(at, at + 512) for at in range(0, hidden_width, 512)]
    chunks = len(cuts)

    def ff_weights(layer):
        return [Held(w_up, 0, layer, None, cut) for cut in cuts] + [Held(w_down, 0, layer, cut) for cut in cuts]

    def flip(block, bit):
        return lax.ppermute(block, "dp", [(i, i ^ bit) for i in range(n_dp)])

    def exchange(*parts):
        return [*parts, *(other(part, "mp") for part in parts)]

    wide = ((seq, d_model), F32)
    thin = ((seq, d_model), LOW)
    fore = [((seq // FORE, d_model), LOW)] * FORE
    back = [((seq // BACK, d_model), LOW)] * BACK
    proj = ((seq, width), LOW)
    turned = [((width, seq), LOW)] * 2
    ff = [((seq, 512), LOW)] * chunks
    stats = ((seq, LANES), F32)
    vec = ((1, d_model), F32)
    halves = [((d_model // 2, hidden_width), LOW)] * 2 if pairs else [((d_model, hidden_width), LOW)]
    flat = [pltpu.VMEM((d_model, seq), LOW)] * 2
    saved = lambda *shapes: [(*shape, SAVE) for shape in shapes]
    x = Held(inputs, 0, 0)
    box = Held(boxes, 0, None, 0)
    page = Held(pages, None, 0)
    table = Held(jnp.transpose(box_table[0], (1, 0, 2)))
    norms = [[Held(array, 0, layer) for array in (norm_gain, norm_shift)] for layer in range(2)]

    assert n_dp % 2 == 0
    mine = fetch_weights(w_key, w_value)
    near_weights = other(mine, "stream")
    far_weights = flip(near_weights, 1)
    q0, k0, v0, lse0, ctx0, ext0, *rest = call(
        functools.partial(first_attention, levels),
        [*saved(proj, proj, proj, stats, proj, ((seq, heads * LANES), LOW)), *fore],
        box, page, table, x, Held(w_query, 0, 0), Held(w_key, 0, 0), Held(w_value, 0, 0), Held(w_out, 0, 0),
        after=[mine], fetch=[*ff_weights(0), x],
    )
    parts, ff_w, x_here = rest[:FORE], rest[FORE:-1], rest[-1]
    mixed_here, middle0, *rest = call(
        functools.partial(feed_forward, chunks),
        [wide, thin, *ff, *ff, *fore],
        *exchange(*parts), x_here, *norms[0], *ff_w, fetch=[Held(w_query, 0, 1)],
    )
    upward0, active0, parts = rest[:chunks], rest[chunks : 2 * chunks], rest[2 * chunks : -1]
    mixed0, wq1 = mixed_here, rest[-1]
    sums = exchange(*parts)
    shares = call(shared_states, fore[:2], *sums, mixed_here, *norms[0])
    near = [other(share, "stream") for share in shares]
    combined0, hidden1, rounded1 = call(
        next_states, [*saved(wide), wide, thin], *sums, mixed_here, *norms[0], after=shares[:1],
    )
    q1, wo1 = call(next_queries, [proj], rounded1, wq1, fetch=[Held(w_out, 0, 1)])
    *near, q1 = lax.optimization_barrier((*near, q1))
    far = [other(share, "mp") for share in near]
    k1, v1, lse1, ctx1, *rest = call(
        functools.partial(next_attention, len(near)), [proj, proj, stats, proj, *fore],
        *near, *far, near_weights, far_weights, q1, box, page, wo1, after=[q1], fetch=ff_weights(1),
    )
    parts, ff_w = rest[:FORE], rest[FORE:]
    mixed1, middle1, *rest = call(
        functools.partial(feed_forward, chunks), [wide, thin, *ff, *ff, *fore],
        *exchange(*parts), hidden1, *norms[1], *ff_w, fetch=[Held(cotangent, 0, 0)],
    )
    upward1, active1, parts, cot = rest[:chunks], rest[chunks : 2 * chunks], rest[2 * chunks : -1], rest[-1]

    output, grad_comb, down_cot, dgain11, dshift11, *down1 = call(
        functools.partial(last_down_back, near_first, chunks), [(*thin, SAVE), wide, thin, vec, vec, *([((d_model // 2, seq), LOW), halves[1]] if pairs else halves)],
        *exchange(*parts), mixed1, *norms[1], cot, *active1, scratch=flat,
    )
    if pairs:
        got_down1 = flip(down1[1], bits[0])
    rest = call(functools.partial(up_back, chunks), [*ff, *back], down_cot, *upward1, *ff_w, after=down1[-1:])
    grad_up, parts = rest[:chunks], rest[chunks:]
    up1 = weight_gradients(far_first, [(middle1, [(ref, False) for ref in grad_up])])
    if pairs:
        got_up1 = flip(up1[1], far_bits[0])
    grad_mixed, out_cot, gq, *rest = call(
        next_attention_back, [wide, thin, proj, *turned, vec, vec],
        *exchange(*parts), grad_comb, mixed1, norms[1][0], wo1, q1, k1, v1, lse1, ctx1, box, page, after=up1[-1:],
    )
    gkv, (dgain10, dshift10) = [other(ref, "stream") for ref in rest[:2]], rest[2:]
    qo1 = weight_gradients(near_first, [(rounded1, [(gq, False)]), (out_cot, [(ctx1, False)])])
    before = qo1[-1:]
    if pairs:
        got_qo1 = flip(qo1[1], bits[0])
        (kept,) = call(kept_products, halves[:1], down1[0], *active1, after=qo1[1:])
        down1 = [kept, down1[1]]
        down1 = merge(down1[0], got_down1, after=qo1[1:])
        got_down1 = flip(down1[1], bits[1])
        before = down1[1:]
    parts = call(
        input_back, back, gq, *gkv, Held(w_query, 0, 1), Held(w_key, 0, 1), Held(w_value, 0, 1), after=before
    )
    kv1 = weight_gradients(near_first, [(rounded1, [(ref, True) for ref in gkv])], after=parts[:1])
    before = kv1[-1:]
    if pairs:
        got_kv1 = flip(kv1[1], bits[0])
        up1 = merge(up1[0], got_up1, after=[kv1[1], got_qo1])
        got_up1 = flip(up1[1], far_bits[1])
        before = up1[1:]

    grad_comb, down_cot, dgain01, dshift01, *rest = call(
        functools.partial(first_down_back, near_first, chunks), [wide, thin, vec, vec, *halves],
        *exchange(*parts), grad_mixed, combined0, norms[0][0], *active0, scratch=flat, after=before, fetch=ff_weights(0),
    )
    down0, ff_w = rest[: len(halves)], rest[len(halves) :]
    if pairs:
        got_down0 = flip(down0[1], bits[0])
    rest = call(functools.partial(up_back, chunks), [*ff, *back], down_cot, *upward0, *ff_w, after=down0[-1:])
    grad_up, parts = rest[:chunks], rest[chunks:]
    before = []
    if pairs:
        at1 = join((qo1[0], got_qo1), (kv1[0], got_kv1), after=[parts[0], got_down1])
        got_at1 = flip(at1[1], bits[1])
        down1 = merge(down1[0], got_down1, after=at1[1:], last=True)
        got_down1 = flip(down1[1], bits[2])
        before = down1[1:]
    grad_mixed, out_cot, dgain00, dshift00, gq, gkt, gvt, dtable, part = call(
        functools.partial(first_attention_back, levels),
        [wide, thin, vec, vec, proj, *turned, ((2, 8, LANES), F32), thin],
        *exchange(*parts), grad_comb, mixed0, norms[0][0], Held(w_out, 0, 0),
        q0, k0, v0, lse0, ctx0, ext0, box, page, Held(w_query, 0, 0), Held(w_key, 0, 0), Held(w_value, 0, 0), after=before,
    )
    vectors = [dgain00, dgain01, dgain10, dgain11, dshift00, dshift01, dshift10, dshift11]
    before = [dgain00, got_up1] if pairs else [dgain00]
    up0 = weight_gradients(near_first, [(middle0, [(ref, False) for ref in grad_up])], after=before)
    before = up0[-1:]
    if pairs:
        got_up0 = flip(up0[1], bits[0])
        at1 = merge(at1[0], got_at1, after=[up0[1], got_down0], last=True)
        got_at1 = flip(at1[1], bits[2])
        down0 = merge(down0[0], got_down0, after=at1[1:])
        got_down0 = flip(down0[1], bits[1])
        before = down0[1:]
    kv0 = weight_gradients(
        near_first, [(x, [(gkt, True), (gvt, True)])], after=before, extras=[*vectors, dtable] if pairs else ()
    )
    qo0 = weight_gradients(near_first, [(x, [(gq, False)]), (out_cot, [(ctx0, False)])], after=kv0[-1:])

    before = qo0[-1:]
    if pairs:
        got_kv0, got_qo0 = (flip(block[1], bits[0]) for block in (kv0, qo0))
        down0 = merge(down0[0], got_down0, after=[qo0[1], got_at1, got_down1], last=True)
        got_down0 = flip(down0[1], bits[2])

        up0 = merge(up0[0], got_up0, after=down0[1:])
        got_up0 = flip(up0[1], bits[1])

        kv0 = merge(kv0[0], got_kv0, after=[up0[1], got_up0, got_down0])
        got_kv0 = flip(kv0[1], bits[1])
        up0 = merge(up0[0], got_up0, after=kv0[1:], last=True)
        got_up0 = flip(up0[1], bits[2])
        up1 = merge(up1[0], got_up1, after=up0[1:], last=True)
        got_up1 = flip(up1[1], far_bits[2])
        before = up1[1:]
    grad_inputs, token = call(
        input_sum, [(*wide, SAVE), TOKEN], *exchange(part), grad_mixed, after=before,
    )
    before = [token]
    if pairs:
        qo0 = merge(qo0[0], got_qo0, after=[token, got_kv0])
        got_qo0 = flip(qo0[1], bits[1])
        kv0 = merge(kv0[0], got_kv0, after=qo0[1:], last=True)
        got_kv0 = flip(kv0[1], bits[2])
        before = kv0[1:]
        down0, up0, down1, up1, at1 = (
            (down0[0], got_down0), (up0[0], got_up0), (down1[0], got_down1), (up1[0], got_up1), (at1[0], got_at1)
        )
    else:
        (small,) = call(pack_kernel, [((24, d_model), F32)], *vectors, dtable)
        small = lax.psum(small, "dp")
        at1 = [jnp.concatenate([qo1[0], kv1[0]], axis=1)]
        down0, up0, down1, up1, kv0, qo0, at1 = (
            (lax.psum_scatter(g[0], "dp", scatter_dimension=0, tiled=True),)
            for g in (down0, up0, down1, up1, kv0, qo0, at1)
        )
    grad_down, grad_up, token = finish(
        [[(0, 0)], [(0, 1)], [(1, 0)], [(1, 1)]], [down0, down1, up0, up1], 2, hidden_width, after=before
    )
    if pairs:
        qo0 = merge(qo0[0], got_qo0, after=[token], last=True)
        got_qo0 = flip(qo0[1], bits[2])
        token = qo0[1]
        kv0, qo0 = (kv0[0], got_kv0), (qo0[0], got_qo0)
    grad_k, grad_v, *rest, token = finish(
        [[(0, 0), (1, 0)], [None, None, (0, 1), (1, 1)]], [kv0, at1], 2, width, 0 if pairs else None, after=[token], fresh=pairs
    )
    (layer1,) = call(sum_kernel, [((d_model // n_dp, 2 * width), F32)], *(Held(a) if isinstance(a, jax.Array) else a for a in at1), after=[token])
    grad_q, grad_o = call(
        last_kernel, [((2, d_model // n_dp, width), F32, SAVE)] * 2, layer1, *qo0
    )
    grad_q, grad_o = grad_q.array, grad_o.array
    cut = d_model // n_dp
    some = 2 * levels // n_dp
    if pairs:
        vectors, grad_table = rest[0][:8, :cut], rest[0][8:24, :some]
    else:
        vectors = lax.dynamic_slice_in_dim(small[:8], me * cut, cut, 1)
        grad_table = lax.dynamic_slice_in_dim(small[8:], me * some, some, 1)
    vectors = vectors.reshape(2, 2, 2, cut)
    grad_table = grad_table.reshape(1, 2, 8, some)[:, :, :heads]
    flipped = lambda block: jnp.transpose(block, (0, 2, 1))[None]
    return (
        output.array[None, None],
        grad_inputs.array[None, None],
        grad_q[None],
        grad_k[None],
        grad_v[None],
        flipped(grad_o),
        grad_up[None],
        flipped(grad_down),
        vectors[:1],
        vectors[1:],
        grad_table,
    )


def solution(mesh):
    in_specs = (
        P("stream", "dp", None, None),
        P("stream", None, None, "mp"),
        P("stream", None, None, "mp"),
        P("stream", None, None, "mp"),
        P("stream", None, "mp", None),
        P("stream", None, None, "mp"),
        P("stream", None, "mp", None),
        P("stream", None, None, None),
        P("stream", None, None, None),
        P("stream", None, "mp", None),
        P("stream", None, "dp", None),
        P(None, "dp", None),
        P("stream", "dp", None, None),
    )
    out_specs = (
        P("stream", "dp", None, None),
        P("stream", "dp", None, None),
        P("stream", None, "dp", "mp"),
        P("stream", None, "dp", "mp"),
        P("stream", None, "dp", "mp"),
        P("stream", None, "mp", "dp"),
        P("stream", None, "dp", "mp"),
        P("stream", None, "mp", "dp"),
        P("stream", None, None, "dp"),
        P("stream", None, None, "dp"),
        P("stream", None, "mp", "dp"),
    )
    return jax.shard_map(body, mesh=mesh, in_specs=in_specs, out_specs=out_specs, check_vma=False)
```
